32 devices in a mesh: groups: 2 (over y), rows: 4 (over z), mp: 2 (over x), sub: 2 (over core).
Axes of the slice: x: 2, y: 2, z: 4, core: 2. Of those that a mesh axis runs over, the one named last changes fastest.
Arguments:
- hidden: bfloat16 [4096, 4096], P(('groups', 'rows'), ('mp', 'sub')), parts along dimension 0, may hold values from -600 to 600
- neighbour_states: bfloat16 [128, 128, 4096], P(('groups', 'rows'), None, ('mp', 'sub')), parts along dimension 0, may hold values from -600 to 600
- query_weight: bfloat16 [4096, 4096], P(None, ('mp', 'sub')), may hold values from -0.1875 to 0.1875
- encoder_weight: bfloat16 [4096, 256], P(('mp', 'sub')), may hold values from -0.09375 to 0.09375
- output_weight: bfloat16 [4096, 4096], P(('mp', 'sub')), may hold values from -0.5 to 0.5
- neighbour_owner: int32 [64, 2], P(('groups', 'rows')), parts along dimension 0, may hold values from 0 to 3, all different within a row; in each aligned block of 8 rows (0 to 7, 8 to 15, ...) at most 4 rows name the same one
- neighbour_slot: int32 [64, 2], P(('groups', 'rows')), parts along dimension 0, may hold values from 0 to 15
- neighbour_length: int32 [128], P(('groups', 'rows')), parts along dimension 0, may hold values from 1 to 128, 6144 in all
Outputs:
- mixed: bfloat16 [4096, 4096], P(('groups', 'rows'), ('mp', 'sub')), parts along dimension 0
The draws below stay inside these ranges and needn't reach their ends.
There are 2 independent parts, one for each index of `groups`. The reference program is written for one: setup_inputs(seed, part) draws one part's arguments, and reference() takes and returns one part's arrays. A program takes and returns all parts, laid end to end along the dimension named above; an argument that names none is the same for every part. Nothing has to cross between parts.
Inputs may be any that keep to these rules, and one draw needn't show every extreme that they name: `neighbour_owner`: A span's two owners differ; among the 8 spans of one index of rows no owner is named more than 4 times, a bound that some block reaches. `neighbour_length`: in each part (each index of groups) the lengths sum to 6144; some neighbour is live in all 128 slots.
All inputs are finite; a program needn't handle non-finite values.
Results may differ from the reference program's by a relative error of at most 0.033.
Values may be sent and summed in bfloat16 or wider, within the bound.
No kernel may reach another device: no remote copies, remote signals or barrier semaphores. Data moves between devices by JAX's collectives and lax.ppermute only.
A program may use at most 128 MiB of HBM per device.

```python
import math
import jax
import jax.numpy as jnp
import numpy as np
from jax import lax

D = 4096
HEADS = 32
HEAD_DIM = 128
SPAN = 64
NBR_LEN = 128
CH_DEV = 8
NBR_DEV = 16
CAP = 4
SPANS = 32
NBRS = 64
TOKENS = 2048
HEADS_GRP = 8
N_ROWS = 4


def feature_scales(key, width):
    ramp = 1.0 + 2.0 * jnp.arange(width, dtype=jnp.float32) / (width - 1)
    return ramp * jnp.power(10.0, 0.5 * jax.random.uniform(key, (width,)))


def row_scales(key, count):
    return jnp.power(10.0, jax.random.uniform(key, (count,)))


def draw_hidden(key, part):
    key = jax.random.fold_in(key, 11)
    key_noise, key_cols, key_rows = jax.random.split(key, 3)
    noise = jnp.clip(jax.random.normal(key_noise, (TOKENS, D)), -6.0, 6.0)
    values = noise * feature_scales(key_cols, D)[None, :] * row_scales(key_rows, TOKENS)[:, None]
    return values.astype(jnp.bfloat16)


def draw_neighbour_states(key, part):
    key = jax.random.fold_in(key, 23)
    key_noise, key_cols, key_rows = jax.random.split(key, 3)
    count = NBRS * NBR_LEN
    noise = jnp.clip(jax.random.normal(key_noise, (count, D)), -6.0, 6.0)
    values = noise * feature_scales(key_cols, D)[None, :] * row_scales(key_rows, count)[:, None]
    return values.reshape(NBRS, NBR_LEN, D).astype(jnp.bfloat16)


def plant(array, stream_key, smallest, top_value):
    longest = array.shape.index(max(array.shape))
    spots = []
    for shift in (0, 1):
        where = [jax.random.randint(jax.random.fold_in(stream_key, axis), (), 0, length) for axis, length in enumerate(array.shape)]
        where[longest] = (where[longest] + shift) % array.shape[longest]
        spots.append(tuple(where))
    return array.at[spots[0]].set(smallest).at[spots[1]].set(top_value)


def spiked(result, stream_key, source, target, blocks, factor):
    def block_of(position):
        return (jnp.arange(result.shape[position]) // (result.shape[position] // blocks)).reshape((-1,) + (1,) * (result.ndim - 1 - position))

    one_side = jax.random.permutation(stream_key, blocks)[block_of(target)]
    far = (block_of(target) + blocks // 2) % blocks
    return jnp.where((block_of(source) == one_side) | (block_of(source) == far), factor * result, result)


def shard_levels(key, extent, pieces, low, high):
    loudness = 1.0
    for position, blocks in pieces:
        heights = jax.random.uniform(jax.random.fold_in(jax.random.fold_in(key, 6), position), (blocks,), jnp.float32, low / len(pieces), high / len(pieces))
        loudness = loudness * jnp.repeat(jnp.exp(heights), extent[position] // blocks).reshape((-1,) + (1,) * (len(extent) - 1 - position))
    return loudness


def split_up(number_of, total, most, lean):
    weights = [(1 << 20) // math.isqrt(standing ** lean) + 1 for standing in range(2, number_of + 1)]
    surplus, given = total - most - (number_of - 1), [1] * (number_of - 1)
    while surplus > 0:
        movable = [i for i in range(number_of - 1) if given[i] < most]
        pool, remaining = sum([weights[i] for i in movable]), surplus
        for i in movable:
            extra = min(most - given[i], max(1, remaining * weights[i] // pool), surplus)
            given[i] = given[i] + extra
            surplus = surplus - extra
    return np.array([most] + given)


def ragged(key, number_of, total, limit, slope):
    if number_of == 2:
        one = jax.random.randint(key, (), max(1, total - limit), min(limit, total - 1) + 1)
        return jnp.stack([one, total - one])
    tallies = jnp.asarray(split_up(number_of, total, limit, slope), jnp.int32)
    twos = (number_of - 1) // 2
    donor, taker = tallies[1:1 + 2 * twos:2], tallies[2:2 + 2 * twos:2]
    margin = jnp.minimum(donor - 1, limit - taker)
    moved = jax.random.randint(jax.random.fold_in(key, 1), (twos,), 0, 1 << 20) % (margin + 1)
    tallies = tallies.at[1:1 + 2 * twos:2].set(donor - moved).at[2:2 + 2 * twos:2].set(taker + moved)
    return tallies[jax.random.permutation(jax.random.fold_in(key, 2), number_of)]


def shared_out(own_key, own, number, rows, number_of, top, most, slope):
    sequence = jax.random.permutation(own_key, number_of)
    heavy_load, usual = shares(number_of, rows * top, most, slope, True), shares(number_of, rows * top, most, slope, False)
    places = jnp.arange(number_of)

    def named(tallies, rotation):
        used = int((tallies > 0).sum())
        fixed = max(1, used // 4)
        passed = fixed + (places - fixed + rotation * (used - fixed)) % max(1, number_of - fixed)
        return jnp.zeros((number_of,), jnp.int32).at[sequence[jnp.where(places < fixed, places, passed)]].set(jnp.asarray(tallies, jnp.int32))

    tallies = jnp.where(number % 4 == 0, named(heavy_load, number // 4), named(usual, number - number // 4 - 1))
    mixed = jax.random.permutation(jax.random.fold_in(own, 3), number_of)
    donor, sink = mixed[0:number_of // 2 * 2:2], mixed[1:number_of // 2 * 2:2]
    room = jnp.minimum(tallies[donor] - 1, most - tallies[sink]) // 2
    room = jnp.where((donor == sequence[0]) | (sink == sequence[0]) | (tallies[sink] == 0), 0, jnp.maximum(room, 0))
    passed = jax.random.randint(jax.random.fold_in(own, 4), (number_of // 2,), 0, 1 << 20) % (room + 1)
    tallies = tallies.at[donor].add(-passed).at[sink].add(passed)
    members = jnp.searchsorted(jnp.cumsum(tallies), jnp.arange(rows * top), side="right").astype(jnp.int32)
    listing = members.reshape(top, rows).T
    listing = listing[jax.random.permutation(jax.random.fold_in(own, 1), rows)]
    rotation = jax.random.randint(jax.random.fold_in(own, 2), (rows, 1), 0, top)
    return jnp.take_along_axis(listing, (jnp.arange(top)[None, :] + rotation) % top, axis=1)


def shares(amount, total, reach, skew, full):
    loads = [(1 << 20) // math.isqrt(rank ** skew) + 1 for rank in range(1, amount + 1)]
    largest = reach if full else min(reach, max(-(-total // amount), total * loads[0] // sum(loads)))
    least = 1 if total - largest >= amount - 1 else 0
    counts, surplus = [largest] + [least] * (amount - 1), total - largest - least * (amount - 1)
    while surplus > 0:
        candidates = [i for i in range(1, amount) if counts[i] < largest] or [i for i in range(1, amount) if counts[i] < reach]
        pool, budget = sum([loads[i] for i in candidates]), surplus
        for i in candidates:
            addition = min(reach - counts[i], max(1, budget * loads[i] // pool), surplus)
            counts[i] = counts[i] + addition
            surplus = surplus - addition
    return np.array(counts)


def scatter_about(stream_key, dims, deviation, limit, pieces=(), kind=jnp.bfloat16):
    array = deviation * jax.random.normal(stream_key, dims, jnp.float32)
    if pieces:
        array = array * shard_levels(stream_key, dims, pieces, -0.22, 0.18)
    return jnp.clip(array, -limit, limit).astype(kind)


def heavy_noise(key, dims, scale, most, pieces, heavy, kind=jnp.bfloat16):
    drawn = scale * jax.random.normal(key, dims, jnp.float32)
    if pieces:
        drawn = drawn * shard_levels(key, dims, pieces, -0.22, 0.18)
    return jnp.clip(spiked(drawn, jax.random.fold_in(key, 3), *heavy), -most, most).astype(kind)


def setup_inputs(seed: int = 0, part: int = 0) -> dict:
    splits = jax.random.split(jax.random.key(seed), 9)
    part_keys = jax.random.split(jax.random.fold_in(splits[8], part), 9)
    hidden = draw_hidden(jax.random.fold_in(jax.random.fold_in(splits[8], part), 71), part)
    neighbour_states = draw_neighbour_states(jax.random.fold_in(jax.random.fold_in(splits[8], part), 71), part)
    query_weight = scatter_about(splits[2], (D, HEADS * HEAD_DIM), (D // 4) ** -0.5, 0.1875, ((1, 4),))
    encoder_weight = scatter_about(splits[3], (D, 2 * HEAD_DIM), D ** -0.5, 0.09375, ((0, 4),))
    output_weight = heavy_noise(splits[4], (HEADS * HEAD_DIM, D), (2 * HEAD_DIM) ** -0.5, 0.5, ((0, 4),), (0, 1, 4, 2.0))
    neighbour_owner_keys = jax.random.split(jax.random.fold_in(part_keys[5], 1), SPANS // CH_DEV)
    neighbour_owner_turns = jax.random.permutation(jax.random.fold_in(part_keys[5], 3), SPANS // CH_DEV)
    neighbour_owner = jax.vmap(lambda own, number: shared_out(jax.random.fold_in(part_keys[5], 2), own, number, CH_DEV, N_ROWS, 2, CAP, 2))(neighbour_owner_keys, neighbour_owner_turns).reshape((SPANS, 2))
    neighbour_slot = plant(jax.random.randint(part_keys[6], (SPANS, 2), 0, NBR_DEV), jax.random.fold_in(part_keys[6], 1), 0, NBR_DEV - 1).astype(jnp.int32)
    neighbour_length = ragged(part_keys[7], NBRS, NBRS * NBR_LEN * 3 // 4, NBR_LEN, 2).astype(jnp.int32)
    return {"hidden": hidden, "neighbour_states": neighbour_states, "query_weight": query_weight, "encoder_weight": encoder_weight, "output_weight": output_weight, "neighbour_owner": neighbour_owner, "neighbour_slot": neighbour_slot, "neighbour_length": neighbour_length}


eps = 1e-05
softcap = 10.0

def inverse_rms(states):
    return lax.rsqrt(lax.optimization_barrier(jnp.mean(jnp.square(states.astype(jnp.float32)), axis=-1)) + eps)

def reference(hidden, neighbour_states, query_weight, encoder_weight, output_weight, neighbour_owner, neighbour_slot, neighbour_length):
    key_raw = jnp.dot(neighbour_states.reshape(NBRS * NBR_LEN, D), encoder_weight, preferred_element_type=jnp.float32)
    key_raw = key_raw.reshape(NBRS, NBR_LEN, 2 * HEAD_DIM)
    encoded = (key_raw * inverse_rms(neighbour_states)[..., None]).astype(jnp.bfloat16)
    neighbour_ids = (neighbour_owner * NBR_DEV + neighbour_slot).astype(jnp.int32).reshape(SPANS * 2)
    picked = encoded[neighbour_ids].reshape(SPANS, 2 * NBR_LEN, 2 * HEAD_DIM)
    live_lengths = neighbour_length[neighbour_ids]
    valid = (jnp.arange(NBR_LEN)[None, :] < live_lengths[:, None]).reshape(SPANS, 2 * NBR_LEN)
    query_raw = jnp.dot(hidden, query_weight, preferred_element_type=jnp.float32)
    queries = (query_raw * inverse_rms(hidden)[:, None]).astype(jnp.bfloat16)
    query_heads = queries.reshape(SPANS, SPAN, HEADS, HEAD_DIM).astype(jnp.float32)
    keys = picked[..., :HEAD_DIM].astype(jnp.float32)
    values = picked[..., HEAD_DIM:].astype(jnp.float32)
    raw_scores = jnp.einsum('cthd,ckd->chtk', query_heads, keys)
    scores = softcap * jnp.tanh(raw_scores / (softcap * jnp.sqrt(jnp.float32(HEAD_DIM))))
    exp_scores = jnp.where(valid[:, None, None, :], jnp.exp(scores), jnp.float32(0.0))
    weights = (exp_scores / lax.optimization_barrier(jnp.sum(exp_scores, axis=-1, keepdims=True))).astype(jnp.bfloat16)
    attended = jnp.einsum('chtk,ckd->cthd', weights.astype(jnp.float32), values).astype(jnp.bfloat16)
    group_count = HEADS // HEADS_GRP
    width = HEADS_GRP * HEAD_DIM
    attended_groups = attended.reshape(TOKENS, group_count, width).transpose(1, 0, 2)
    weight_groups = output_weight.reshape(group_count, width, D)

    def add_group(total, group_pair):
        partial_value = jnp.dot(group_pair[0], group_pair[1], preferred_element_type=jnp.float32).astype(jnp.bfloat16)
        partial_value = lax.optimization_barrier(partial_value)
        return (total + partial_value.astype(jnp.float32), None)
    total, unused = lax.scan(add_group, jnp.zeros((TOKENS, D), jnp.float32), (attended_groups, weight_groups))
    return total.astype(jnp.bfloat16)
```

```python
import functools
import math

import jax
import jax.numpy as jnp
from jax import lax
from jax.experimental import pallas as pl
from jax.experimental.pallas import tpu as pltpu
from jax.sharding import PartitionSpec as P

eps = 1e-05
softcap = 10.0
f32 = jnp.float32
bf16 = jnp.bfloat16

VMEM_LIMIT = 48 * 1024 * 1024


def shift(value, axis, by):
    size = lax.axis_size(axis)
    return lax.ppermute(value, axis, [(i, (i + by) % size) for i in range(size)])


def cost(flops, nbytes, transcendentals=0):
    return pl.CostEstimate(flops=flops, bytes_accessed=nbytes, transcendentals=transcendentals)


def params():
    return pltpu.CompilerParams(vmem_limit_bytes=VMEM_LIMIT)


def encode_kernel(meta, x_ref, w_ref, out_ref, squares, *, pieces, piece, count):
    step = pl.program_id(0)
    mp, sub, size = meta[1], meta[2], pieces // 2
    block, tokens, width = x_ref.shape
    x = x_ref[...].reshape(block * tokens, width)
    product = jnp.dot(x, w_ref[...], preferred_element_type=f32).astype(bf16)
    xf = x.astype(f32)
    square = jnp.sum(xf * xf, axis=1, keepdims=True)
    diagonal = lax.broadcasted_iota(jnp.int32, (piece, 128), 0) == lax.broadcasted_iota(
        jnp.int32, (piece, 128), 1
    )
    for a in range(pieces):
        far_mp = lax.rem(a // 2 - mp + size, size)
        far_sub = lax.rem(a % 2 + sub, 2)
        for n in range(block):
            low = n * tokens + a * piece
            out_ref[far_sub, far_mp, pl.ds(pl.multiple_of((step * block + n) * piece, piece), piece), :] = (
                product[low : low + piece]
            )
            column = jnp.broadcast_to(square[low : low + piece], (piece, 128))
            squares[a, pl.ds(step * block + n, 1), :] = jnp.sum(
                jnp.where(diagonal, column, 0.0), axis=0, keepdims=True
            )

    @pl.when(step == pl.num_programs(0) - 1)
    def _():
        for a in range(pieces):
            far_mp = lax.rem(a // 2 - mp + size, size)
            far_sub = lax.rem(a % 2 + sub, 2)
            out_ref[far_sub, far_mp, pl.ds(count * piece, count), :] = jnp.concatenate(
                [squares[a], jnp.zeros_like(squares[a])], axis=1
            ).astype(bf16)


def encode(meta, states, weight, pieces):
    count, tokens, width = states.shape
    out_width = weight.shape[1]
    piece = tokens // pieces
    rows = count * piece + count
    block = 4
    return pl.pallas_call(
        functools.partial(encode_kernel, pieces=pieces, piece=piece, count=count),
        grid_spec=pltpu.PrefetchScalarGridSpec(
            num_scalar_prefetch=1,
            grid=(count // block,),
            in_specs=[
                pl.BlockSpec((block, tokens, width), lambda i, m: (i, 0, 0)),
                pl.BlockSpec((width, out_width), lambda i, m: (0, 0)),
            ],
            out_specs=pl.BlockSpec((2, pieces // 2, rows, out_width), lambda i, m: (0, 0, 0, 0)),
            scratch_shapes=[pltpu.VMEM((pieces, count, 128), f32)],
        ),
        out_shape=jax.ShapeDtypeStruct((2, pieces // 2, rows, out_width), bf16),
        compiler_params=params(),
        cost_estimate=cost(2 * count * tokens * width * out_width, 2 * count * tokens * width),
        name="encode",
    )(meta, states, weight)


def route_kernel(meta, table, *refs, row_count, cap, piece, count, requests, features, terms):
    ins, outs = refs[:terms], refs[terms : terms + row_count]
    encoded, picks = refs[terms + row_count :]
    me = meta[0]
    total = ins[0][...].astype(f32)
    for ref in ins[1:]:
        total = total + ref[...].astype(f32)
    total = total.reshape(total.shape[-2:])
    scale = lax.rsqrt(total[count * piece :, :128] * (1.0 / features) + eps)
    diagonal = lax.broadcasted_iota(jnp.int32, (piece, 128), 0) == lax.broadcasted_iota(
        jnp.int32, (piece, 128), 1
    )
    for n in range(count):
        row = jnp.broadcast_to(scale[n : n + 1], (piece, 128))
        column = jnp.sum(jnp.where(diagonal, row, 0.0), axis=1, keepdims=True)
        encoded[n] = (total[n * piece : (n + 1) * piece] * column).astype(bf16)
    for d in range(row_count):
        for r in range(cap):
            picks[d, r] = 0
        seen = jnp.int32(0)
        for q in range(requests):
            mine = table[d, q] == me

            @pl.when(mine)
            def _(seen=seen, q=q, d=d):
                picks[d, jnp.minimum(seen, cap - 1)] = table[d, requests + q]

            seen = seen + mine.astype(jnp.int32)
        for r in range(cap):
            outs[d][r] = encoded[picks[d, r]]


def route(meta, table, kept, received, crossed, cap, features, count, requests):
    row_count = table.shape[0]
    rows, width = kept.shape[-2:]
    piece = rows // count - 1
    terms = 2 + len(crossed)
    lead = pl.BlockSpec((None, 1, rows, width), lambda i, m, t: (0, 0, 0, 0))
    return pl.pallas_call(
        functools.partial(
            route_kernel, row_count=row_count, cap=cap, piece=piece, count=count,
            requests=requests, features=features, terms=terms,
        ),
        grid_spec=pltpu.PrefetchScalarGridSpec(
            num_scalar_prefetch=2,
            grid=(1,),
            in_specs=[lead, pl.BlockSpec((1, rows, width), lambda i, m, t: (0, 0, 0))]
            + [pl.BlockSpec((rows, width), lambda i, m, t: (0, 0))] * len(crossed),
            out_specs=[pl.BlockSpec((cap, piece, width), lambda i, m, t: (0, 0, 0))] * row_count,
            scratch_shapes=[
                pltpu.VMEM((count, piece, width), bf16),
                pltpu.SMEM((row_count, cap), jnp.int32),
            ],
        ),
        out_shape=[jax.ShapeDtypeStruct((cap, piece, width), bf16)] * row_count,
        compiler_params=params(),
        cost_estimate=cost(8 * rows * width, 2 * rows * width * terms),
        name="route",
    )(meta, table, kept, received, *crossed)


def query_kernel(blocks, *refs, pieces, features, gain):
    hs, w_ref, out_ref, total, squares = refs[:pieces], *refs[pieces:]
    step = pl.program_id(0)

    @pl.when(step == 0)
    def _():
        total[...] = jnp.zeros_like(total)
        squares[...] = jnp.zeros_like(squares)

    for k in range(pieces):

        @pl.when(step == k)
        def _(k=k):
            h = hs[k][...]
            total[...] += jnp.dot(h, w_ref[...], preferred_element_type=f32)
            hf = h.astype(f32)
            squares[...] += jnp.sum(hf * hf, axis=1, keepdims=True)

    @pl.when(step == pieces - 1)
    def _():
        scale = lax.rsqrt(squares[...] * (1.0 / features) + eps) * gain
        out_ref[...] = (total[...] * scale).astype(bf16)


def project_queries(blocks, parts, weight, gain):
    tokens, width = parts[0].shape
    pieces = len(parts)
    out_width = weight.shape[1]
    return pl.pallas_call(
        functools.partial(query_kernel, pieces=pieces, features=width * pieces, gain=gain),
        grid_spec=pltpu.PrefetchScalarGridSpec(
            num_scalar_prefetch=1,
            grid=(pieces,),
            in_specs=[pl.BlockSpec((tokens, width), lambda i, b: (0, 0))] * pieces
            + [pl.BlockSpec((width, out_width), lambda i, b: (b[i], 0))],
            out_specs=pl.BlockSpec((tokens, out_width), lambda i, b: (0, 0)),
            scratch_shapes=[pltpu.VMEM((tokens, out_width), f32), pltpu.VMEM((tokens, 1), f32)],
        ),
        out_shape=jax.ShapeDtypeStruct((tokens, out_width), bf16),
        compiler_params=params(),
        cost_estimate=cost(2 * tokens * width * pieces * out_width, 2 * width * pieces * out_width),
        name="queries",
    )(blocks, *parts, weight)


def attend_kernel(
    meta, table, live, blocks, *refs, chunk, spans, span, heads, size, pieces, cap, piece, requests
):
    q_ref = refs[0]
    kvs = refs[1 : 1 + pieces]
    w_ref, out_ref, att_ref, pair = refs[1 + pieces :]
    me, mp, sub = meta[0], meta[1], meta[2]
    row_count = table.shape[0]
    group = pieces // 2

    @pl.when(pl.program_id(0) == 0)
    def _():
        local = lax.broadcasted_iota(jnp.int32, (piece, size), 0)
        for c in range(spans):
            masks = []
            for j in range(2):
                q = 2 * (chunk * spans + c) + j
                owner = table[0, q]
                rank = jnp.int32(0)
                for e in range(q):
                    rank = rank + (table[0, e] == owner).astype(jnp.int32)
                slot = lax.rem(me - owner + row_count, row_count) * cap + rank
                length = live[lax.rem(owner - me + row_count, row_count), table[0, requests + q]]
                for p in range(pieces):
                    low = (j * pieces + p) * piece
                    pair[low : low + piece, :] = kvs[p][slot]
                    place = lax.rem(mp - p // 2 + group, group) * 2 + lax.rem(sub + p % 2, 2)
                    masks.append((local + place * piece < length).astype(f32))
            mask = jnp.concatenate(masks, axis=0)
            keys = pair[:, :size]
            values = jnp.concatenate(
                [(pair[:, size:].astype(f32) * mask).astype(bf16), mask.astype(bf16)], axis=1
            )
            rows = slice(c * span, (c + 1) * span)
            query = jnp.concatenate(
                [q_ref[rows, h * size : (h + 1) * size] for h in range(heads)], axis=0
            )
            scores = lax.dot_general(
                query, keys, (((1,), (1,)), ((), ())), preferred_element_type=f32
            )
            weights = jnp.exp(softcap * jnp.tanh(scores)).astype(bf16)
            summed = jnp.dot(weights, values, preferred_element_type=f32)
            attended = (summed[:, :size] / summed[:, size:]).astype(bf16)
            for h in range(heads):
                att_ref[rows, h * size : (h + 1) * size] = attended[h * span : (h + 1) * span]

    out_ref[...] = jnp.dot(att_ref[...], w_ref[...], preferred_element_type=f32).astype(bf16)


def attend(meta, table, live, blocks, queries, pairs, weight, chunk, spans, span, out_width, cap):
    tokens, width = queries.shape
    pieces = len(pairs)
    piece = pairs[0].shape[1]
    pair_width = pairs[0].shape[2]
    size = pair_width // 2
    steps = blocks.shape[0]
    requests = table.shape[1] // 2
    whole = lambda shape: pl.BlockSpec(shape, lambda i, *_: (0,) * len(shape))
    return pl.pallas_call(
        functools.partial(
            attend_kernel, chunk=chunk, spans=spans, span=span, heads=width // size, size=size,
            pieces=pieces, cap=cap, piece=piece, requests=requests,
        ),
        grid_spec=pltpu.PrefetchScalarGridSpec(
            num_scalar_prefetch=4,
            grid=(steps,),
            in_specs=[whole((tokens, width))]
            + [whole(pairs[0].shape)] * pieces
            + [pl.BlockSpec((width, out_width), lambda i, m, t, l, b: (0, b[i]))],
            out_specs=[
                pl.BlockSpec((None, tokens, out_width), lambda i, *_: (i, 0, 0)),
                whole((tokens, width)),
            ],
            scratch_shapes=[pltpu.VMEM((2 * pieces * piece, pair_width), bf16)],
        ),
        out_shape=[
            jax.ShapeDtypeStruct((steps, tokens, out_width), bf16),
            jax.ShapeDtypeStruct((tokens, width), bf16),
        ],
        compiler_params=params(),
        cost_estimate=cost(
            2 * tokens * width * out_width * steps, 2 * width * out_width * steps,
            2 * tokens * width * 2,
        ),
        name="attend",
    )(meta, table, live, blocks, queries, *pairs, weight)


def output_kernel(blocks, a_ref, w_ref, out_ref):
    out_ref[...] = jnp.dot(a_ref[...], w_ref[...], preferred_element_type=f32).astype(bf16)


def project_output(blocks, attended, weight, out_width):
    tokens, width = attended.shape
    steps = blocks.shape[0]
    return pl.pallas_call(
        output_kernel,
        grid_spec=pltpu.PrefetchScalarGridSpec(
            num_scalar_prefetch=1,
            grid=(steps,),
            in_specs=[
                pl.BlockSpec((tokens, width), lambda i, b: (0, 0)),
                pl.BlockSpec((width, out_width), lambda i, b: (0, b[i])),
            ],
            out_specs=pl.BlockSpec((None, tokens, out_width), lambda i, b: (i, 0, 0)),
        ),
        out_shape=jax.ShapeDtypeStruct((steps, tokens, out_width), bf16),
        compiler_params=params(),
        cost_estimate=cost(2 * tokens * width * out_width * steps, 2 * width * out_width * steps),
        name="output",
    )(blocks, attended, weight)


def shards(
    hidden,
    neighbour_states,
    query_weight,
    encoder_weight,
    output_weight,
    neighbour_owner,
    neighbour_slot,
    neighbour_length,
):
    row_count = lax.axis_size("rows")
    group = lax.axis_size("mp")
    pieces = group * lax.axis_size("sub")
    me, mp, sub = lax.axis_index("rows"), lax.axis_index("mp"), lax.axis_index("sub")
    spans_here = neighbour_owner.shape[0]
    count, slot_tokens, feature_shard = neighbour_states.shape
    features = feature_shard * pieces
    size = encoder_weight.shape[1] // 2
    token_count = hidden.shape[0]
    span_tokens = token_count // spans_here
    requests = 2 * spans_here
    cap = max(2, (requests + row_count - 1) // row_count)
    chunks = 4
    chunk_spans = spans_here // chunks
    chunk_tokens = token_count // chunks
    gain = 1.0 / (softcap * math.sqrt(size))
    add = lambda *terms: functools.reduce(
        lambda a, b: a + b, [t.astype(f32) for t in terms]
    ).astype(bf16)

    meta = jnp.stack([me, mp, sub]).astype(jnp.int32)
    gathered_blocks = jnp.stack(
        [((mp - dm + group) % group) * 2 + (sub + ds) % 2 for dm in range(group) for ds in range(2)]
    ).astype(jnp.int32)
    away_blocks = jnp.stack(
        [((mp + dm) % group) * 2 + (sub + ds) % 2 for ds in (1, 0) for dm in range(1, group)]
    ).astype(jnp.int32)
    here_blocks = jnp.stack([mp * 2 + (sub + 1) % 2, mp * 2 + sub]).astype(jnp.int32)

    own = jnp.concatenate(
        [neighbour_owner.reshape(1, -1), neighbour_slot.reshape(1, -1), neighbour_length.reshape(1, -1)],
        axis=1,
    )
    everyone = jnp.concatenate([own] + [shift(own, "rows", -d) for d in range(1, row_count)], axis=0)
    table, live = everyone[:, : 2 * requests], everyone[:, 2 * requests :]

    near = shift(hidden, "sub", 1)
    parts = []
    for c in range(chunks):
        low = c * chunk_tokens
        mine = hidden[low : low + chunk_tokens]
        chunk_parts = [mine, near[low : low + chunk_tokens]]
        for dm in range(1, group):
            far = shift(mine, "mp", dm)
            chunk_parts += [far, shift(far, "sub", 1)]
        parts.append(chunk_parts)

    partial = encode(meta, neighbour_states, encoder_weight, pieces)
    received = shift(partial[1], "sub", 1)
    crossed = []
    for dm in range(1, group):
        crossed.append(shift(add(partial[0, dm], received[dm]), "mp", dm))
    routed = route(meta, table, partial, received, crossed, cap, features, count, requests)
    encoded = jnp.concatenate(
        [routed[0]] + [shift(routed[d], "rows", d) for d in range(1, row_count)], axis=0
    )
    pairs = [encoded, shift(encoded, "sub", 1)]
    for dm in range(1, group):
        far = shift(encoded, "mp", dm)
        pairs += [far, shift(far, "sub", 1)]

    outs = []
    for c in range(chunks):
        queries = project_queries(gathered_blocks, parts[c], query_weight, gain)
        away, attended = attend(
            meta, table, live, away_blocks, queries, pairs, output_weight, c, chunk_spans,
            span_tokens, feature_shard, cap,
        )
        away_received = shift(away[: group - 1], "sub", 1)
        arrived = []
        for dm in range(1, group):
            arrived.append(shift(add(away[group - 1 + dm - 1], away_received[dm - 1]), "mp", dm))
        here = project_output(here_blocks, attended, output_weight, feature_shard)
        here_received = shift(here[0], "sub", 1)
        outs.append(add(here[1], here_received, *arrived))
    return jnp.concatenate(outs, axis=0)


def solution(mesh):
    placed = (
        P(("groups", "rows"), ("mp", "sub")),
        P(("groups", "rows"), None, ("mp", "sub")),
        P(None, ("mp", "sub")),
        P(("mp", "sub"), None),
        P(("mp", "sub"), None),
        P(("groups", "rows"), None),
        P(("groups", "rows"), None),
        P(("groups", "rows")),
    )
    return jax.shard_map(
        shards,
        mesh=mesh,
        in_specs=placed,
        out_specs=P(("groups", "rows"), ("mp", "sub")),
        check_vma=False,
    )
```

```python
import functools
import math

import jax
import jax.numpy as jnp
from jax import lax
from jax.experimental import pallas as pl
from jax.experimental.pallas import tpu as pltpu
from jax.sharding import PartitionSpec as P

eps = 1e-05
softcap = 10.0
f32 = jnp.float32
bf16 = jnp.bfloat16

COST_SCALE = 64
VMEM = pl.BlockSpec(memory_space=pltpu.VMEM)
SMEM = pl.BlockSpec(memory_space=pltpu.SMEM)
HBM = pl.BlockSpec(memory_space=pltpu.HBM)


def shift(value, axis, by):
    size = lax.axis_size(axis)
    return lax.ppermute(value, axis, [(i, (i + by) % size) for i in range(size)])


def swap(value, axis, by):
    size = lax.axis_size(axis)
    return lax.ppermute(value, axis, [(i, i ^ by) for i in range(size)])


def after(value, *earlier):
    return lax.optimization_barrier((value, *earlier))[0]


def cost(flops, nbytes, transcendentals=0):
    return pl.CostEstimate(
        flops=flops // COST_SCALE, bytes_accessed=nbytes // COST_SCALE,
        transcendentals=transcendentals // COST_SCALE,
    )


def params(mib=16):
    return pltpu.CompilerParams(vmem_limit_bytes=mib * 1024 * 1024)


def diagonal_of(piece):
    down = lax.broadcasted_iota(jnp.int32, (piece, 128), 0)
    return down == lax.broadcasted_iota(jnp.int32, (piece, 128), 1)


def encode_kernel(meta, x_hbm, w_ref, kept_ref, sent_ref, held, squares, arrived, *, pieces, piece, block):
    mp, sub, size = meta[1], meta[2], pieces // 2
    count, tokens, width = held.shape
    steps = count // block
    copies = [
        pltpu.make_async_copy(
            x_hbm.at[pl.ds(i * block, block)], held.at[pl.ds(i * block, block)], arrived.at[i]
        )
        for i in range(steps)
    ]
    for copy in copies:
        copy.start()
    diagonal = diagonal_of(piece)

    def store(a, rows, values):
        far_mp = lax.rem(a // 2 - mp + size, size)

        @pl.when(sub == a % 2)
        def _():
            kept_ref[far_mp, rows, :] = values

        @pl.when(sub != a % 2)
        def _():
            sent_ref[far_mp, rows, :] = values

    for i, copy in enumerate(copies):
        copy.wait()
        x = held[i * block : (i + 1) * block].reshape(block * tokens, width)
        product = jnp.dot(x, w_ref[...], preferred_element_type=f32).astype(bf16)
        xf = x.astype(f32)
        square = jnp.sum(xf * xf, axis=1, keepdims=True)
        for a in range(pieces):
            own = []
            for n in range(block):
                low = n * tokens + a * piece
                own.append(product[low : low + piece])
                column = jnp.broadcast_to(square[low : low + piece], (piece, 128))
                squares[a, i * block + n : i * block + n + 1, :] = jnp.sum(
                    jnp.where(diagonal, column, 0.0), axis=0, keepdims=True
                )
            store(a, slice(i * block * piece, (i + 1) * block * piece), jnp.concatenate(own, axis=0))
    for a in range(pieces):
        tail = jnp.concatenate([squares[a], jnp.zeros_like(squares[a])], axis=1)
        store(a, slice(count * piece, count * piece + count), tail.astype(bf16))


def encode(meta, states, weight, pieces):
    count, tokens, width = states.shape
    out_width = weight.shape[1]
    piece = tokens // pieces
    rows = count * piece + count
    block = 4
    return pl.pallas_call(
        functools.partial(encode_kernel, pieces=pieces, piece=piece, block=block),
        in_specs=[SMEM, HBM, VMEM],
        out_specs=[VMEM] * 2,
        scratch_shapes=[
            pltpu.VMEM(states.shape, bf16),
            pltpu.VMEM((pieces, count, 128), f32),
            pltpu.SemaphoreType.DMA((count // block,)),
        ],
        out_shape=[jax.ShapeDtypeStruct((pieces // 2, rows, out_width), bf16)] * 2,
        compiler_params=params(57),
        cost_estimate=cost(2 * count * tokens * width * out_width, 2 * count * tokens * width),
        name="encode",
    )(meta, states, weight)


def join_kernel(a_ref, b_ref, *outs, first):
    for i, out in enumerate(outs):
        out[...] = (a_ref[first + i].astype(f32) + b_ref[first + i].astype(f32)).astype(bf16)


def join(a, b, first=0):
    return pl.pallas_call(
        functools.partial(join_kernel, first=first),
        in_specs=[VMEM, VMEM],
        out_specs=[VMEM] * (a.shape[0] - first),
        out_shape=[jax.ShapeDtypeStruct(a.shape[1:], bf16)] * (a.shape[0] - first),
        compiler_params=params(),
        cost_estimate=cost(a.size, 6 * a.size),
        name="join",
    )(a, b)


def route_kernel(meta, table, kept, received, *refs, row_count, cap, piece, count, requests, features):
    crossed, outs = refs[: -2 - row_count], refs[-2 - row_count : -2]
    encoded, picks = refs[-2:]
    me = meta[0]
    total = kept[0].astype(f32) + received[0].astype(f32)
    for ref in crossed:
        total = total + ref[...].astype(f32)
    scale = lax.rsqrt(total[count * piece :, :128] * (1.0 / features) + eps)
    diagonal = diagonal_of(piece)
    for n in range(count):
        row = jnp.broadcast_to(scale[n : n + 1], (piece, 128))
        column = jnp.sum(jnp.where(diagonal, row, 0.0), axis=1, keepdims=True)
        encoded[n] = (total[n * piece : (n + 1) * piece] * column).astype(bf16)
    for d in range(row_count):
        for r in range(cap):
            picks[d, r] = 0
        seen = jnp.int32(0)
        for q in range(requests):
            mine = table[d, q] == me

            @pl.when(mine)
            def _(seen=seen, q=q, d=d):
                picks[d, jnp.minimum(seen, cap - 1)] = table[d, requests + q]

            seen = seen + mine.astype(jnp.int32)
        for r in range(cap):
            outs[d][r] = encoded[picks[d, r]]


def route(meta, table, kept, received, crossed, cap, features, count, requests):
    row_count = table.shape[0]
    rows, width = kept.shape[-2:]
    piece = rows // count - 1
    return pl.pallas_call(
        functools.partial(
            route_kernel, row_count=row_count, cap=cap, piece=piece, count=count,
            requests=requests, features=features,
        ),
        in_specs=[SMEM] * 2 + [VMEM] * (2 + len(crossed)),
        out_specs=[VMEM] * row_count,
        scratch_shapes=[
            pltpu.VMEM((count, piece, width), bf16),
            pltpu.SMEM((row_count, cap), jnp.int32),
        ],
        out_shape=[jax.ShapeDtypeStruct((cap, piece, width), bf16)] * row_count,
        compiler_params=params(),
        cost_estimate=cost(8 * rows * width, 2 * rows * width * 3),
        name="route",
    )(meta, table, kept, received, *crossed)


def query_kernel(meta, *refs, low, features, gain):
    hs, w_ref, out_ref = refs[:-2], *refs[-2:]
    mp, sub = meta[1], meta[2]
    tokens, width = out_ref.shape[0], hs[0].shape[1]
    group = features // width // 2
    total, squares = None, None
    for k, part in enumerate(hs):
        block = lax.rem(mp - k // 2 + group, group) * 2 + lax.rem(sub + k % 2, 2)
        rows = pl.ds(pl.multiple_of(block * width, width), width)
        h = part[low : low + tokens] if part.shape[0] > tokens else part[...]
        hf = h.astype(f32)
        hf = hf * hf
        for i in range(0, width, 128):
            square = hf[:, i : i + 128]
            squares = square if squares is None else squares + square
        product = jnp.dot(h, w_ref[rows, :], preferred_element_type=f32)
        total = product if total is None else total + product
    squares = jnp.sum(squares, axis=1, keepdims=True)
    out_ref[...] = (total * (lax.rsqrt(squares * (1.0 / features) + eps) * gain)).astype(bf16)


def project_queries(meta, parts, weight, low, tokens, gain):
    depth, out_width = weight.shape
    return pl.pallas_call(
        functools.partial(query_kernel, low=low, features=depth, gain=gain),
        in_specs=[SMEM] + [VMEM] * (len(parts) + 1),
        out_specs=VMEM,
        out_shape=jax.ShapeDtypeStruct((tokens, out_width), bf16),
        compiler_params=params(),
        cost_estimate=cost(2 * tokens * depth * out_width, 2 * tokens * depth),
        name="queries",
    )(meta, *parts, weight)


def column_block(meta, dm, ds, w_ref, width):
    group = w_ref.shape[1] // width // 2
    block = lax.rem(meta[1] + dm, group) * 2 + lax.rem(meta[2] + ds, 2)
    return w_ref[:, pl.ds(pl.multiple_of(block * width, width), width)]


def attend_kernel(
    meta, table, live, *refs, first, low, span, heads, size, pieces, cap, piece, requests
):
    q_ref = refs[0]
    kvs = refs[1 : 1 + pieces]
    w_ref, kept_ref, sent_ref, att_ref, pair = refs[1 + pieces :]
    me, mp, sub = meta[0], meta[1], meta[2]
    group = pieces // 2
    local = lax.broadcasted_iota(jnp.int32, (piece, size), 0)
    for c in range(pair.shape[0]):
        masks = []
        for j in range(2):
            q = 2 * (first + c) + j
            owner = table[0, q]
            rank = jnp.int32(0)
            for e in range(q):
                rank = rank + (table[0, e] == owner).astype(jnp.int32)
            away = owner ^ me
            slot = away * cap + rank
            length = live[away, table[0, requests + q]]
            for p in range(pieces):
                at = (j * pieces + p) * piece
                pair[c, at : at + piece, :] = kvs[p][slot]
                place = lax.rem(mp - p // 2 + group, group) * 2 + lax.rem(sub + p % 2, 2)
                masks.append((local + place * piece < length).astype(f32))
        mask = jnp.concatenate(masks, axis=0)
        keys = pair[c, :, :size]
        values = jnp.concatenate(
            [(pair[c, :, size:].astype(f32) * mask).astype(bf16), mask.astype(bf16)], axis=1
        )
        rows = slice(c * span, (c + 1) * span)
        query = jnp.concatenate(
            [
                q_ref[low + c * span : low + (c + 1) * span, h * size : (h + 1) * size]
                for h in range(heads)
            ],
            axis=0,
        )
        scores = lax.dot_general(query, keys, (((1,), (1,)), ((), ())), preferred_element_type=f32)
        weights = jnp.exp(softcap * jnp.tanh(scores)).astype(bf16)
        summed = jnp.dot(weights, values, preferred_element_type=f32)
        attended = (summed[:, :size] / summed[:, size:]).astype(bf16)
        for h in range(heads):
            att_ref[rows, h * size : (h + 1) * size] = attended[h * span : (h + 1) * span]
    width = kept_ref.shape[2]
    for ds, out_ref in ((1, sent_ref), (0, kept_ref)):
        for dm in range(1, group):
            w = column_block(meta, dm, ds, w_ref, width)
            out_ref[dm - 1] = jnp.dot(att_ref[...], w, preferred_element_type=f32).astype(bf16)


def attend(meta, table, live, queries, pairs, weight, first, low, spans, span, out_width, cap):
    width = queries.shape[1]
    tokens = spans * span
    pieces = len(pairs)
    piece, pair_width = pairs[0].shape[1:]
    size = pair_width // 2
    steps = pieces // 2 - 1
    requests = table.shape[1] // 2
    return pl.pallas_call(
        functools.partial(
            attend_kernel, first=first, low=low, span=span, heads=width // size, size=size,
            pieces=pieces, cap=cap, piece=piece, requests=requests,
        ),
        in_specs=[SMEM] * 3 + [VMEM] * (2 + pieces),
        out_specs=[VMEM] * 3,
        scratch_shapes=[pltpu.VMEM((spans, 2 * pieces * piece, pair_width), bf16)],
        out_shape=[
            jax.ShapeDtypeStruct((steps, tokens, out_width), bf16),
            jax.ShapeDtypeStruct((steps, tokens, out_width), bf16),
            jax.ShapeDtypeStruct((tokens, width), bf16),
        ],
        compiler_params=params(),
        cost_estimate=cost(
            4 * tokens * width * out_width * steps + 4 * tokens * width * 2 * pieces * piece,
            2 * tokens * width, 2 * tokens * width * 2,
        ),
        name="attend",
    )(meta, table, live, queries, *pairs, weight)


def output_kernel(meta, a_ref, w_ref, kept_ref, sent_ref):
    for ds, out_ref in ((1, sent_ref), (0, kept_ref)):
        w = column_block(meta, 0, ds, w_ref, out_ref.shape[1])
        out_ref[...] = jnp.dot(a_ref[...], w, preferred_element_type=f32).astype(bf16)


def project_output(meta, attended, weight, out_width):
    tokens, width = attended.shape
    return pl.pallas_call(
        output_kernel,
        in_specs=[SMEM, VMEM, VMEM],
        out_specs=[VMEM] * 2,
        out_shape=[jax.ShapeDtypeStruct((tokens, out_width), bf16)] * 2,
        compiler_params=params(),
        cost_estimate=cost(4 * tokens * width * out_width, 2 * tokens * width),
        name="output",
    )(meta, attended, weight)


def shards(
    hidden,
    neighbour_states,
    query_weight,
    encoder_weight,
    output_weight,
    neighbour_owner,
    neighbour_slot,
    neighbour_length,
):
    row_count = lax.axis_size("rows")
    group = lax.axis_size("mp")
    pieces = group * lax.axis_size("sub")
    me, mp, sub = lax.axis_index("rows"), lax.axis_index("mp"), lax.axis_index("sub")
    spans_here = neighbour_owner.shape[0]
    count, slot_tokens, feature_shard = neighbour_states.shape
    features = feature_shard * pieces
    size = encoder_weight.shape[1] // 2
    token_count = hidden.shape[0]
    span_tokens = token_count // spans_here
    requests = 2 * spans_here
    cap = max(2, (requests + row_count - 1) // row_count)
    halves, chunks = 2, 4
    half_tokens, chunk_tokens = token_count // halves, token_count // chunks
    chunk_spans = spans_here // chunks
    gain = 1.0 / (softcap * math.sqrt(size))
    add = lambda *terms: functools.reduce(
        lambda a, b: a + b, [t.astype(f32) for t in terms]
    ).astype(bf16)

    meta = jnp.stack([me, mp, sub]).astype(jnp.int32)

    kept, sent = encode(meta, neighbour_states, encoder_weight, pieces)
    received = shift(sent, "sub", 1)
    leaving = join(kept, received, 1)
    crossed = [shift(leaving[dm - 1], "mp", dm) for dm in range(1, group)]

    def cross(c, *earlier):
        mine = after(hidden, *earlier)[c * half_tokens : (c + 1) * half_tokens]
        return [shift(mine, "mp", dm) for dm in range(1, group)]

    def queries_of(c, crossed, *earlier):
        parts = [hidden, near]
        for far in lax.optimization_barrier((crossed, *earlier))[0]:
            parts += [far, shift(far, "sub", 1)]
        return project_queries(meta, parts, query_weight, c * half_tokens, half_tokens, gain)

    fars = cross(0, *leaving)

    own = jnp.concatenate(
        [neighbour_owner.reshape(1, -1), neighbour_slot.reshape(1, -1), neighbour_length.reshape(1, -1)],
        axis=1,
    )
    own = after(own, *leaving)
    everyone = jnp.concatenate([own] + [swap(own, "rows", d) for d in range(1, row_count)], axis=0)
    table, live = everyone[:, : 2 * requests], everyone[:, 2 * requests :]
    near = shift(after(hidden, table), "sub", 1)

    routed = route(meta, table, kept, received, crossed, cap, features, count, requests)
    encoded = jnp.concatenate(
        [routed[0]]
        + list(lax.optimization_barrier([swap(routed[d], "rows", d) for d in range(1, row_count)])),
        axis=0,
    )
    pairs = [encoded, shift(encoded, "sub", 1)]
    for dm in range(1, group):
        far = shift(encoded, "mp", dm)
        pairs += [far, shift(far, "sub", 1)]
    queries = queries_of(0, fars, encoded)
    fars = cross(1, encoded)

    terms, outs = [], []
    earlier = []
    for c in range(chunks):
        half, low = divmod(c * chunk_tokens, half_tokens)
        if half and not low:
            queries = queries_of(half, fars, *earlier)
        kept, sent, attended = attend(
            meta, table, live, after(queries, *earlier, *outs[-1:]), pairs, output_weight,
            c * chunk_spans, low, chunk_spans, span_tokens, feature_shard, cap,
        )
        received = shift(sent, "sub", 1)
        here_kept, here_sent = project_output(meta, attended, output_weight, feature_shard)
        leaving = join(kept, after(received, here_kept))
        arrived = [shift(leaving[dm - 1], "mp", dm) for dm in range(1, group)]
        here = add(here_kept, shift(here_sent, "sub", 1))
        earlier = [*leaving, here]
        terms.append([here, *arrived])
        if c:
            outs.append(add(after(terms[c - 1][0], *earlier), *terms[c - 1][1:]))
    outs.append(add(*terms[-1]))
    return jnp.concatenate(outs, axis=0)


def solution(mesh):
    placed = (
        P(("groups", "rows"), ("mp", "sub")),
        P(("groups", "rows"), None, ("mp", "sub")),
        P(None, ("mp", "sub")),
        P(("mp", "sub"), None),
        P(("mp", "sub"), None),
        P(("groups", "rows"), None),
        P(("groups", "rows"), None),
        P(("groups", "rows")),
    )
    return jax.shard_map(
        shards,
        mesh=mesh,
        in_specs=placed,
        out_specs=P(("groups", "rows"), ("mp", "sub")),
        check_vma=False,
    )
```

```python
import functools
import math

import jax
import jax.numpy as jnp
from jax import lax
from jax.experimental import pallas as pl
from jax.experimental.pallas import tpu as pltpu
from jax.sharding import PartitionSpec as P

eps = 1e-05
softcap = 10.0
FIRST = 48
f32 = jnp.float32
bf16 = jnp.bfloat16

VMEM = pl.BlockSpec(memory_space=pltpu.VMEM)
SMEM = pl.BlockSpec(memory_space=pltpu.SMEM)


def shift(value, axis, by):
    size = lax.axis_size(axis)
    return lax.ppermute(value, axis, [(i, (i + by) % size) for i in range(size)])


def swap(value, axis, by):
    size = lax.axis_size(axis)
    return lax.ppermute(value, axis, [(i, i ^ by) for i in range(size)])


def after(value, *earlier):
    return lax.optimization_barrier((value, *earlier))[0]


def cost(flops, nbytes, transcendentals=0):
    return pl.CostEstimate(flops=flops, bytes_accessed=nbytes, transcendentals=transcendentals)


def params():
    return pltpu.CompilerParams(vmem_limit_bytes=16 * 1024 * 1024)


def diagonal_of(piece):
    down = lax.broadcasted_iota(jnp.int32, (piece, 128), 0)
    return down == lax.broadcasted_iota(jnp.int32, (piece, 128), 1)


def encode_kernel(meta, x_ref, w_ref, kept_ref, sent_ref, squares, *, pieces, piece, block):
    mp, sub, size = meta[1], meta[2], pieces // 2
    count, tokens, width = x_ref.shape
    diagonal = diagonal_of(piece)

    def store(a, rows, values):
        far_mp = lax.rem(a // 2 - mp + size, size)

        @pl.when(sub == a % 2)
        def _():
            kept_ref[far_mp, rows, :] = values

        @pl.when(sub != a % 2)
        def _():
            sent_ref[far_mp, rows, :] = values

    for i in range(count // block):
        x = x_ref[i * block : (i + 1) * block].reshape(block * tokens, width)
        product = jnp.dot(x, w_ref[...], preferred_element_type=f32).astype(bf16)
        lanes = None
        for j in range(0, width, 128):
            part = x[:, j : j + 128].astype(f32)
            lanes = part * part if lanes is None else lanes + part * part
        square = jnp.sum(lanes, axis=1, keepdims=True)
        for a in range(pieces):
            own = []
            for n in range(block):
                low = n * tokens + a * piece
                own.append(product[low : low + piece])
                column = jnp.broadcast_to(square[low : low + piece], (piece, 128))
                squares[a, i * block + n : i * block + n + 1, :] = jnp.sum(
                    jnp.where(diagonal, column, 0.0), axis=0, keepdims=True
                )
            store(a, slice(i * block * piece, (i + 1) * block * piece), jnp.concatenate(own, axis=0))
    for a in range(pieces):
        tail = jnp.concatenate([squares[a], jnp.zeros_like(squares[a])], axis=1)
        store(a, slice(count * piece, count * piece + count), tail.astype(bf16))


def encode(meta, states, weight, pieces):
    count, tokens, width = states.shape
    out_width = weight.shape[1]
    piece = tokens // pieces
    rows = count * piece + count
    return pl.pallas_call(
        functools.partial(encode_kernel, pieces=pieces, piece=piece, block=2),
        in_specs=[SMEM, VMEM, VMEM],
        out_specs=[VMEM] * 2,
        scratch_shapes=[pltpu.VMEM((pieces, count, 128), f32)],
        out_shape=[jax.ShapeDtypeStruct((pieces // 2, rows, out_width), bf16)] * 2,
        compiler_params=params(),
        cost_estimate=cost(2 * count * tokens * width * out_width, 2 * count * tokens * width),
        name="encode",
    )(meta, states, weight)


def route_kernel(meta, table, kept, received, *refs, row_count, cap, piece, count, requests, features):
    crossed, outs = refs[: -2 - row_count], refs[-2 - row_count : -2]
    encoded, picks = refs[-2:]
    me = meta[0]
    total = kept[0].astype(f32) + received[0].astype(f32)
    for ref in crossed:
        total = total + ref[...].astype(f32)
    scale = lax.rsqrt(total[count * piece :, :128] * (1.0 / features) + eps)
    diagonal = diagonal_of(piece)
    for n in range(count):
        row = jnp.broadcast_to(scale[n : n + 1], (piece, 128))
        column = jnp.sum(jnp.where(diagonal, row, 0.0), axis=1, keepdims=True)
        encoded[n] = (total[n * piece : (n + 1) * piece] * column).astype(bf16)
    for d in range(row_count):
        for r in range(cap):
            picks[d, r] = 0
        seen = jnp.int32(0)
        for q in range(requests):
            mine = table[d, q] == me

            @pl.when(mine)
            def _(seen=seen, q=q, d=d):
                picks[d, jnp.minimum(seen, cap - 1)] = table[d, requests + q]

            seen = seen + mine.astype(jnp.int32)
        for r in range(cap):
            outs[d][r] = encoded[picks[d, r]]


def route(meta, table, kept, received, crossed, cap, features, count, requests):
    row_count = table.shape[0]
    rows, width = kept.shape[-2:]
    piece = rows // count - 1
    return pl.pallas_call(
        functools.partial(
            route_kernel, row_count=row_count, cap=cap, piece=piece, count=count,
            requests=requests, features=features,
        ),
        in_specs=[SMEM] * 2 + [VMEM] * (2 + len(crossed)),
        out_specs=[VMEM] * row_count,
        scratch_shapes=[
            pltpu.VMEM((count, piece, width), bf16),
            pltpu.SMEM((row_count, cap), jnp.int32),
        ],
        out_shape=[jax.ShapeDtypeStruct((cap, piece, width), bf16)] * row_count,
        compiler_params=params(),
        cost_estimate=cost(8 * rows * width, 2 * rows * width * 3),
        name="route",
    )(meta, table, kept, received, *crossed)


def queries_from(meta, hs, w_ref, low, gain):
    mp, sub = meta[1], meta[2]
    tokens, width = hs[-1].shape
    features = w_ref.shape[0]
    group = features // width // 2
    total, squares = None, None
    for k, part in enumerate(hs):
        block = lax.rem(mp - k // 2 + group, group) * 2 + lax.rem(sub + k % 2, 2)
        rows = pl.ds(pl.multiple_of(block * width, width), width)
        h = part[low : low + tokens] if k < 2 else part[...]
        for i in range(0, width, 128):
            square = h[:, i : i + 128].astype(f32)
            square = square * square
            squares = square if squares is None else squares + square
        product = jnp.dot(h, w_ref[rows, :], preferred_element_type=f32)
        total = product if total is None else total + product
    squares = jnp.sum(squares, axis=1, keepdims=True)
    return (total * (lax.rsqrt(squares * (1.0 / features) + eps) * gain)).astype(bf16)


def query_kernel(meta, own_ref, near_ref, *refs, lows, gain):
    fars, w_ref, out_ref = refs[:-2], *refs[-2:]
    each = len(fars) // len(lows)
    for i, low in enumerate(lows):
        far = fars[i * each : (i + 1) * each]
        out_ref[low : low + far[0].shape[0], :] = queries_from(
            meta, (own_ref, near_ref, *far), w_ref, low, gain
        )


def project_queries(meta, own, near, segments, weight, gain):
    lows, tokens = [], 0
    for far in segments:
        lows.append(tokens)
        tokens += far[0].shape[0]
    parts = [own, near] + [part for far in segments for part in far]
    depth, out_width = weight.shape
    return pl.pallas_call(
        functools.partial(query_kernel, lows=tuple(lows), gain=gain),
        in_specs=[SMEM] + [VMEM] * (len(parts) + 1),
        out_specs=VMEM,
        out_shape=jax.ShapeDtypeStruct((tokens, out_width), bf16),
        compiler_params=params(),
        cost_estimate=cost(2 * tokens * depth * out_width, 2 * tokens * depth),
        name="queries",
    )(meta, *parts, weight)


def chunk_kernel(
    meta, table, live, *refs, first, low, span, heads, size, pieces, cap, requests, gain
):
    sources, kvs = refs[: -5 - pieces], refs[-5 - pieces : -5]
    w_ref, kept_ref, sent_ref, att, pair = refs[-5:]
    me, mp, sub = meta[0], meta[1], meta[2]
    group = pieces // 2
    piece = kvs[0].shape[1]
    tokens = att.shape[0]
    if len(sources) == 1:
        queries = sources[0][low : low + tokens]
    else:
        queries = queries_from(meta, sources[:-1], sources[-1], low, gain)
    local = lax.broadcasted_iota(jnp.int32, (piece, size), 0)
    for c in range(pair.shape[0]):
        masks = []
        for j in range(2):
            q = 2 * (first + c) + j
            owner = table[0, q]
            rank = jnp.int32(0)
            for e in range(q):
                rank = rank + (table[0, e] == owner).astype(jnp.int32)
            away = owner ^ me
            slot = away * cap + rank
            length = live[away, table[0, requests + q]]
            for p in range(pieces):
                at = (j * pieces + p) * piece
                pair[c, at : at + piece, :] = kvs[p][slot]
                place = lax.rem(mp - p // 2 + group, group) * 2 + lax.rem(sub + p % 2, 2)
                masks.append((local + place * piece < length).astype(f32))
        mask = jnp.concatenate(masks, axis=0)
        keys = pair[c, :, :size]
        values = jnp.concatenate(
            [(pair[c, :, size:].astype(f32) * mask).astype(bf16), mask.astype(bf16)], axis=1
        )
        rows = slice(c * span, (c + 1) * span)
        query = jnp.concatenate(
            [queries[rows, h * size : (h + 1) * size] for h in range(heads)], axis=0
        )
        scores = lax.dot_general(query, keys, (((1,), (1,)), ((), ())), preferred_element_type=f32)
        weights = jnp.exp(softcap * jnp.tanh(scores)).astype(bf16)
        summed = jnp.dot(weights, values, preferred_element_type=f32)
        attended = (summed[:, :size] / summed[:, size:]).astype(bf16)
        for h in range(heads):
            att[rows, h * size : (h + 1) * size] = attended[h * span : (h + 1) * span]
    width = kept_ref.shape[2]
    for ds, out_ref in ((1, sent_ref), (0, kept_ref)):
        for dm in range(group):
            block = lax.rem(mp + dm, group) * 2 + lax.rem(sub + ds, 2)
            w = w_ref[:, pl.ds(pl.multiple_of(block * width, width), width)]
            out_ref[dm] = jnp.dot(att[...], w, preferred_element_type=f32).astype(bf16)


def run_chunk(meta, table, live, sources, pairs, weight, first, low, spans, span, out_width, cap, gain):
    width = weight.shape[0]
    tokens = spans * span
    pieces = len(pairs)
    piece, pair_width = pairs[0].shape[1:]
    size = pair_width // 2
    group = pieces // 2
    requests = table.shape[1] // 2
    return pl.pallas_call(
        functools.partial(
            chunk_kernel, first=first, low=low, span=span, heads=width // size, size=size,
            pieces=pieces, cap=cap, requests=requests, gain=gain,
        ),
        in_specs=[SMEM] * 3 + [VMEM] * (1 + pieces + len(sources)),
        out_specs=[VMEM] * 2,
        scratch_shapes=[
            pltpu.VMEM((tokens, width), bf16),
            pltpu.VMEM((spans, 2 * pieces * piece, pair_width), bf16),
        ],
        out_shape=[jax.ShapeDtypeStruct((group, tokens, out_width), bf16)] * 2,
        compiler_params=params(),
        cost_estimate=cost(
            4 * tokens * width * out_width * group + 4 * tokens * width * 2 * pieces * piece,
            2 * tokens * width, 2 * tokens * width * 2,
        ),
        name="chunk",
    )(meta, table, live, *sources, *pairs, weight)


def shards(
    hidden,
    neighbour_states,
    query_weight,
    encoder_weight,
    output_weight,
    neighbour_owner,
    neighbour_slot,
    neighbour_length,
):
    row_count = lax.axis_size("rows")
    group = lax.axis_size("mp")
    pieces = group * lax.axis_size("sub")
    me, mp, sub = lax.axis_index("rows"), lax.axis_index("mp"), lax.axis_index("sub")
    spans_here = neighbour_owner.shape[0]
    count, slot_tokens, feature_shard = neighbour_states.shape
    features = feature_shard * pieces
    size = encoder_weight.shape[1] // 2
    token_count = hidden.shape[0]
    span_tokens = token_count // spans_here
    requests = 2 * spans_here
    cap = max(2, (requests + row_count - 1) // row_count)
    chunks = 4
    chunk_spans = spans_here // chunks
    chunk_tokens = token_count // chunks
    gain = 1.0 / (softcap * math.sqrt(size))
    add = lambda *terms: functools.reduce(
        lambda a, b: a + b, [t.astype(f32) for t in terms]
    ).astype(bf16)

    meta = jnp.stack([me, mp, sub]).astype(jnp.int32)

    def cross(mine):
        return [shift(mine, "mp", dm) for dm in range(1, group)]

    def with_near(fars, *earlier):
        out = []
        for far in lax.optimization_barrier((fars, *earlier))[0]:
            out += [far, shift(far, "sub", 1)]
        return out

    fars_first = cross(hidden[:FIRST])

    table = jnp.concatenate(
        [neighbour_owner.reshape(1, -1), neighbour_slot.reshape(1, -1), neighbour_length.reshape(1, -1)],
        axis=1,
    )
    table = jnp.concatenate([table, swap(table, "rows", 1)], axis=0)

    kept, sent = encode(meta, neighbour_states, encoder_weight, pieces)
    received = after(shift(after(sent, *fars_first), "sub", 1), table)
    leaving = [add(kept[dm], received[dm]) for dm in range(1, group)]
    crossed = [shift(leaving[dm - 1], "mp", dm) for dm in range(1, group)]
    near = shift(after(hidden, *leaving), "sub", 1)
    table = after(table, *leaving)
    while table.shape[0] < row_count:
        table = jnp.concatenate([table, swap(table, "rows", table.shape[0])], axis=0)
    table, live = table[:, : 2 * requests], table[:, 2 * requests :]

    fars_rest = cross(after(hidden, table, *crossed)[FIRST:])

    routed = route(meta, table, kept, received, crossed, cap, features, count, requests)
    encoded = jnp.concatenate(
        [routed[0]]
        + list(lax.optimization_barrier([swap(routed[d], "rows", d) for d in range(1, row_count)])),
        axis=0,
    )
    pairs = [encoded, shift(encoded, "sub", 1)]
    fars = [shift(encoded, "mp", dm) for dm in range(1, group)]
    queries = project_queries(
        after(meta, encoded), hidden, near,
        [with_near(fars_first, encoded), with_near(fars_rest, encoded)], query_weight, gain,
    )
    pairs += with_near(fars, queries)

    kept, sent, received, leaving, arrived, outs = [], [], [], [], [], []

    def send(c, *earlier):
        got = after(received[c], *earlier)
        leaving.append([add(kept[c][dm], got[dm]) for dm in range(1, group)])
        arrived.append([shift(leaving[c][dm - 1], "mp", dm) for dm in range(1, group)])

    def total(c, *earlier):
        outs.append(add(after(kept[c], *earlier)[0], received[c][0], *arrived[c]))

    for c in range(chunks):
        gate = (leaving[c - 2] if c > 1 else []) + ([outs[c - 3]] if c > 2 else [])
        one, other = run_chunk(
            after(meta, *gate), table, live, [queries], pairs, output_weight, c * chunk_spans,
            c * chunk_tokens, chunk_spans, span_tokens, feature_shard, cap, gain,
        )
        kept.append(one)
        if c:
            send(c - 1, one)
            other = after(other, *leaving[c - 1])
        if c > 1:
            total(c - 2, *leaving[c - 1])
        if c > 1 and c == chunks - 1:
            other = after(other, outs[-1])
        received.append(shift(other, "sub", 1))
    send(chunks - 1)
    total(chunks - 2, *leaving[-1])
    total(chunks - 1)
    return jnp.concatenate(outs, axis=0)


def solution(mesh):
    placed = (
        P(("groups", "rows"), ("mp", "sub")),
        P(("groups", "rows"), None, ("mp", "sub")),
        P(None, ("mp", "sub")),
        P(("mp", "sub"), None),
        P(("mp", "sub"), None),
        P(("groups", "rows"), None),
        P(("groups", "rows"), None),
        P(("groups", "rows")),
    )
    return jax.shard_map(
        shards,
        mesh=mesh,
        in_specs=placed,
        out_specs=P(("groups", "rows"), ("mp", "sub")),
        check_vma=False,
    )
```

```python
import functools
import math

import jax
import jax.numpy as jnp
from jax import lax
from jax.experimental import pallas as pl
from jax.experimental.pallas import tpu as pltpu
from jax.sharding import PartitionSpec as P

eps = 1e-05
softcap = 10.0
f32 = jnp.float32
bf16 = jnp.bfloat16

VMEM = pl.BlockSpec(memory_space=pltpu.VMEM)
SMEM = pl.BlockSpec(memory_space=pltpu.SMEM)


def shift(value, axis, by):
    size = lax.axis_size(axis)
    return lax.ppermute(value, axis, [(i, (i + by) % size) for i in range(size)])


def swap(value, axis, by):
    size = lax.axis_size(axis)
    return lax.ppermute(value, axis, [(i, i ^ by) for i in range(size)])


def after(value, *earlier):
    return lax.optimization_barrier((value, *earlier))[0]


def cost(flops, nbytes, transcendentals=0):
    return pl.CostEstimate(flops=flops, bytes_accessed=nbytes, transcendentals=transcendentals)


def params():
    return pltpu.CompilerParams(vmem_limit_bytes=16 * 1024 * 1024)


def diagonal_of(piece):
    down = lax.broadcasted_iota(jnp.int32, (piece, 128), 0)
    return down == lax.broadcasted_iota(jnp.int32, (piece, 128), 1)


def encode_kernel(meta, x_ref, w_ref, kept_ref, sent_ref, product, squares, *, pieces, piece, count):
    step = pl.program_id(0)
    mp, sub, size = meta[1], meta[2], pieces // 2
    block, tokens, width = x_ref.shape
    x = x_ref[...].reshape(block * tokens, width)
    product[...] = jnp.dot(x, w_ref[...], preferred_element_type=f32).astype(bf16).reshape(product.shape)
    xf = x.astype(f32)
    square = jnp.sum(xf * xf, axis=1, keepdims=True)
    diagonal = diagonal_of(piece)
    for a in range(pieces):
        for n in range(block):
            low = n * tokens + a * piece
            column = jnp.broadcast_to(square[low : low + piece], (piece, 128))
            squares[a, pl.ds(step * block + n, 1), :] = jnp.sum(
                jnp.where(diagonal, column, 0.0), axis=0, keepdims=True
            )
    rows = pl.ds(pl.multiple_of(step * block * piece, block * piece), block * piece)
    for ds, out_ref in ((0, kept_ref), (1, sent_ref)):
        for dm in range(size):
            a = lax.rem(mp + dm, size) * 2 + lax.rem(sub + ds, 2)
            taken = product[:, pl.ds(pl.multiple_of(a * piece, piece), piece), :]
            out_ref[dm, rows, :] = taken.reshape(block * piece, taken.shape[2])

    @pl.when(step == pl.num_programs(0) - 1)
    def _():
        for ds, out_ref in ((0, kept_ref), (1, sent_ref)):
            for dm in range(size):
                a = lax.rem(mp + dm, size) * 2 + lax.rem(sub + ds, 2)
                tail = jnp.concatenate([squares[a], jnp.zeros_like(squares[a])], axis=1)
                out_ref[dm, pl.ds(count * piece, count), :] = tail.astype(bf16)


def encode(meta, states, weight, pieces):
    count, tokens, width = states.shape
    out_width = weight.shape[1]
    piece = tokens // pieces
    rows = count * piece + count
    block = 4
    return pl.pallas_call(
        functools.partial(encode_kernel, pieces=pieces, piece=piece, count=count),
        grid_spec=pltpu.PrefetchScalarGridSpec(
            num_scalar_prefetch=1,
            grid=(count // block,),
            in_specs=[
                pl.BlockSpec((block, tokens, width), lambda i, m: (i, 0, 0)),
                pl.BlockSpec((width, out_width), lambda i, m: (0, 0)),
            ],
            out_specs=[pl.BlockSpec((pieces // 2, rows, out_width), lambda i, m: (0, 0, 0))] * 2,
            scratch_shapes=[
                pltpu.VMEM((block, tokens, out_width), bf16),
                pltpu.VMEM((pieces, count, 128), f32),
            ],
        ),
        out_shape=[jax.ShapeDtypeStruct((pieces // 2, rows, out_width), bf16)] * 2,
        compiler_params=params(),
        cost_estimate=cost(2 * count * tokens * width * out_width, 2 * count * tokens * width),
        name="encode",
    )(meta, states, weight)


def route_kernel(meta, table, kept, received, *refs, row_count, cap, piece, count, requests, features):
    crossed, outs = refs[: -2 - row_count], refs[-2 - row_count : -2]
    encoded, picks = refs[-2:]
    me = meta[0]
    total = kept[0].astype(f32) + received[0].astype(f32)
    for ref in crossed:
        total = total + ref[...].astype(f32)
    scale = lax.rsqrt(total[count * piece :, :128] * (1.0 / features) + eps)
    diagonal = diagonal_of(piece)
    for n in range(count):
        row = jnp.broadcast_to(scale[n : n + 1], (piece, 128))
        column = jnp.sum(jnp.where(diagonal, row, 0.0), axis=1, keepdims=True)
        encoded[n] = (total[n * piece : (n + 1) * piece] * column).astype(bf16)
    for d in range(row_count):
        for r in range(cap):
            picks[d, r] = 0
        seen = jnp.int32(0)
        for q in range(requests):
            mine = table[d, q] == me

            @pl.when(mine)
            def _(seen=seen, q=q, d=d):
                picks[d, jnp.minimum(seen, cap - 1)] = table[d, requests + q]

            seen = seen + mine.astype(jnp.int32)
        for r in range(cap):
            outs[d][r] = encoded[picks[d, r]]


def route(meta, table, kept, received, crossed, cap, features, count, requests):
    row_count = table.shape[0]
    rows, width = kept.shape[-2:]
    piece = rows // count - 1
    return pl.pallas_call(
        functools.partial(
            route_kernel, row_count=row_count, cap=cap, piece=piece, count=count,
            requests=requests, features=features,
        ),
        in_specs=[SMEM] * 2 + [VMEM] * (2 + len(crossed)),
        out_specs=[VMEM] * row_count,
        scratch_shapes=[
            pltpu.VMEM((count, piece, width), bf16),
            pltpu.SMEM((row_count, cap), jnp.int32),
        ],
        out_shape=[jax.ShapeDtypeStruct((cap, piece, width), bf16)] * row_count,
        compiler_params=params(),
        cost_estimate=cost(8 * rows * width, 2 * rows * width * 3),
        name="route",
    )(meta, table, kept, received, *crossed)


def queries_from(meta, hs, w_ref, low, gain):
    mp, sub = meta[1], meta[2]
    tokens, width = hs[-1].shape
    features = w_ref.shape[0]
    group = features // width // 2
    total, squares = None, None
    for k, part in enumerate(hs):
        block = lax.rem(mp - k // 2 + group, group) * 2 + lax.rem(sub + k % 2, 2)
        rows = pl.ds(pl.multiple_of(block * width, width), width)
        h = part[low : low + tokens] if k < 2 else part[...]
        for i in range(0, width, 128):
            square = h[:, i : i + 128].astype(f32)
            square = square * square
            squares = square if squares is None else squares + square
        product = jnp.dot(h, w_ref[rows, :], preferred_element_type=f32)
        total = product if total is None else total + product
    squares = jnp.sum(squares, axis=1, keepdims=True)
    return (total * (lax.rsqrt(squares * (1.0 / features) + eps) * gain)).astype(bf16)


def query_kernel(meta, own_ref, near_ref, *refs, lows, gain):
    fars, w_ref, out_ref = refs[:-2], *refs[-2:]
    each = len(fars) // len(lows)
    for i, low in enumerate(lows):
        far = fars[i * each : (i + 1) * each]
        out_ref[low : low + far[0].shape[0], :] = queries_from(
            meta, (own_ref, near_ref, *far), w_ref, low, gain
        )


def project_queries(meta, own, near, segments, weight, gain):
    lows, tokens = [], 0
    for far in segments:
        lows.append(tokens)
        tokens += far[0].shape[0]
    parts = [own, near] + [part for far in segments for part in far]
    depth, out_width = weight.shape
    return pl.pallas_call(
        functools.partial(query_kernel, lows=tuple(lows), gain=gain),
        in_specs=[SMEM] + [VMEM] * (len(parts) + 1),
        out_specs=VMEM,
        out_shape=jax.ShapeDtypeStruct((tokens, out_width), bf16),
        compiler_params=params(),
        cost_estimate=cost(2 * tokens * depth * out_width, 2 * tokens * depth),
        name="queries",
    )(meta, *parts, weight)


def chunk_kernel(
    meta, table, live, *refs, first, low, span, heads, size, pieces, cap, requests, gain
):
    sources, kvs = refs[: -5 - pieces], refs[-5 - pieces : -5]
    w_ref, kept_ref, sent_ref, att, pair = refs[-5:]
    me, mp, sub = meta[0], meta[1], meta[2]
    group = pieces // 2
    piece = kvs[0].shape[1]
    tokens = att.shape[0]
    if len(sources) == 1:
        queries = sources[0][low : low + tokens]
    else:
        queries = queries_from(meta, sources[:-1], sources[-1], low, gain)
    local = lax.broadcasted_iota(jnp.int32, (piece, size), 0)
    for c in range(pair.shape[0]):
        masks = []
        for j in range(2):
            q = 2 * (first + c) + j
            owner = table[0, q]
            rank = jnp.int32(0)
            for e in range(q):
                rank = rank + (table[0, e] == owner).astype(jnp.int32)
            away = owner ^ me
            slot = away * cap + rank
            length = live[away, table[0, requests + q]]
            for p in range(pieces):
                at = (j * pieces + p) * piece
                pair[c, at : at + piece, :] = kvs[p][slot]
                place = lax.rem(mp - p // 2 + group, group) * 2 + lax.rem(sub + p % 2, 2)
                masks.append((local + place * piece < length).astype(f32))
        mask = jnp.concatenate(masks, axis=0)
        keys = pair[c, :, :size]
        values = jnp.concatenate(
            [(pair[c, :, size:].astype(f32) * mask).astype(bf16), mask.astype(bf16)], axis=1
        )
        rows = slice(c * span, (c + 1) * span)
        query = jnp.concatenate(
            [queries[rows, h * size : (h + 1) * size] for h in range(heads)], axis=0
        )
        scores = lax.dot_general(query, keys, (((1,), (1,)), ((), ())), preferred_element_type=f32)
        weights = jnp.exp(softcap * jnp.tanh(scores)).astype(bf16)
        summed = jnp.dot(weights, values, preferred_element_type=f32)
        attended = (summed[:, :size] / summed[:, size:]).astype(bf16)
        for h in range(heads):
            att[rows, h * size : (h + 1) * size] = attended[h * span : (h + 1) * span]
    width = kept_ref.shape[2]
    for ds, out_ref in ((1, sent_ref), (0, kept_ref)):
        for dm in range(group):
            block = lax.rem(mp + dm, group) * 2 + lax.rem(sub + ds, 2)
            w = w_ref[:, pl.ds(pl.multiple_of(block * width, width), width)]
            out_ref[dm] = jnp.dot(att[...], w, preferred_element_type=f32).astype(bf16)


def run_chunk(meta, table, live, sources, pairs, weight, first, low, spans, span, out_width, cap, gain):
    width = weight.shape[0]
    tokens = spans * span
    pieces = len(pairs)
    piece, pair_width = pairs[0].shape[1:]
    size = pair_width // 2
    group = pieces // 2
    requests = table.shape[1] // 2
    return pl.pallas_call(
        functools.partial(
            chunk_kernel, first=first, low=low, span=span, heads=width // size, size=size,
            pieces=pieces, cap=cap, requests=requests, gain=gain,
        ),
        in_specs=[SMEM] * 3 + [VMEM] * (1 + pieces + len(sources)),
        out_specs=[VMEM] * 2,
        scratch_shapes=[
            pltpu.VMEM((tokens, width), bf16),
            pltpu.VMEM((spans, 2 * pieces * piece, pair_width), bf16),
        ],
        out_shape=[jax.ShapeDtypeStruct((group, tokens, out_width), bf16)] * 2,
        compiler_params=params(),
        cost_estimate=cost(
            4 * tokens * width * out_width * group + 4 * tokens * width * 2 * pieces * piece,
            2 * tokens * width, 2 * tokens * width * 2,
        ),
        name="chunk",
    )(meta, table, live, *sources, *pairs, weight)


def shards(
    hidden,
    neighbour_states,
    query_weight,
    encoder_weight,
    output_weight,
    neighbour_owner,
    neighbour_slot,
    neighbour_length,
):
    row_count = lax.axis_size("rows")
    group = lax.axis_size("mp")
    pieces = group * lax.axis_size("sub")
    me, mp, sub = lax.axis_index("rows"), lax.axis_index("mp"), lax.axis_index("sub")
    spans_here = neighbour_owner.shape[0]
    count, slot_tokens, feature_shard = neighbour_states.shape
    features = feature_shard * pieces
    size = encoder_weight.shape[1] // 2
    token_count = hidden.shape[0]
    span_tokens = token_count // spans_here
    requests = 2 * spans_here
    cap = max(2, (requests + row_count - 1) // row_count)
    chunks = 4
    chunk_spans = spans_here // chunks
    chunk_tokens = token_count // chunks
    gain = 1.0 / (softcap * math.sqrt(size))
    add = lambda *terms: functools.reduce(
        lambda a, b: a + b, [t.astype(f32) for t in terms]
    ).astype(bf16)

    meta = jnp.stack([me, mp, sub]).astype(jnp.int32)

    def cross(mine):
        return [shift(mine, "mp", dm) for dm in range(1, group)]

    def with_near(fars, *earlier):
        out = []
        for far in lax.optimization_barrier((fars, *earlier))[0]:
            out += [far, shift(far, "sub", 1)]
        return out

    fars_first = cross(hidden[:chunk_tokens])

    table = jnp.concatenate(
        [neighbour_owner.reshape(1, -1), neighbour_slot.reshape(1, -1), neighbour_length.reshape(1, -1)],
        axis=1,
    )

    kept, sent = encode(meta, neighbour_states, encoder_weight, pieces)
    received = shift(after(sent, *fars_first), "sub", 1)
    leaving = [add(kept[dm], received[dm]) for dm in range(1, group)]
    crossed = [shift(leaving[dm - 1], "mp", dm) for dm in range(1, group)]
    near = shift(after(hidden, *leaving), "sub", 1)
    table = after(table, *leaving)
    while table.shape[0] < row_count:
        table = jnp.concatenate([table, swap(table, "rows", table.shape[0])], axis=0)
    table, live = table[:, : 2 * requests], table[:, 2 * requests :]

    last_low = token_count - chunk_tokens
    fars_second = cross(after(hidden, table, *crossed)[chunk_tokens:last_low])

    routed = route(meta, table, kept, received, crossed, cap, features, count, requests)
    encoded = jnp.concatenate(
        [routed[0]]
        + list(lax.optimization_barrier([swap(routed[d], "rows", d) for d in range(1, row_count)])),
        axis=0,
    )
    pairs = [encoded, shift(encoded, "sub", 1)]
    fars = [shift(encoded, "mp", dm) for dm in range(1, group)]
    queries = project_queries(
        after(meta, encoded), hidden, near,
        [with_near(fars_first, encoded), with_near(fars_second, encoded)], query_weight, gain,
    )
    fars_last = cross(after(hidden, encoded)[last_low:])
    pairs += with_near(fars, queries)

    kept, sent, received, leaving, arrived, outs = [], [], [], [], [], []

    def send(c, *earlier):
        got = after(received[c], *earlier)
        leaving.append([add(kept[c][dm], got[dm]) for dm in range(1, group)])
        arrived.append([shift(leaving[c][dm - 1], "mp", dm) for dm in range(1, group)])

    def total(c, *earlier):
        outs.append(add(after(kept[c], *earlier)[0], received[c][0], *arrived[c]))

    for c in range(chunks):
        sources = [queries]
        if c == chunks - 1:
            sources = [hidden, near, *with_near(fars_last, *leaving[0]), query_weight]
        gate = (fars_last if c == 2 else []) + (leaving[c - 2] if c > 1 else []) + ([outs[c - 3]] if c > 2 else [])
        one, other = run_chunk(
            after(meta, *gate), table, live, sources, pairs, output_weight, c * chunk_spans,
            c * chunk_tokens, chunk_spans, span_tokens, feature_shard, cap, gain,
        )
        kept.append(one)
        if c:
            send(c - 1, one)
            other = after(other, *leaving[c - 1])
        if c > 1:
            total(c - 2, *leaving[c - 1])
        if c > 1 and c == chunks - 1:
            other = after(other, outs[-1])
        received.append(shift(other, "sub", 1))
    send(chunks - 1)
    total(chunks - 2, *leaving[-1])
    total(chunks - 1)
    return jnp.concatenate(outs, axis=0)


def solution(mesh):
    placed = (
        P(("groups", "rows"), ("mp", "sub")),
        P(("groups", "rows"), None, ("mp", "sub")),
        P(None, ("mp", "sub")),
        P(("mp", "sub"), None),
        P(("mp", "sub"), None),
        P(("groups", "rows"), None),
        P(("groups", "rows"), None),
        P(("groups", "rows")),
    )
    return jax.shard_map(
        shards,
        mesh=mesh,
        in_specs=placed,
        out_specs=P(("groups", "rows"), ("mp", "sub")),
        check_vma=False,
    )
```

```python
import functools
import math

import jax
import jax.numpy as jnp
from jax import lax
from jax.experimental import pallas as pl
from jax.experimental.pallas import tpu as pltpu
from jax.sharding import PartitionSpec as P

eps = 1e-05
softcap = 10.0
f32 = jnp.float32
bf16 = jnp.bfloat16

VMEM = pl.BlockSpec(memory_space=pltpu.VMEM)
SMEM = pl.BlockSpec(memory_space=pltpu.SMEM)


def shift(value, axis, by):
    size = lax.axis_size(axis)
    return lax.ppermute(value, axis, [(i, (i + by) % size) for i in range(size)])


def swap(value, axis, by):
    size = lax.axis_size(axis)
    return lax.ppermute(value, axis, [(i, i ^ by) for i in range(size)])


def after(value, *earlier):
    return lax.optimization_barrier((value, *earlier))[0]


def cost(flops, nbytes, transcendentals=0):
    return pl.CostEstimate(flops=flops, bytes_accessed=nbytes, transcendentals=transcendentals)


def params():
    return pltpu.CompilerParams(vmem_limit_bytes=16 * 1024 * 1024)


def diagonal_of(piece):
    down = lax.broadcasted_iota(jnp.int32, (piece, 128), 0)
    return down == lax.broadcasted_iota(jnp.int32, (piece, 128), 1)


def encode_kernel(meta, x_ref, w_ref, kept_ref, sent_ref, product, squares, *, pieces, piece, count):
    step = pl.program_id(0)
    mp, sub, size = meta[1], meta[2], pieces // 2
    block, tokens, width = x_ref.shape
    x = x_ref[...].reshape(block * tokens, width)
    product[...] = jnp.dot(x, w_ref[...], preferred_element_type=f32).astype(bf16).reshape(product.shape)
    xf = x.astype(f32)
    square = jnp.sum(xf * xf, axis=1, keepdims=True)
    diagonal = diagonal_of(piece)
    for a in range(pieces):
        for n in range(block):
            low = n * tokens + a * piece
            column = jnp.broadcast_to(square[low : low + piece], (piece, 128))
            squares[a, pl.ds(step * block + n, 1), :] = jnp.sum(
                jnp.where(diagonal, column, 0.0), axis=0, keepdims=True
            )
    rows = pl.ds(pl.multiple_of(step * block * piece, block * piece), block * piece)
    for ds, out_ref in ((0, kept_ref), (1, sent_ref)):
        for dm in range(size):
            a = lax.rem(mp + dm, size) * 2 + lax.rem(sub + ds, 2)
            taken = product[:, pl.ds(pl.multiple_of(a * piece, piece), piece), :]
            out_ref[dm, rows, :] = taken.reshape(block * piece, taken.shape[2])

    @pl.when(step == pl.num_programs(0) - 1)
    def _():
        for ds, out_ref in ((0, kept_ref), (1, sent_ref)):
            for dm in range(size):
                a = lax.rem(mp + dm, size) * 2 + lax.rem(sub + ds, 2)
                tail = jnp.concatenate([squares[a], jnp.zeros_like(squares[a])], axis=1)
                out_ref[dm, pl.ds(count * piece, count), :] = tail.astype(bf16)


def encode(meta, states, weight, pieces):
    count, tokens, width = states.shape
    out_width = weight.shape[1]
    piece = tokens // pieces
    rows = count * piece + count
    block = 4
    return pl.pallas_call(
        functools.partial(encode_kernel, pieces=pieces, piece=piece, count=count),
        grid_spec=pltpu.PrefetchScalarGridSpec(
            num_scalar_prefetch=1,
            grid=(count // block,),
            in_specs=[
                pl.BlockSpec((block, tokens, width), lambda i, m: (i, 0, 0)),
                pl.BlockSpec((width, out_width), lambda i, m: (0, 0)),
            ],
            out_specs=[pl.BlockSpec((pieces // 2, rows, out_width), lambda i, m: (0, 0, 0))] * 2,
            scratch_shapes=[
                pltpu.VMEM((block, tokens, out_width), bf16),
                pltpu.VMEM((pieces, count, 128), f32),
            ],
        ),
        out_shape=[jax.ShapeDtypeStruct((pieces // 2, rows, out_width), bf16)] * 2,
        compiler_params=params(),
        cost_estimate=cost(2 * count * tokens * width * out_width, 2 * count * tokens * width),
        name="encode",
    )(meta, states, weight)


def route_kernel(meta, table, kept, received, *refs, row_count, cap, piece, count, requests, features):
    crossed, outs = refs[: -2 - row_count], refs[-2 - row_count : -2]
    encoded, picks = refs[-2:]
    me = meta[0]
    total = kept[0].astype(f32) + received[0].astype(f32)
    for ref in crossed:
        total = total + ref[...].astype(f32)
    scale = lax.rsqrt(total[count * piece :, :128] * (1.0 / features) + eps)
    diagonal = diagonal_of(piece)
    for n in range(count):
        row = jnp.broadcast_to(scale[n : n + 1], (piece, 128))
        column = jnp.sum(jnp.where(diagonal, row, 0.0), axis=1, keepdims=True)
        encoded[n] = (total[n * piece : (n + 1) * piece] * column).astype(bf16)
    for d in range(row_count):
        for r in range(cap):
            picks[d, r] = 0
        seen = jnp.int32(0)
        for q in range(requests):
            mine = table[d, q] == me

            @pl.when(mine)
            def _(seen=seen, q=q, d=d):
                picks[d, jnp.minimum(seen, cap - 1)] = table[d, requests + q]

            seen = seen + mine.astype(jnp.int32)
        for r in range(cap):
            outs[d][r] = encoded[picks[d, r]]


def route(meta, table, kept, received, crossed, cap, features, count, requests):
    row_count = table.shape[0]
    rows, width = kept.shape[-2:]
    piece = rows // count - 1
    return pl.pallas_call(
        functools.partial(
            route_kernel, row_count=row_count, cap=cap, piece=piece, count=count,
            requests=requests, features=features,
        ),
        in_specs=[SMEM] * 2 + [VMEM] * (2 + len(crossed)),
        out_specs=[VMEM] * row_count,
        scratch_shapes=[
            pltpu.VMEM((count, piece, width), bf16),
            pltpu.SMEM((row_count, cap), jnp.int32),
        ],
        out_shape=[jax.ShapeDtypeStruct((cap, piece, width), bf16)] * row_count,
        compiler_params=params(),
        cost_estimate=cost(8 * rows * width, 2 * rows * width * 3),
        name="route",
    )(meta, table, kept, received, *crossed)


def queries_from(meta, hs, w_ref, low, gain):
    mp, sub = meta[1], meta[2]
    tokens, width = hs[-1].shape
    features = w_ref.shape[0]
    group = features // width // 2
    total, squares = None, None
    for k, part in enumerate(hs):
        block = lax.rem(mp - k // 2 + group, group) * 2 + lax.rem(sub + k % 2, 2)
        rows = pl.ds(pl.multiple_of(block * width, width), width)
        h = part[low : low + tokens] if k < 2 else part[...]
        for i in range(0, width, 128):
            square = h[:, i : i + 128].astype(f32)
            square = square * square
            squares = square if squares is None else squares + square
        product = jnp.dot(h, w_ref[rows, :], preferred_element_type=f32)
        total = product if total is None else total + product
    squares = jnp.sum(squares, axis=1, keepdims=True)
    return (total * (lax.rsqrt(squares * (1.0 / features) + eps) * gain)).astype(bf16)


def query_kernel(meta, own_ref, near_ref, *refs, lows, gain):
    fars, w_ref, out_ref = refs[:-2], *refs[-2:]
    each = len(fars) // len(lows)
    for i, low in enumerate(lows):
        far = fars[i * each : (i + 1) * each]
        out_ref[low : low + far[0].shape[0], :] = queries_from(
            meta, (own_ref, near_ref, *far), w_ref, low, gain
        )


def project_queries(meta, own, near, segments, weight, gain):
    lows, tokens = [], 0
    for far in segments:
        lows.append(tokens)
        tokens += far[0].shape[0]
    parts = [own, near] + [part for far in segments for part in far]
    depth, out_width = weight.shape
    return pl.pallas_call(
        functools.partial(query_kernel, lows=tuple(lows), gain=gain),
        in_specs=[SMEM] + [VMEM] * (len(parts) + 1),
        out_specs=VMEM,
        out_shape=jax.ShapeDtypeStruct((tokens, out_width), bf16),
        compiler_params=params(),
        cost_estimate=cost(2 * tokens * depth * out_width, 2 * tokens * depth),
        name="queries",
    )(meta, *parts, weight)


def chunk_kernel(
    meta, table, live, *refs, first, low, span, heads, size, pieces, cap, requests, gain
):
    sources, kvs = refs[: -6 - pieces], refs[-6 - pieces : -6]
    w_ref, kept_ref, upper_ref, lower_ref, att, pair = refs[-6:]
    me, mp, sub = meta[0], meta[1], meta[2]
    group = pieces // 2
    piece = kvs[0].shape[1]
    tokens = att.shape[0]
    if len(sources) == 1:
        queries = sources[0][low : low + tokens]
    else:
        queries = queries_from(meta, sources[:-1], sources[-1], low, gain)
    local = lax.broadcasted_iota(jnp.int32, (piece, size), 0)
    for c in range(pair.shape[0]):
        masks = []
        for j in range(2):
            q = 2 * (first + c) + j
            owner = table[0, q]
            rank = jnp.int32(0)
            for e in range(q):
                rank = rank + (table[0, e] == owner).astype(jnp.int32)
            away = owner ^ me
            slot = away * cap + rank
            length = live[away, table[0, requests + q]]
            for p in range(pieces):
                at = (j * pieces + p) * piece
                pair[c, at : at + piece, :] = kvs[p][slot]
                place = lax.rem(mp - p // 2 + group, group) * 2 + lax.rem(sub + p % 2, 2)
                masks.append((local + place * piece < length).astype(f32))
        mask = jnp.concatenate(masks, axis=0)
        keys = pair[c, :, :size]
        values = jnp.concatenate(
            [(pair[c, :, size:].astype(f32) * mask).astype(bf16), mask.astype(bf16)], axis=1
        )
        rows = slice(c * span, (c + 1) * span)
        query = jnp.concatenate(
            [queries[rows, h * size : (h + 1) * size] for h in range(heads)], axis=0
        )
        scores = lax.dot_general(query, keys, (((1,), (1,)), ((), ())), preferred_element_type=f32)
        weights = jnp.exp(softcap * jnp.tanh(scores)).astype(bf16)
        summed = jnp.dot(weights, values, preferred_element_type=f32)
        attended = (summed[:, :size] / summed[:, size:]).astype(bf16)
        for h in range(heads):
            att[rows, h * size : (h + 1) * size] = attended[h * span : (h + 1) * span]
    width = kept_ref.shape[2]
    half = tokens // 2
    for ds in (1, 0):
        for dm in range(group):
            block = lax.rem(mp + dm, group) * 2 + lax.rem(sub + ds, 2)
            w = w_ref[:, pl.ds(pl.multiple_of(block * width, width), width)]
            result = jnp.dot(att[...], w, preferred_element_type=f32).astype(bf16)
            if ds:
                upper_ref[dm] = result[:half]
                lower_ref[dm] = result[half:]
            else:
                kept_ref[dm] = result


def run_chunk(meta, table, live, sources, pairs, weight, first, low, spans, span, out_width, cap, gain):
    width = weight.shape[0]
    tokens = spans * span
    pieces = len(pairs)
    piece, pair_width = pairs[0].shape[1:]
    size = pair_width // 2
    group = pieces // 2
    requests = table.shape[1] // 2
    return pl.pallas_call(
        functools.partial(
            chunk_kernel, first=first, low=low, span=span, heads=width // size, size=size,
            pieces=pieces, cap=cap, requests=requests, gain=gain,
        ),
        in_specs=[SMEM] * 3 + [VMEM] * (1 + pieces + len(sources)),
        out_specs=[VMEM] * 3,
        scratch_shapes=[
            pltpu.VMEM((tokens, width), bf16),
            pltpu.VMEM((spans, 2 * pieces * piece, pair_width), bf16),
        ],
        out_shape=[
            jax.ShapeDtypeStruct((group, tokens, out_width), bf16),
            jax.ShapeDtypeStruct((group, tokens // 2, out_width), bf16),
            jax.ShapeDtypeStruct((group, tokens // 2, out_width), bf16),
        ],
        compiler_params=params(),
        cost_estimate=cost(
            4 * tokens * width * out_width * group + 4 * tokens * width * 2 * pieces * piece,
            2 * tokens * width, 2 * tokens * width * 2,
        ),
        name="chunk",
    )(meta, table, live, *sources, *pairs, weight)


def shards(
    hidden,
    neighbour_states,
    query_weight,
    encoder_weight,
    output_weight,
    neighbour_owner,
    neighbour_slot,
    neighbour_length,
):
    row_count = lax.axis_size("rows")
    group = lax.axis_size("mp")
    pieces = group * lax.axis_size("sub")
    me, mp, sub = lax.axis_index("rows"), lax.axis_index("mp"), lax.axis_index("sub")
    spans_here = neighbour_owner.shape[0]
    count, slot_tokens, feature_shard = neighbour_states.shape
    features = feature_shard * pieces
    size = encoder_weight.shape[1] // 2
    token_count = hidden.shape[0]
    span_tokens = token_count // spans_here
    requests = 2 * spans_here
    cap = max(2, (requests + row_count - 1) // row_count)
    chunks = 4
    chunk_spans = spans_here // chunks
    chunk_tokens = token_count // chunks
    gain = 1.0 / (softcap * math.sqrt(size))
    add = lambda *terms: functools.reduce(
        lambda a, b: a + b, [t.astype(f32) for t in terms]
    ).astype(bf16)

    meta = jnp.stack([me, mp, sub]).astype(jnp.int32)

    def cross(mine):
        return [shift(mine, "mp", dm) for dm in range(1, group)]

    def with_near(fars, *earlier):
        out = []
        for far in lax.optimization_barrier((fars, *earlier))[0]:
            out += [far, shift(far, "sub", 1)]
        return out

    fars_first = cross(hidden[:chunk_tokens])

    table = jnp.concatenate(
        [neighbour_owner.reshape(1, -1), neighbour_slot.reshape(1, -1), neighbour_length.reshape(1, -1)],
        axis=1,
    )
    table = jnp.concatenate([table, swap(table, "rows", 1)], axis=0)

    kept, sent = encode(meta, neighbour_states, encoder_weight, pieces)
    received = shift(after(sent, table, *fars_first), "sub", 1)
    leaving = [add(kept[dm], received[dm]) for dm in range(1, group)]
    crossed = [shift(leaving[dm - 1], "mp", dm) for dm in range(1, group)]
    near = shift(after(hidden, *leaving), "sub", 1)
    table = after(table, *leaving)
    while table.shape[0] < row_count:
        table = jnp.concatenate([table, swap(table, "rows", table.shape[0])], axis=0)
    table, live = table[:, : 2 * requests], table[:, 2 * requests :]

    last_low = token_count - chunk_tokens
    fars_second = cross(after(hidden, table, *crossed)[chunk_tokens:last_low])

    routed = route(meta, table, kept, received, crossed, cap, features, count, requests)
    encoded = jnp.concatenate(
        [routed[0]]
        + list(lax.optimization_barrier([swap(routed[d], "rows", d) for d in range(1, row_count)])),
        axis=0,
    )
    pairs = [encoded, shift(encoded, "sub", 1)]
    fars = [shift(encoded, "mp", dm) for dm in range(1, group)]
    queries = project_queries(
        after(meta, encoded), hidden, near,
        [with_near(fars_first, encoded), with_near(fars_second, encoded)], query_weight, gain,
    )
    fars_last = cross(after(hidden, encoded)[last_low:])
    pairs += with_near(fars, queries)

    def join(c, *earlier):
        got = after(received[c], *earlier)
        step = chunk_tokens // 2
        parts = [
            [add(kept[c][dm, i * step : (i + 1) * step], g[dm]) for i, g in enumerate(got)]
            for dm in range(1, group)
        ]
        return [jnp.concatenate(p, axis=0) for p in parts]

    kept, received, leaving, arrived, outs = [], [], [], [], []

    def total(c, *earlier):
        got = jnp.concatenate([g[0] for g in received[c]], axis=0)
        outs.append(add(after(kept[c], *earlier)[0], got, *arrived[c]))

    for c in range(chunks):
        sources, low = [queries], c * chunk_tokens
        if c == chunks - 1:
            sources = [hidden, near, *with_near(fars_last, *leaving[0]), query_weight]
        gate = (leaving[c - 1] if c else []) + ([outs[c - 2]] if c > 1 else [])
        one, *others = run_chunk(
            after(meta, *gate), table, live, sources, pairs, output_weight, c * chunk_spans,
            low, chunk_spans, span_tokens, feature_shard, cap, gain,
        )
        kept.append(one)
        received.append([shift(other, "sub", 1) for other in others])
        leaving.append(join(c, *([] if c else fars_last)))
        arrived.append([shift(leaving[c][dm - 1], "mp", dm) for dm in range(1, group)])
        if c:
            total(c - 1, *leaving[c])
    total(chunks - 1)
    mixed = jnp.zeros((token_count, feature_shard), bf16)
    for c, out in enumerate(outs):
        mixed = lax.dynamic_update_slice(after(mixed, meta), out, (c * chunk_tokens, 0))
    return mixed


def solution(mesh):
    placed = (
        P(("groups", "rows"), ("mp", "sub")),
        P(("groups", "rows"), None, ("mp", "sub")),
        P(None, ("mp", "sub")),
        P(("mp", "sub"), None),
        P(("mp", "sub"), None),
        P(("groups", "rows"), None),
        P(("groups", "rows"), None),
        P(("groups", "rows")),
    )
    return jax.shard_map(
        shards,
        mesh=mesh,
        in_specs=placed,
        out_specs=P(("groups", "rows"), ("mp", "sub")),
        check_vma=False,
    )
```

```python
import functools
import math

import jax
import jax.numpy as jnp
from jax import lax
from jax.experimental import pallas as pl
from jax.experimental.pallas import tpu as pltpu
from jax.sharding import PartitionSpec as P

eps = 1e-05
softcap = 10.0
f32 = jnp.float32
bf16 = jnp.bfloat16

VMEM = pl.BlockSpec(memory_space=pltpu.VMEM)
SMEM = pl.BlockSpec(memory_space=pltpu.SMEM)


def shift(value, axis, by):
    size = lax.axis_size(axis)
    return lax.ppermute(value, axis, [(i, (i + by) % size) for i in range(size)])


def swap(value, axis, by):
    size = lax.axis_size(axis)
    return lax.ppermute(value, axis, [(i, i ^ by) for i in range(size)])


def after(value, *earlier):
    return lax.optimization_barrier((value, *earlier))[0]


def cost(flops, nbytes, transcendentals=0):
    return pl.CostEstimate(flops=flops, bytes_accessed=nbytes, transcendentals=transcendentals)


def params():
    return pltpu.CompilerParams(vmem_limit_bytes=16 * 1024 * 1024)


def diagonal_of(piece):
    down = lax.broadcasted_iota(jnp.int32, (piece, 128), 0)
    return down == lax.broadcasted_iota(jnp.int32, (piece, 128), 1)


def encode_kernel(meta, x_ref, w_ref, kept_ref, sent_ref, product, squares, *, pieces, piece, count):
    step = pl.program_id(0)
    mp, sub, size = meta[1], meta[2], pieces // 2
    block, tokens, width = x_ref.shape
    x = x_ref[...].reshape(block * tokens, width)
    product[...] = jnp.dot(x, w_ref[...], preferred_element_type=f32).astype(bf16).reshape(product.shape)
    xf = x.astype(f32)
    square = jnp.sum(xf * xf, axis=1, keepdims=True)
    diagonal = diagonal_of(piece)
    for a in range(pieces):
        for n in range(block):
            low = n * tokens + a * piece
            column = jnp.broadcast_to(square[low : low + piece], (piece, 128))
            squares[a, pl.ds(step * block + n, 1), :] = jnp.sum(
                jnp.where(diagonal, column, 0.0), axis=0, keepdims=True
            )
    rows = pl.ds(pl.multiple_of(step * block * piece, block * piece), block * piece)
    for ds, out_ref in ((0, kept_ref), (1, sent_ref)):
        for dm in range(size):
            a = lax.rem(mp + dm, size) * 2 + lax.rem(sub + ds, 2)
            taken = product[:, pl.ds(pl.multiple_of(a * piece, piece), piece), :]
            out_ref[dm, rows, :] = taken.reshape(block * piece, taken.shape[2])

    @pl.when(step == pl.num_programs(0) - 1)
    def _():
        for ds, out_ref in ((0, kept_ref), (1, sent_ref)):
            for dm in range(size):
                a = lax.rem(mp + dm, size) * 2 + lax.rem(sub + ds, 2)
                tail = jnp.concatenate([squares[a], jnp.zeros_like(squares[a])], axis=1)
                out_ref[dm, pl.ds(count * piece, count), :] = tail.astype(bf16)


def encode(meta, states, weight, pieces):
    count, tokens, width = states.shape
    out_width = weight.shape[1]
    piece = tokens // pieces
    rows = count * piece + count
    block = 4
    return pl.pallas_call(
        functools.partial(encode_kernel, pieces=pieces, piece=piece, count=count),
        grid_spec=pltpu.PrefetchScalarGridSpec(
            num_scalar_prefetch=1,
            grid=(count // block,),
            in_specs=[
                pl.BlockSpec((block, tokens, width), lambda i, m: (i, 0, 0)),
                pl.BlockSpec((width, out_width), lambda i, m: (0, 0)),
            ],
            out_specs=[pl.BlockSpec((pieces // 2, rows, out_width), lambda i, m: (0, 0, 0))] * 2,
            scratch_shapes=[
                pltpu.VMEM((block, tokens, out_width), bf16),
                pltpu.VMEM((pieces, count, 128), f32),
            ],
        ),
        out_shape=[jax.ShapeDtypeStruct((pieces // 2, rows, out_width), bf16)] * 2,
        compiler_params=params(),
        cost_estimate=cost(2 * count * tokens * width * out_width, 2 * count * tokens * width),
        name="encode",
    )(meta, states, weight)


def route_kernel(meta, table, kept, received, *refs, row_count, cap, piece, count, requests, features):
    crossed, outs = refs[: -2 - row_count], refs[-2 - row_count : -2]
    encoded, picks = refs[-2:]
    me = meta[0]
    total = kept[0].astype(f32) + received[0].astype(f32)
    for ref in crossed:
        total = total + ref[...].astype(f32)
    scale = lax.rsqrt(total[count * piece :, :128] * (1.0 / features) + eps)
    diagonal = diagonal_of(piece)
    for n in range(count):
        row = jnp.broadcast_to(scale[n : n + 1], (piece, 128))
        column = jnp.sum(jnp.where(diagonal, row, 0.0), axis=1, keepdims=True)
        encoded[n] = (total[n * piece : (n + 1) * piece] * column).astype(bf16)
    for d in range(row_count):
        for r in range(cap):
            picks[d, r] = 0
        seen = jnp.int32(0)
        for q in range(requests):
            mine = table[d, q] == me

            @pl.when(mine)
            def _(seen=seen, q=q, d=d):
                picks[d, jnp.minimum(seen, cap - 1)] = table[d, requests + q]

            seen = seen + mine.astype(jnp.int32)
        for r in range(cap):
            outs[d][r] = encoded[picks[d, r]]


def route(meta, table, kept, received, crossed, cap, features, count, requests):
    row_count = table.shape[0]
    rows, width = kept.shape[-2:]
    piece = rows // count - 1
    return pl.pallas_call(
        functools.partial(
            route_kernel, row_count=row_count, cap=cap, piece=piece, count=count,
            requests=requests, features=features,
        ),
        in_specs=[SMEM] * 2 + [VMEM] * (2 + len(crossed)),
        out_specs=[VMEM] * row_count,
        scratch_shapes=[
            pltpu.VMEM((count, piece, width), bf16),
            pltpu.SMEM((row_count, cap), jnp.int32),
        ],
        out_shape=[jax.ShapeDtypeStruct((cap, piece, width), bf16)] * row_count,
        compiler_params=params(),
        cost_estimate=cost(8 * rows * width, 2 * rows * width * 3),
        name="route",
    )(meta, table, kept, received, *crossed)


def queries_from(meta, hs, w_ref, low, gain):
    mp, sub = meta[1], meta[2]
    tokens, width = hs[-1].shape
    features = w_ref.shape[0]
    group = features // width // 2
    total, squares = None, None
    for k, part in enumerate(hs):
        block = lax.rem(mp - k // 2 + group, group) * 2 + lax.rem(sub + k % 2, 2)
        rows = pl.ds(pl.multiple_of(block * width, width), width)
        h = part[low : low + tokens] if k < 2 else part[...]
        for i in range(0, width, 128):
            square = h[:, i : i + 128].astype(f32)
            square = square * square
            squares = square if squares is None else squares + square
        product = jnp.dot(h, w_ref[rows, :], preferred_element_type=f32)
        total = product if total is None else total + product
    squares = jnp.sum(squares, axis=1, keepdims=True)
    return (total * (lax.rsqrt(squares * (1.0 / features) + eps) * gain)).astype(bf16)


def query_kernel(meta, own_ref, near_ref, *refs, lows, gain):
    fars, w_ref, out_ref = refs[:-2], *refs[-2:]
    each = len(fars) // len(lows)
    for i, low in enumerate(lows):
        far = fars[i * each : (i + 1) * each]
        out_ref[low : low + far[0].shape[0], :] = queries_from(
            meta, (own_ref, near_ref, *far), w_ref, low, gain
        )


def project_queries(meta, own, near, segments, weight, gain):
    lows, tokens = [], 0
    for far in segments:
        lows.append(tokens)
        tokens += far[0].shape[0]
    parts = [own, near] + [part for far in segments for part in far]
    depth, out_width = weight.shape
    return pl.pallas_call(
        functools.partial(query_kernel, lows=tuple(lows), gain=gain),
        in_specs=[SMEM] + [VMEM] * (len(parts) + 1),
        out_specs=VMEM,
        out_shape=jax.ShapeDtypeStruct((tokens, out_width), bf16),
        compiler_params=params(),
        cost_estimate=cost(2 * tokens * depth * out_width, 2 * tokens * depth),
        name="queries",
    )(meta, *parts, weight)


def chunk_kernel(
    meta, table, live, *refs, first, low, span, heads, size, pieces, cap, requests, gain
):
    sources, kvs = refs[: -6 - pieces], refs[-6 - pieces : -6]
    w_ref, kept_ref, upper_ref, lower_ref, att, pair = refs[-6:]
    me, mp, sub = meta[0], meta[1], meta[2]
    group = pieces // 2
    piece = kvs[0].shape[1]
    tokens = att.shape[0]
    if len(sources) == 1:
        queries = sources[0][low : low + tokens]
    else:
        queries = queries_from(meta, sources[:-1], sources[-1], low, gain)
    local = lax.broadcasted_iota(jnp.int32, (piece, size), 0)
    for c in range(pair.shape[0]):
        masks = []
        for j in range(2):
            q = 2 * (first + c) + j
            owner = table[0, q]
            rank = jnp.int32(0)
            for e in range(q):
                rank = rank + (table[0, e] == owner).astype(jnp.int32)
            away = owner ^ me
            slot = away * cap + rank
            length = live[away, table[0, requests + q]]
            for p in range(pieces):
                at = (j * pieces + p) * piece
                pair[c, at : at + piece, :] = kvs[p][slot]
                place = lax.rem(mp - p // 2 + group, group) * 2 + lax.rem(sub + p % 2, 2)
                masks.append((local + place * piece < length).astype(f32))
        mask = jnp.concatenate(masks, axis=0)
        keys = pair[c, :, :size]
        values = jnp.concatenate(
            [(pair[c, :, size:].astype(f32) * mask).astype(bf16), mask.astype(bf16)], axis=1
        )
        rows = slice(c * span, (c + 1) * span)
        query = jnp.concatenate(
            [queries[rows, h * size : (h + 1) * size] for h in range(heads)], axis=0
        )
        scores = lax.dot_general(query, keys, (((1,), (1,)), ((), ())), preferred_element_type=f32)
        weights = jnp.exp(softcap * jnp.tanh(scores)).astype(bf16)
        summed = jnp.dot(weights, values, preferred_element_type=f32)
        attended = (summed[:, :size] / summed[:, size:]).astype(bf16)
        for h in range(heads):
            att[rows, h * size : (h + 1) * size] = attended[h * span : (h + 1) * span]
    width = kept_ref.shape[2]
    half = tokens // 2
    for ds in (1, 0):
        for dm in range(group):
            block = lax.rem(mp + dm, group) * 2 + lax.rem(sub + ds, 2)
            w = w_ref[:, pl.ds(pl.multiple_of(block * width, width), width)]
            result = jnp.dot(att[...], w, preferred_element_type=f32).astype(bf16)
            if ds:
                upper_ref[dm] = result[:half]
                lower_ref[dm] = result[half:]
            else:
                kept_ref[dm] = result


def run_chunk(meta, table, live, sources, pairs, weight, first, low, spans, span, out_width, cap, gain):
    width = weight.shape[0]
    tokens = spans * span
    pieces = len(pairs)
    piece, pair_width = pairs[0].shape[1:]
    size = pair_width // 2
    group = pieces // 2
    requests = table.shape[1] // 2
    return pl.pallas_call(
        functools.partial(
            chunk_kernel, first=first, low=low, span=span, heads=width // size, size=size,
            pieces=pieces, cap=cap, requests=requests, gain=gain,
        ),
        in_specs=[SMEM] * 3 + [VMEM] * (1 + pieces + len(sources)),
        out_specs=[VMEM] * 3,
        scratch_shapes=[
            pltpu.VMEM((tokens, width), bf16),
            pltpu.VMEM((spans, 2 * pieces * piece, pair_width), bf16),
        ],
        out_shape=[
            jax.ShapeDtypeStruct((group, tokens, out_width), bf16),
            jax.ShapeDtypeStruct((group, tokens // 2, out_width), bf16),
            jax.ShapeDtypeStruct((group, tokens // 2, out_width), bf16),
        ],
        compiler_params=params(),
        cost_estimate=cost(
            4 * tokens * width * out_width * group + 4 * tokens * width * 2 * pieces * piece,
            2 * tokens * width, 2 * tokens * width * 2,
        ),
        name="chunk",
    )(meta, table, live, *sources, *pairs, weight)


def shards(
    hidden,
    neighbour_states,
    query_weight,
    encoder_weight,
    output_weight,
    neighbour_owner,
    neighbour_slot,
    neighbour_length,
):
    row_count = lax.axis_size("rows")
    group = lax.axis_size("mp")
    pieces = group * lax.axis_size("sub")
    me, mp, sub = lax.axis_index("rows"), lax.axis_index("mp"), lax.axis_index("sub")
    spans_here = neighbour_owner.shape[0]
    count, slot_tokens, feature_shard = neighbour_states.shape
    features = feature_shard * pieces
    size = encoder_weight.shape[1] // 2
    token_count = hidden.shape[0]
    span_tokens = token_count // spans_here
    requests = 2 * spans_here
    cap = max(2, (requests + row_count - 1) // row_count)
    last_spans = spans_here // 4
    chunk_spans = [last_spans] * 4
    firsts = [c * last_spans for c in range(4)]
    chunks = len(chunk_spans)
    first_tokens = token_count // 4
    last_low = token_count - last_spans * span_tokens
    gain = 1.0 / (softcap * math.sqrt(size))
    add = lambda *terms: functools.reduce(
        lambda a, b: a + b, [t.astype(f32) for t in terms]
    ).astype(bf16)

    meta = jnp.stack([me, mp, sub]).astype(jnp.int32)

    def cross(mine):
        return [shift(mine, "mp", dm) for dm in range(1, group)]

    def with_near(fars, *earlier):
        out = []
        for far in lax.optimization_barrier((fars, *earlier))[0]:
            out += [far, shift(far, "sub", 1)]
        return out

    fars_first = cross(hidden[:first_tokens])

    table = jnp.concatenate(
        [neighbour_owner.reshape(1, -1), neighbour_slot.reshape(1, -1), neighbour_length.reshape(1, -1)],
        axis=1,
    )

    kept, sent = encode(meta, neighbour_states, encoder_weight, pieces)
    received = shift(after(sent, *fars_first), "sub", 1)
    leaving = [add(kept[dm], received[dm]) for dm in range(1, group)]
    crossed = [shift(leaving[dm - 1], "mp", dm) for dm in range(1, group)]
    near = shift(after(hidden, *leaving), "sub", 1)
    table = after(table, *leaving)
    while table.shape[0] < row_count:
        table = jnp.concatenate([table, swap(table, "rows", table.shape[0])], axis=0)
    table, live = table[:, : 2 * requests], table[:, 2 * requests :]

    fars_second = cross(after(hidden, table, *crossed)[first_tokens:last_low])

    routed = route(meta, table, kept, received, crossed, cap, features, count, requests)
    encoded = jnp.concatenate(
        [routed[0]]
        + list(lax.optimization_barrier([swap(routed[d], "rows", d) for d in range(1, row_count)])),
        axis=0,
    )
    pairs = [encoded, shift(encoded, "sub", 1)]
    fars = [shift(encoded, "mp", dm) for dm in range(1, group)]
    queries = project_queries(
        after(meta, encoded), hidden, near,
        [with_near(fars_first, encoded), with_near(fars_second, encoded)], query_weight, gain,
    )
    fars_last = cross(after(hidden, encoded)[last_low:])
    pairs += with_near(fars, queries)

    def join(c, *earlier):
        got = after(received[c], *earlier)
        step = chunk_spans[c] * span_tokens // 2
        parts = [
            [add(kept[c][dm, i * step : (i + 1) * step], g[dm]) for i, g in enumerate(got)]
            for dm in range(1, group)
        ]
        return [jnp.concatenate(p, axis=0) for p in parts]

    kept, received, leaving, arrived, outs = [], [], [], [], []

    def total(c, *earlier):
        got = jnp.concatenate([g[0] for g in received[c]], axis=0)
        outs.append(add(after(kept[c], *earlier)[0], got, *arrived[c]))

    for c in range(chunks):
        sources, low = [queries], firsts[c] * span_tokens
        if c == chunks - 1:
            sources = [hidden, near, *with_near(fars_last, *leaving[0]), query_weight]
        gate = (leaving[c - 1] if c else []) + ([outs[c - 2]] if c > 1 else [])
        one, *others = run_chunk(
            after(meta, *gate), table, live, sources, pairs, output_weight, firsts[c],
            low, chunk_spans[c], span_tokens, feature_shard, cap, gain,
        )
        kept.append(one)
        received.append([shift(other, "sub", 1) for other in others])
        leaving.append(join(c, *([] if c else fars_last)))
        arrived.append([shift(leaving[c][dm - 1], "mp", dm) for dm in range(1, group)])
        if c:
            total(c - 1, *leaving[c])
    total(chunks - 1)
    mixed = jnp.zeros((token_count, feature_shard), bf16)
    for c, out in enumerate(outs):
        mixed = lax.dynamic_update_slice(after(mixed, meta), out, (firsts[c] * span_tokens, 0))
    return mixed


def solution(mesh):
    placed = (
        P(("groups", "rows"), ("mp", "sub")),
        P(("groups", "rows"), None, ("mp", "sub")),
        P(None, ("mp", "sub")),
        P(("mp", "sub"), None),
        P(("mp", "sub"), None),
        P(("groups", "rows"), None),
        P(("groups", "rows"), None),
        P(("groups", "rows")),
    )
    return jax.shard_map(
        shards,
        mesh=mesh,
        in_specs=placed,
        out_specs=P(("groups", "rows"), ("mp", "sub")),
        check_vma=False,
    )
```

```python
import functools
import math

import jax
import jax.numpy as jnp
from jax import lax
from jax.experimental import pallas as pl
from jax.experimental.pallas import tpu as pltpu
from jax.sharding import PartitionSpec as P

eps = 1e-05
softcap = 10.0
f32 = jnp.float32
bf16 = jnp.bfloat16

VMEM = pl.BlockSpec(memory_space=pltpu.VMEM)
SMEM = pl.BlockSpec(memory_space=pltpu.SMEM)


def shift(value, axis, by):
    size = lax.axis_size(axis)
    return lax.ppermute(value, axis, [(i, (i + by) % size) for i in range(size)])


def swap(value, axis, by):
    size = lax.axis_size(axis)
    return lax.ppermute(value, axis, [(i, i ^ by) for i in range(size)])


def after(value, *earlier):
    return lax.optimization_barrier((value, *earlier))[0]


def cost(flops, nbytes, transcendentals=0):
    return pl.CostEstimate(flops=flops, bytes_accessed=nbytes, transcendentals=transcendentals)


def params():
    return pltpu.CompilerParams(vmem_limit_bytes=16 * 1024 * 1024)


def diagonal_of(piece):
    down = lax.broadcasted_iota(jnp.int32, (piece, 128), 0)
    return down == lax.broadcasted_iota(jnp.int32, (piece, 128), 1)


def encode_kernel(meta, x_ref, w_ref, kept_ref, sent_ref, product, squares, *, pieces, piece, count):
    step = pl.program_id(0)
    mp, sub, size = meta[1], meta[2], pieces // 2
    block, tokens, width = x_ref.shape
    x = x_ref[...].reshape(block * tokens, width)
    product[...] = jnp.dot(x, w_ref[...], preferred_element_type=f32).astype(bf16).reshape(product.shape)
    xf = x.astype(f32)
    square = jnp.sum(xf * xf, axis=1, keepdims=True)
    diagonal = diagonal_of(piece)
    for a in range(pieces):
        for n in range(block):
            low = n * tokens + a * piece
            column = jnp.broadcast_to(square[low : low + piece], (piece, 128))
            squares[a, pl.ds(step * block + n, 1), :] = jnp.sum(
                jnp.where(diagonal, column, 0.0), axis=0, keepdims=True
            )
    rows = pl.ds(pl.multiple_of(step * block * piece, block * piece), block * piece)
    for ds, out_ref in ((0, kept_ref), (1, sent_ref)):
        for dm in range(size):
            a = lax.rem(mp + dm, size) * 2 + lax.rem(sub + ds, 2)
            taken = product[:, pl.ds(pl.multiple_of(a * piece, piece), piece), :]
            out_ref[dm, rows, :] = taken.reshape(block * piece, taken.shape[2])

    @pl.when(step == pl.num_programs(0) - 1)
    def _():
        for ds, out_ref in ((0, kept_ref), (1, sent_ref)):
            for dm in range(size):
                a = lax.rem(mp + dm, size) * 2 + lax.rem(sub + ds, 2)
                tail = jnp.concatenate([squares[a], jnp.zeros_like(squares[a])], axis=1)
                out_ref[dm, pl.ds(count * piece, count), :] = tail.astype(bf16)


def encode(meta, states, weight, pieces):
    count, tokens, width = states.shape
    out_width = weight.shape[1]
    piece = tokens // pieces
    rows = count * piece + count
    block = 4
    return pl.pallas_call(
        functools.partial(encode_kernel, pieces=pieces, piece=piece, count=count),
        grid_spec=pltpu.PrefetchScalarGridSpec(
            num_scalar_prefetch=1,
            grid=(count // block,),
            in_specs=[
                pl.BlockSpec((block, tokens, width), lambda i, m: (i, 0, 0)),
                pl.BlockSpec((width, out_width), lambda i, m: (0, 0)),
            ],
            out_specs=[pl.BlockSpec((pieces // 2, rows, out_width), lambda i, m: (0, 0, 0))] * 2,
            scratch_shapes=[
                pltpu.VMEM((block, tokens, out_width), bf16),
                pltpu.VMEM((pieces, count, 128), f32),
            ],
        ),
        out_shape=[jax.ShapeDtypeStruct((pieces // 2, rows, out_width), bf16)] * 2,
        compiler_params=params(),
        cost_estimate=cost(2 * count * tokens * width * out_width, 2 * count * tokens * width),
        name="encode",
    )(meta, states, weight)


def route_kernel(meta, table, kept, received, *refs, row_count, cap, piece, count, requests, features):
    crossed, outs = refs[: -2 - row_count], refs[-2 - row_count : -2]
    encoded, picks = refs[-2:]
    me = meta[0]
    total = kept[0].astype(f32) + received[0].astype(f32)
    for ref in crossed:
        total = total + ref[...].astype(f32)
    scale = lax.rsqrt(total[count * piece :, :128] * (1.0 / features) + eps)
    diagonal = diagonal_of(piece)
    for n in range(count):
        row = jnp.broadcast_to(scale[n : n + 1], (piece, 128))
        column = jnp.sum(jnp.where(diagonal, row, 0.0), axis=1, keepdims=True)
        encoded[n] = (total[n * piece : (n + 1) * piece] * column).astype(bf16)
    for d in range(row_count):
        for r in range(cap):
            picks[d, r] = 0
        seen = jnp.int32(0)
        for q in range(requests):
            mine = table[d, q % 2, q // 2] == me

            @pl.when(mine)
            def _(seen=seen, q=q, d=d):
                picks[d, jnp.minimum(seen, cap - 1)] = table[d, 2 + q % 2, q // 2]

            seen = seen + mine.astype(jnp.int32)
        for r in range(cap):
            outs[d][r] = encoded[picks[d, r]]


def route(meta, table, kept, received, crossed, cap, features, count, requests):
    row_count = table.shape[0]
    rows, width = kept.shape[-2:]
    piece = rows // count - 1
    return pl.pallas_call(
        functools.partial(
            route_kernel, row_count=row_count, cap=cap, piece=piece, count=count,
            requests=requests, features=features,
        ),
        in_specs=[SMEM] * 2 + [VMEM] * (2 + len(crossed)),
        out_specs=[VMEM] * row_count,
        scratch_shapes=[
            pltpu.VMEM((count, piece, width), bf16),
            pltpu.SMEM((row_count, cap), jnp.int32),
        ],
        out_shape=[jax.ShapeDtypeStruct((cap, piece, width), bf16)] * row_count,
        compiler_params=params(),
        cost_estimate=cost(8 * rows * width, 2 * rows * width * 3),
        name="route",
    )(meta, table, kept, received, *crossed)


def queries_from(meta, hs, w_ref, low, gain):
    mp, sub = meta[1], meta[2]
    tokens, width = hs[-1].shape
    features = w_ref.shape[0]
    group = features // width // 2
    total, squares = None, None
    for k, part in enumerate(hs):
        block = lax.rem(mp - k // 2 + group, group) * 2 + lax.rem(sub + k % 2, 2)
        rows = pl.ds(pl.multiple_of(block * width, width), width)
        h = part[low : low + tokens] if k < 2 else part[...]
        for i in range(0, width, 128):
            square = h[:, i : i + 128].astype(f32)
            square = square * square
            squares = square if squares is None else squares + square
        product = jnp.dot(h, w_ref[rows, :], preferred_element_type=f32)
        total = product if total is None else total + product
    squares = jnp.sum(squares, axis=1, keepdims=True)
    return (total * (lax.rsqrt(squares * (1.0 / features) + eps) * gain)).astype(bf16)


def query_kernel(meta, own_ref, near_ref, *refs, lows, gain):
    fars, w_ref, out_ref = refs[:-2], *refs[-2:]
    each = len(fars) // len(lows)
    for i, low in enumerate(lows):
        far = fars[i * each : (i + 1) * each]
        out_ref[low : low + far[0].shape[0], :] = queries_from(
            meta, (own_ref, near_ref, *far), w_ref, low, gain
        )


def project_queries(meta, own, near, segments, weight, gain):
    lows, tokens = [], 0
    for far in segments:
        lows.append(tokens)
        tokens += far[0].shape[0]
    parts = [own, near] + [part for far in segments for part in far]
    depth, out_width = weight.shape
    return pl.pallas_call(
        functools.partial(query_kernel, lows=tuple(lows), gain=gain),
        in_specs=[SMEM] + [VMEM] * (len(parts) + 1),
        out_specs=VMEM,
        out_shape=jax.ShapeDtypeStruct((tokens, out_width), bf16),
        compiler_params=params(),
        cost_estimate=cost(2 * tokens * depth * out_width, 2 * tokens * depth),
        name="queries",
    )(meta, *parts, weight)


def chunk_kernel(
    meta, table, *refs, first, low, spans, span, heads, size, pieces, cap, gain
):
    own_end = -4 - spans
    sources, kvs = refs[: own_end - pieces], refs[own_end - pieces : own_end]
    w_ref, kept_ref, *sent_refs, att, pair = refs[-4 - spans :]
    me, mp, sub = meta[0], meta[1], meta[2]
    group = pieces // 2
    piece = kvs[0].shape[1]
    tokens = att.shape[0]
    if len(sources) == 1:
        queries = sources[0][low : low + tokens]
    else:
        queries = queries_from(meta, sources[:-1], sources[-1], low, gain)
    local = lax.broadcasted_iota(jnp.int32, (piece, size), 0)
    for c in range(pair.shape[0]):
        masks = []
        for j in range(2):
            q = 2 * (first + c) + j
            owner = table[0, j, first + c]
            rank = jnp.int32(0)
            for e in range(q):
                rank = rank + (table[0, e % 2, e // 2] == owner).astype(jnp.int32)
            away = owner ^ me
            slot = away * cap + rank
            length = table[away, 4, table[0, 2 + j, first + c]]
            for p in range(pieces):
                at = (j * pieces + p) * piece
                pair[c, at : at + piece, :] = kvs[p][slot]
                place = lax.rem(mp - p // 2 + group, group) * 2 + lax.rem(sub + p % 2, 2)
                masks.append((local + place * piece < length).astype(f32))
        mask = jnp.concatenate(masks, axis=0)
        keys = pair[c, :, :size]
        values = jnp.concatenate(
            [(pair[c, :, size:].astype(f32) * mask).astype(bf16), mask.astype(bf16)], axis=1
        )
        rows = slice(c * span, (c + 1) * span)
        query = jnp.concatenate(
            [queries[rows, h * size : (h + 1) * size] for h in range(heads)], axis=0
        )
        scores = lax.dot_general(query, keys, (((1,), (1,)), ((), ())), preferred_element_type=f32)
        weights = jnp.exp(softcap * jnp.tanh(scores)).astype(bf16)
        summed = jnp.dot(weights, values, preferred_element_type=f32)
        attended = (summed[:, :size] / summed[:, size:]).astype(bf16)
        for h in range(heads):
            att[rows, h * size : (h + 1) * size] = attended[h * span : (h + 1) * span]
    width = kept_ref.shape[2]
    for ds in (1, 0):
        for dm in range(group):
            block = lax.rem(mp + dm, group) * 2 + lax.rem(sub + ds, 2)
            w = w_ref[:, pl.ds(pl.multiple_of(block * width, width), width)]
            result = jnp.dot(att[...], w, preferred_element_type=f32).astype(bf16)
            if ds:
                for c, sent_ref in enumerate(sent_refs):
                    sent_ref[dm] = result[c * span : (c + 1) * span]
            else:
                kept_ref[dm] = result


def run_chunk(meta, table, sources, pairs, weight, first, low, spans, span, out_width, cap, gain):
    width = weight.shape[0]
    tokens = spans * span
    pieces = len(pairs)
    piece, pair_width = pairs[0].shape[1:]
    size = pair_width // 2
    group = pieces // 2
    return pl.pallas_call(
        functools.partial(
            chunk_kernel, first=first, low=low, spans=spans, span=span, heads=width // size, size=size,
            pieces=pieces, cap=cap, gain=gain,
        ),
        in_specs=[SMEM] * 2 + [VMEM] * (1 + pieces + len(sources)),
        out_specs=[VMEM] * (1 + spans),
        scratch_shapes=[
            pltpu.VMEM((tokens, width), bf16),
            pltpu.VMEM((spans, 2 * pieces * piece, pair_width), bf16),
        ],
        out_shape=[jax.ShapeDtypeStruct((group, tokens, out_width), bf16)]
        + [jax.ShapeDtypeStruct((group, span, out_width), bf16)] * spans,
        compiler_params=params(),
        cost_estimate=cost(
            4 * tokens * width * out_width * group + 4 * tokens * width * 2 * pieces * piece,
            2 * tokens * width, 2 * tokens * width * 2,
        ),
        name="chunk",
    )(meta, table, *sources, *pairs, weight)


def shards(
    hidden,
    neighbour_states,
    query_weight,
    encoder_weight,
    output_weight,
    neighbour_owner,
    neighbour_slot,
    neighbour_length,
):
    row_count = lax.axis_size("rows")
    group = lax.axis_size("mp")
    pieces = group * lax.axis_size("sub")
    me, mp, sub = lax.axis_index("rows"), lax.axis_index("mp"), lax.axis_index("sub")
    spans_here = neighbour_owner.shape[0]
    count, slot_tokens, feature_shard = neighbour_states.shape
    features = feature_shard * pieces
    size = encoder_weight.shape[1] // 2
    token_count = hidden.shape[0]
    span_tokens = token_count // spans_here
    requests = 2 * spans_here
    cap = max(2, (requests + row_count - 1) // row_count)
    last_spans = spans_here // 4
    middle_spans = (spans_here - last_spans) // 2
    chunk_spans = [spans_here - last_spans - middle_spans, middle_spans, last_spans]
    firsts = [0, chunk_spans[0], spans_here - last_spans]
    chunks = len(chunk_spans)
    first_tokens = token_count // 4
    last_low = token_count - last_spans * span_tokens
    gain = 1.0 / (softcap * math.sqrt(size))
    add = lambda *terms: functools.reduce(
        lambda a, b: a + b, [t.astype(f32) for t in terms]
    ).astype(bf16)

    meta = jnp.stack([me, mp, sub]).astype(jnp.int32)

    def cross(mine):
        return [shift(mine, "mp", dm) for dm in range(1, group)]

    def with_near(fars, *earlier):
        out = []
        for far in lax.optimization_barrier((fars, *earlier))[0]:
            out += [far, shift(far, "sub", 1)]
        return out

    fars_first = cross(hidden[:first_tokens])

    lanes = max(spans_here, count)
    widen = lambda t: jnp.pad(t, ((0, 0), (0, lanes - t.shape[1])))
    table = jnp.concatenate(
        [widen(neighbour_owner.T), widen(neighbour_slot.T), widen(neighbour_length[None])], axis=0
    )[None]

    kept, sent = encode(meta, neighbour_states, encoder_weight, pieces)
    received = shift(after(sent, *fars_first), "sub", 1)
    leaving = [add(kept[dm], received[dm]) for dm in range(1, group)]
    crossed = [shift(leaving[dm - 1], "mp", dm) for dm in range(1, group)]
    near = shift(after(hidden, *leaving), "sub", 1)
    table = after(table, *leaving)
    while table.shape[0] < row_count:
        table = jnp.concatenate([table, swap(table, "rows", table.shape[0])], axis=0)

    fars_second = cross(after(hidden[first_tokens:last_low], table, *crossed))

    routed = route(meta, table, kept, received, crossed, cap, features, count, requests)
    encoded = jnp.concatenate(
        [routed[0]]
        + list(lax.optimization_barrier([swap(routed[d], "rows", d) for d in range(1, row_count)])),
        axis=0,
    )
    pairs = [encoded, shift(encoded, "sub", 1)]
    fars = [shift(encoded, "mp", dm) for dm in range(1, group)]
    queries = project_queries(
        after(meta, encoded), hidden, near,
        [with_near(fars_first, encoded), with_near(fars_second, encoded)], query_weight, gain,
    )
    fars_last = cross(after(hidden[last_low:], encoded))
    pairs += with_near(fars, queries)

    def join(c, *earlier):
        got = after(received[c], *earlier)
        step = span_tokens
        parts = [
            [add(kept[c][dm, i * step : (i + 1) * step], g[dm]) for i, g in enumerate(got)]
            for dm in range(1, group)
        ]
        return [jnp.concatenate(p, axis=0) for p in parts]

    kept, received, leaving, arrived, outs = [], [], [], [], []

    def total(c, *earlier):
        got = jnp.concatenate([g[0] for g in received[c]], axis=0)
        outs.append(add(after(kept[c], *earlier)[0], got, *arrived[c]))

    for c in range(chunks):
        sources, low = [queries], firsts[c] * span_tokens
        if c == chunks - 1:
            sources = [hidden, near, *with_near(fars_last, *leaving[0]), query_weight]
        gate = (leaving[c - 1] if c else []) + ([outs[c - 2]] if c > 1 else [])
        one, *others = run_chunk(
            after(meta, *gate), table, sources, pairs, output_weight, firsts[c],
            low, chunk_spans[c], span_tokens, feature_shard, cap, gain,
        )
        kept.append(one)
        received.append([shift(other, "sub", 1) for other in others])
        leaving.append(join(c, *([] if c else fars_last)))
        arrived.append([shift(leaving[c][dm - 1], "mp", dm) for dm in range(1, group)])
        if c:
            total(c - 1, *leaving[c])
    total(chunks - 1)
    mixed = jnp.zeros((token_count, feature_shard), bf16)
    for c, out in enumerate(outs):
        mixed = lax.dynamic_update_slice(after(mixed, meta), out, (firsts[c] * span_tokens, 0))
    return mixed


def solution(mesh):
    placed = (
        P(("groups", "rows"), ("mp", "sub")),
        P(("groups", "rows"), None, ("mp", "sub")),
        P(None, ("mp", "sub")),
        P(("mp", "sub"), None),
        P(("mp", "sub"), None),
        P(("groups", "rows"), None),
        P(("groups", "rows"), None),
        P(("groups", "rows")),
    )
    return jax.shard_map(
        shards,
        mesh=mesh,
        in_specs=placed,
        out_specs=P(("groups", "rows"), ("mp", "sub")),
        check_vma=False,
    )
```

```python
import functools
import math

import jax
import jax.numpy as jnp
from jax import lax
from jax.experimental import pallas as pl
from jax.experimental.pallas import tpu as pltpu
from jax.sharding import PartitionSpec as P

eps = 1e-05
softcap = 10.0
f32 = jnp.float32
bf16 = jnp.bfloat16

VMEM = pl.BlockSpec(memory_space=pltpu.VMEM)
SMEM = pl.BlockSpec(memory_space=pltpu.SMEM)


def shift(value, axis, by):
    size = lax.axis_size(axis)
    return lax.ppermute(value, axis, [(i, (i + by) % size) for i in range(size)])


def swap(value, axis, by):
    size = lax.axis_size(axis)
    return lax.ppermute(value, axis, [(i, i ^ by) for i in range(size)])


def after(value, *earlier):
    return lax.optimization_barrier((value, *earlier))[0]


def cost(flops, nbytes, transcendentals=0):
    return pl.CostEstimate(flops=flops, bytes_accessed=nbytes, transcendentals=transcendentals)


def params():
    return pltpu.CompilerParams(vmem_limit_bytes=16 * 1024 * 1024)


def diagonal_of(piece):
    down = lax.broadcasted_iota(jnp.int32, (piece, 128), 0)
    return down == lax.broadcasted_iota(jnp.int32, (piece, 128), 1)


def encode_kernel(meta, x_ref, w_ref, kept_ref, sent_ref, product, squares, *, pieces, piece, block):
    mp, sub, size = meta[1], meta[2], pieces // 2
    count, tokens, width = x_ref.shape
    diagonal = diagonal_of(piece)

    @pl.loop(0, count // block)
    def _(step):
        x = x_ref[pl.ds(step * block, block)].reshape(block * tokens, width)
        result = jnp.dot(x, w_ref[...], preferred_element_type=f32).astype(bf16)
        product[...] = result.reshape(product.shape)
        xf = x.astype(f32)
        square = jnp.sum(xf * xf, axis=1, keepdims=True)
        for a in range(pieces):
            for n in range(block):
                low = n * tokens + a * piece
                column = jnp.broadcast_to(square[low : low + piece], (piece, 128))
                squares[a, pl.ds(step * block + n, 1), :] = jnp.sum(
                    jnp.where(diagonal, column, 0.0), axis=0, keepdims=True
                )
        rows = pl.ds(pl.multiple_of(step * block * piece, block * piece), block * piece)
        for ds, out_ref in ((0, kept_ref), (1, sent_ref)):
            for dm in range(size):
                a = lax.rem(mp + dm, size) * 2 + lax.rem(sub + ds, 2)
                taken = product[:, pl.ds(pl.multiple_of(a * piece, piece), piece), :]
                out_ref[dm, rows, :] = taken.reshape(block * piece, taken.shape[2])

    for ds, out_ref in ((0, kept_ref), (1, sent_ref)):
        for dm in range(size):
            a = lax.rem(mp + dm, size) * 2 + lax.rem(sub + ds, 2)
            tail = jnp.concatenate([squares[a], jnp.zeros_like(squares[a])], axis=1)
            out_ref[dm, count * piece : count * piece + count, :] = tail.astype(bf16)


def encode(meta, states, weight, pieces):
    count, tokens, width = states.shape
    out_width = weight.shape[1]
    piece = tokens // pieces
    rows = count * piece + count
    block = 4
    return pl.pallas_call(
        functools.partial(encode_kernel, pieces=pieces, piece=piece, block=block),
        in_specs=[SMEM, VMEM, VMEM],
        out_specs=[VMEM] * 2,
        scratch_shapes=[
            pltpu.VMEM((block, tokens, out_width), bf16),
            pltpu.VMEM((pieces, count, 128), f32),
        ],
        out_shape=[jax.ShapeDtypeStruct((pieces // 2, rows, out_width), bf16)] * 2,
        compiler_params=params(),
        cost_estimate=cost(2 * count * tokens * width * out_width, 2 * count * tokens * width),
        name="encode",
    )(meta, states, weight)


def route_kernel(meta, table, kept, received, *refs, row_count, cap, piece, count, requests, features):
    crossed, outs = refs[: -2 - row_count], refs[-2 - row_count : -2]
    encoded, picks = refs[-2:]
    me = meta[0]
    total = kept[0].astype(f32) + received[0].astype(f32)
    for ref in crossed:
        total = total + ref[...].astype(f32)
    scale = lax.rsqrt(total[count * piece :, :128] * (1.0 / features) + eps)
    diagonal = diagonal_of(piece)
    for n in range(count):
        row = jnp.broadcast_to(scale[n : n + 1], (piece, 128))
        column = jnp.sum(jnp.where(diagonal, row, 0.0), axis=1, keepdims=True)
        encoded[n] = (total[n * piece : (n + 1) * piece] * column).astype(bf16)
    for d in range(row_count):
        for r in range(cap):
            picks[d, r] = 0
        seen = jnp.int32(0)
        for q in range(requests):
            mine = table[d, q % 2, q // 2] == me

            @pl.when(mine)
            def _(seen=seen, q=q, d=d):
                picks[d, jnp.minimum(seen, cap - 1)] = table[d, 2 + q % 2, q // 2]

            seen = seen + mine.astype(jnp.int32)
        for r in range(cap):
            outs[d][r] = encoded[picks[d, r]]


def route(meta, table, kept, received, crossed, cap, features, count, requests):
    row_count = table.shape[0]
    rows, width = kept.shape[-2:]
    piece = rows // count - 1
    return pl.pallas_call(
        functools.partial(
            route_kernel, row_count=row_count, cap=cap, piece=piece, count=count,
            requests=requests, features=features,
        ),
        in_specs=[SMEM] * 2 + [VMEM] * (2 + len(crossed)),
        out_specs=[VMEM] * row_count,
        scratch_shapes=[
            pltpu.VMEM((count, piece, width), bf16),
            pltpu.SMEM((row_count, cap), jnp.int32),
        ],
        out_shape=[jax.ShapeDtypeStruct((cap, piece, width), bf16)] * row_count,
        compiler_params=params(),
        cost_estimate=cost(8 * rows * width, 2 * rows * width * 3),
        name="route",
    )(meta, table, kept, received, *crossed)


def queries_from(meta, hs, w_ref, low, gain):
    mp, sub = meta[1], meta[2]
    tokens, width = hs[-1].shape
    features = w_ref.shape[0]
    group = features // width // 2
    total, squares = None, None
    for k, part in enumerate(hs):
        block = lax.rem(mp - k // 2 + group, group) * 2 + lax.rem(sub + k % 2, 2)
        rows = pl.ds(pl.multiple_of(block * width, width), width)
        h = part[low : low + tokens] if k < 2 else part[...]
        for i in range(0, width, 128):
            square = h[:, i : i + 128].astype(f32)
            square = square * square
            squares = square if squares is None else squares + square
        product = jnp.dot(h, w_ref[rows, :], preferred_element_type=f32)
        total = product if total is None else total + product
    squares = jnp.sum(squares, axis=1, keepdims=True)
    return (total * (lax.rsqrt(squares * (1.0 / features) + eps) * gain)).astype(bf16)


def query_kernel(meta, own_ref, near_ref, *refs, lows, gain):
    fars, w_ref, out_ref = refs[:-2], *refs[-2:]
    each = len(fars) // len(lows)
    for i, low in enumerate(lows):
        far = fars[i * each : (i + 1) * each]
        out_ref[low : low + far[0].shape[0], :] = queries_from(
            meta, (own_ref, near_ref, *far), w_ref, low, gain
        )


def project_queries(meta, own, near, segments, weight, gain):
    lows, tokens = [], 0
    for far in segments:
        lows.append(tokens)
        tokens += far[0].shape[0]
    parts = [own, near] + [part for far in segments for part in far]
    depth, out_width = weight.shape
    return pl.pallas_call(
        functools.partial(query_kernel, lows=tuple(lows), gain=gain),
        in_specs=[SMEM] + [VMEM] * (len(parts) + 1),
        out_specs=VMEM,
        out_shape=jax.ShapeDtypeStruct((tokens, out_width), bf16),
        compiler_params=params(),
        cost_estimate=cost(2 * tokens * depth * out_width, 2 * tokens * depth),
        name="queries",
    )(meta, *parts, weight)


def chunk_kernel(
    meta, table, *refs, first, low, spans, span, heads, size, pieces, cap, gain
):
    own_end = -4 - spans
    sources, kvs = refs[: own_end - pieces], refs[own_end - pieces : own_end]
    w_ref, kept_ref, *sent_refs, att, pair = refs[-4 - spans :]
    me, mp, sub = meta[0], meta[1], meta[2]
    group = pieces // 2
    piece = kvs[0].shape[1]
    tokens = att.shape[0]
    ready = min(tokens, sources[0].shape[0] - low)
    queries = sources[0][low : low + ready]
    if ready < tokens:
        late = queries_from(meta, sources[1:-1], sources[-1], low + ready, gain)
        queries = jnp.concatenate([queries, late], axis=0)
    local = lax.broadcasted_iota(jnp.int32, (piece, size), 0)
    for c in range(pair.shape[0]):
        masks = []
        for j in range(2):
            q = 2 * (first + c) + j
            owner = table[0, j, first + c]
            rank = jnp.int32(0)
            for e in range(q):
                rank = rank + (table[0, e % 2, e // 2] == owner).astype(jnp.int32)
            away = owner ^ me
            slot = away * cap + rank
            length = table[away, 4, table[0, 2 + j, first + c]]
            for p in range(pieces):
                at = (j * pieces + p) * piece
                pair[c, at : at + piece, :] = kvs[p][slot]
                place = lax.rem(mp - p // 2 + group, group) * 2 + lax.rem(sub + p % 2, 2)
                masks.append((local + place * piece < length).astype(f32))
        mask = jnp.concatenate(masks, axis=0)
        keys = pair[c, :, :size]
        values = jnp.concatenate(
            [(pair[c, :, size:].astype(f32) * mask).astype(bf16), mask.astype(bf16)], axis=1
        )
        rows = slice(c * span, (c + 1) * span)
        query = jnp.concatenate(
            [queries[rows, h * size : (h + 1) * size] for h in range(heads)], axis=0
        )
        scores = lax.dot_general(query, keys, (((1,), (1,)), ((), ())), preferred_element_type=f32)
        weights = jnp.exp(softcap * jnp.tanh(scores)).astype(bf16)
        summed = jnp.dot(weights, values, preferred_element_type=f32)
        attended = (summed[:, :size] / summed[:, size:]).astype(bf16)
        for h in range(heads):
            att[rows, h * size : (h + 1) * size] = attended[h * span : (h + 1) * span]
    width = kept_ref.shape[2]
    for ds in (1, 0):
        for dm in range(group):
            block = lax.rem(mp + dm, group) * 2 + lax.rem(sub + ds, 2)
            w = w_ref[:, pl.ds(pl.multiple_of(block * width, width), width)]
            result = jnp.dot(att[...], w, preferred_element_type=f32).astype(bf16)
            if ds:
                for c, sent_ref in enumerate(sent_refs):
                    sent_ref[dm] = result[c * span : (c + 1) * span]
            else:
                kept_ref[dm] = result


def run_chunk(meta, table, sources, pairs, weight, first, low, spans, span, out_width, cap, gain):
    width = weight.shape[0]
    tokens = spans * span
    pieces = len(pairs)
    piece, pair_width = pairs[0].shape[1:]
    size = pair_width // 2
    group = pieces // 2
    return pl.pallas_call(
        functools.partial(
            chunk_kernel, first=first, low=low, spans=spans, span=span, heads=width // size, size=size,
            pieces=pieces, cap=cap, gain=gain,
        ),
        in_specs=[SMEM] * 2 + [VMEM] * (1 + pieces + len(sources)),
        out_specs=[VMEM] * (1 + spans),
        scratch_shapes=[
            pltpu.VMEM((tokens, width), bf16),
            pltpu.VMEM((spans, 2 * pieces * piece, pair_width), bf16),
        ],
        out_shape=[jax.ShapeDtypeStruct((group, tokens, out_width), bf16)]
        + [jax.ShapeDtypeStruct((group, span, out_width), bf16)] * spans,
        compiler_params=params(),
        cost_estimate=cost(
            4 * tokens * width * out_width * group + 4 * tokens * width * 2 * pieces * piece,
            2 * tokens * width, 2 * tokens * width * 2,
        ),
        name="chunk",
    )(meta, table, *sources, *pairs, weight)


def shards(
    hidden,
    neighbour_states,
    query_weight,
    encoder_weight,
    output_weight,
    neighbour_owner,
    neighbour_slot,
    neighbour_length,
):
    row_count = lax.axis_size("rows")
    group = lax.axis_size("mp")
    pieces = group * lax.axis_size("sub")
    me, mp, sub = lax.axis_index("rows"), lax.axis_index("mp"), lax.axis_index("sub")
    spans_here = neighbour_owner.shape[0]
    count, slot_tokens, feature_shard = neighbour_states.shape
    features = feature_shard * pieces
    size = encoder_weight.shape[1] // 2
    token_count = hidden.shape[0]
    span_tokens = token_count // spans_here
    requests = 2 * spans_here
    cap = max(2, (requests + row_count - 1) // row_count)
    chunks = 2
    spans = spans_here // chunks
    first_tokens = token_count // 4
    last_low = token_count - first_tokens
    gain = 1.0 / (softcap * math.sqrt(size))
    add = lambda *terms: functools.reduce(
        lambda a, b: a + b, [t.astype(f32) for t in terms]
    ).astype(bf16)

    meta = jnp.stack([me, mp, sub]).astype(jnp.int32)

    def cross(mine):
        return [shift(mine, "mp", dm) for dm in range(1, group)]

    def with_near(fars, *earlier):
        out = []
        for far in lax.optimization_barrier((fars, *earlier))[0]:
            out += [far, shift(far, "sub", 1)]
        return out

    fars_first = cross(hidden[:first_tokens])

    lanes = max(spans_here, count)
    widen = lambda t: jnp.pad(t, ((0, 0), (0, lanes - t.shape[1])))
    table = jnp.concatenate(
        [widen(neighbour_owner.T), widen(neighbour_slot.T), widen(neighbour_length[None])], axis=0
    )[None]

    kept, sent = encode(meta, neighbour_states, encoder_weight, pieces)
    received = shift(after(sent, *fars_first), "sub", 1)
    leaving = [add(kept[dm], received[dm]) for dm in range(1, group)]
    crossed = [shift(leaving[dm - 1], "mp", dm) for dm in range(1, group)]
    near = shift(after(hidden, *leaving), "sub", 1)
    table = after(table, *leaving)
    while table.shape[0] < row_count:
        table = jnp.concatenate([table, swap(table, "rows", table.shape[0])], axis=0)

    fars_second = cross(after(hidden[first_tokens:last_low], table, *crossed))

    routed = route(meta, table, kept, received, crossed, cap, features, count, requests)
    encoded = jnp.concatenate(
        [routed[0]]
        + list(lax.optimization_barrier([swap(routed[d], "rows", d) for d in range(1, row_count)])),
        axis=0,
    )
    pairs = [encoded, shift(encoded, "sub", 1)]
    fars = [shift(encoded, "mp", dm) for dm in range(1, group)]
    queries = project_queries(
        after(meta, encoded), hidden, near,
        [with_near(fars_first, encoded), with_near(fars_second, encoded)], query_weight, gain,
    )
    fars_last = cross(after(hidden[last_low:], encoded))
    pairs += with_near(fars, queries)

    def join(c, *earlier):
        got = after(received[c], *earlier)
        step = span_tokens
        parts = [
            [add(kept[c][dm, i * step : (i + 1) * step], g[dm]) for i, g in enumerate(got)]
            for dm in range(1, group)
        ]
        return [jnp.concatenate(p, axis=0) for p in parts]

    kept, received, leaving, arrived, outs = [], [], [], [], []

    def total(c, *earlier):
        got = jnp.concatenate([g[0] for g in received[c]], axis=0)
        outs.append(add(after(kept[c], *earlier)[0], got, *arrived[c]))

    for c in range(chunks):
        sources = [queries]
        if c == chunks - 1:
            sources += [hidden, near, *with_near(fars_last, *leaving[0]), query_weight]
        gate = leaving[c - 1] if c else []
        one, *others = run_chunk(
            after(meta, *gate), table, sources, pairs, output_weight, c * spans,
            c * spans * span_tokens, spans, span_tokens, feature_shard, cap, gain,
        )
        kept.append(one)
        received.append([shift(other, "sub", 1) for other in others])
        leaving.append(join(c, *([] if c else fars_last)))
        arrived.append([shift(leaving[c][dm - 1], "mp", dm) for dm in range(1, group)])
        if c:
            total(c - 1, *leaving[c])
    total(chunks - 1)
    mixed = jnp.zeros((token_count, feature_shard), bf16)
    for c, out in enumerate(outs):
        mixed = lax.dynamic_update_slice(after(mixed, meta), out, (c * spans * span_tokens, 0))
    return mixed


def solution(mesh):
    placed = (
        P(("groups", "rows"), ("mp", "sub")),
        P(("groups", "rows"), None, ("mp", "sub")),
        P(None, ("mp", "sub")),
        P(("mp", "sub"), None),
        P(("mp", "sub"), None),
        P(("groups", "rows"), None),
        P(("groups", "rows"), None),
        P(("groups", "rows")),
    )
    return jax.shard_map(
        shards,
        mesh=mesh,
        in_specs=placed,
        out_specs=P(("groups", "rows"), ("mp", "sub")),
        check_vma=False,
    )
```

```python
import functools
import math

import jax
import jax.numpy as jnp
from jax import lax
from jax.experimental import pallas as pl
from jax.experimental.pallas import tpu as pltpu
from jax.sharding import PartitionSpec as P

eps = 1e-05
softcap = 10.0
f32 = jnp.float32
bf16 = jnp.bfloat16

VMEM = pl.BlockSpec(memory_space=pltpu.VMEM)
SMEM = pl.BlockSpec(memory_space=pltpu.SMEM)


def shift(value, axis, by):
    size = lax.axis_size(axis)
    return lax.ppermute(value, axis, [(i, (i + by) % size) for i in range(size)])


def swap(value, axis, by):
    size = lax.axis_size(axis)
    return lax.ppermute(value, axis, [(i, i ^ by) for i in range(size)])


def after(value, *earlier):
    return lax.optimization_barrier((value, *earlier))[0]


def cost(flops, nbytes, transcendentals=0):
    return pl.CostEstimate(flops=flops, bytes_accessed=nbytes, transcendentals=transcendentals)


def params():
    return pltpu.CompilerParams(vmem_limit_bytes=16 * 1024 * 1024)


def diagonal_of(piece):
    down = lax.broadcasted_iota(jnp.int32, (piece, 128), 0)
    return down == lax.broadcasted_iota(jnp.int32, (piece, 128), 1)


def encode_kernel(meta, x_ref, w_ref, kept_ref, sent_ref, product, squares, *, pieces, piece, block):
    mp, sub, size = meta[1], meta[2], pieces // 2
    count, tokens, width = x_ref.shape
    diagonal = diagonal_of(piece)

    @pl.loop(0, count // block)
    def _(step):
        x = x_ref[pl.ds(step * block, block)].reshape(block * tokens, width)
        result = jnp.dot(x, w_ref[...], preferred_element_type=f32).astype(bf16)
        product[...] = result.reshape(product.shape)
        xf = x.astype(f32)
        square = jnp.sum(xf * xf, axis=1, keepdims=True)
        for a in range(pieces):
            for n in range(block):
                low = n * tokens + a * piece
                column = jnp.broadcast_to(square[low : low + piece], (piece, 128))
                squares[a, pl.ds(step * block + n, 1), :] = jnp.sum(
                    jnp.where(diagonal, column, 0.0), axis=0, keepdims=True
                )
        rows = pl.ds(pl.multiple_of(step * block * piece, block * piece), block * piece)
        for ds, out_ref in ((0, kept_ref), (1, sent_ref)):
            for dm in range(size):
                a = lax.rem(mp + dm, size) * 2 + lax.rem(sub + ds, 2)
                taken = product[:, pl.ds(pl.multiple_of(a * piece, piece), piece), :]
                out_ref[dm, rows, :] = taken.reshape(block * piece, taken.shape[2])

    for ds, out_ref in ((0, kept_ref), (1, sent_ref)):
        for dm in range(size):
            a = lax.rem(mp + dm, size) * 2 + lax.rem(sub + ds, 2)
            tail = jnp.concatenate([squares[a], jnp.zeros_like(squares[a])], axis=1)
            out_ref[dm, count * piece : count * piece + count, :] = tail.astype(bf16)


def encode(meta, states, weight, pieces):
    count, tokens, width = states.shape
    out_width = weight.shape[1]
    piece = tokens // pieces
    rows = count * piece + count
    block = 4
    return pl.pallas_call(
        functools.partial(encode_kernel, pieces=pieces, piece=piece, block=block),
        in_specs=[SMEM, VMEM, VMEM],
        out_specs=[VMEM] * 2,
        scratch_shapes=[
            pltpu.VMEM((block, tokens, out_width), bf16),
            pltpu.VMEM((pieces, count, 128), f32),
        ],
        out_shape=[jax.ShapeDtypeStruct((pieces // 2, rows, out_width), bf16)] * 2,
        compiler_params=params(),
        cost_estimate=cost(2 * count * tokens * width * out_width, 2 * count * tokens * width),
        name="encode",
    )(meta, states, weight)


def route_kernel(meta, table, kept, received, *refs, row_count, cap, piece, count, requests, features):
    crossed, outs = refs[: -2 - row_count], refs[-2 - row_count : -2]
    encoded, picks = refs[-2:]
    me = meta[0]
    total = kept[0].astype(f32) + received[0].astype(f32)
    for ref in crossed:
        total = total + ref[...].astype(f32)
    scale = lax.rsqrt(total[count * piece :, :128] * (1.0 / features) + eps)
    diagonal = diagonal_of(piece)
    for n in range(count):
        row = jnp.broadcast_to(scale[n : n + 1], (piece, 128))
        column = jnp.sum(jnp.where(diagonal, row, 0.0), axis=1, keepdims=True)
        encoded[n] = (total[n * piece : (n + 1) * piece] * column).astype(bf16)
    for d in range(row_count):
        for r in range(cap):
            picks[d, r] = 0
        seen = jnp.int32(0)
        for q in range(requests):
            mine = table[d, q % 2, q // 2] == me

            @pl.when(mine)
            def _(seen=seen, q=q, d=d):
                picks[d, jnp.minimum(seen, cap - 1)] = table[d, 2 + q % 2, q // 2]

            seen = seen + mine.astype(jnp.int32)
        for r in range(cap):
            outs[d][r] = encoded[picks[d, r]]


def route(meta, table, kept, received, crossed, cap, features, count, requests):
    row_count = table.shape[0]
    rows, width = kept.shape[-2:]
    piece = rows // count - 1
    return pl.pallas_call(
        functools.partial(
            route_kernel, row_count=row_count, cap=cap, piece=piece, count=count,
            requests=requests, features=features,
        ),
        in_specs=[SMEM] * 2 + [VMEM] * (2 + len(crossed)),
        out_specs=[VMEM] * row_count,
        scratch_shapes=[
            pltpu.VMEM((count, piece, width), bf16),
            pltpu.SMEM((row_count, cap), jnp.int32),
        ],
        out_shape=[jax.ShapeDtypeStruct((cap, piece, width), bf16)] * row_count,
        compiler_params=params(),
        cost_estimate=cost(8 * rows * width, 2 * rows * width * 3),
        name="route",
    )(meta, table, kept, received, *crossed)


def queries_from(meta, hs, w_ref, low, gain):
    mp, sub = meta[1], meta[2]
    tokens, width = hs[-1].shape
    features = w_ref.shape[0]
    group = features // width // 2
    total, squares = None, None
    for k, part in enumerate(hs):
        block = lax.rem(mp - k // 2 + group, group) * 2 + lax.rem(sub + k % 2, 2)
        rows = pl.ds(pl.multiple_of(block * width, width), width)
        h = part[low : low + tokens] if k < 2 else part[...]
        for i in range(0, width, 128):
            square = h[:, i : i + 128].astype(f32)
            square = square * square
            squares = square if squares is None else squares + square
        product = jnp.dot(h, w_ref[rows, :], preferred_element_type=f32)
        total = product if total is None else total + product
    squares = jnp.sum(squares, axis=1, keepdims=True)
    return (total * (lax.rsqrt(squares * (1.0 / features) + eps) * gain)).astype(bf16)


def query_kernel(meta, own_ref, near_ref, *refs, lows, gain):
    fars, w_ref, out_ref = refs[:-2], *refs[-2:]
    each = len(fars) // len(lows)
    for i, low in enumerate(lows):
        far = fars[i * each : (i + 1) * each]
        out_ref[low : low + far[0].shape[0], :] = queries_from(
            meta, (own_ref, near_ref, *far), w_ref, low, gain
        )


def project_queries(meta, own, near, segments, weight, gain):
    lows, tokens = [], 0
    for far in segments:
        lows.append(tokens)
        tokens += far[0].shape[0]
    parts = [own, near] + [part for far in segments for part in far]
    depth, out_width = weight.shape
    return pl.pallas_call(
        functools.partial(query_kernel, lows=tuple(lows), gain=gain),
        in_specs=[SMEM] + [VMEM] * (len(parts) + 1),
        out_specs=VMEM,
        out_shape=jax.ShapeDtypeStruct((tokens, out_width), bf16),
        compiler_params=params(),
        cost_estimate=cost(2 * tokens * depth * out_width, 2 * tokens * depth),
        name="queries",
    )(meta, *parts, weight)


def chunk_kernel(
    meta, table, *refs, first, low, spans, span, heads, size, pieces, cap, gain
):
    own_end = -4 - spans
    sources, kvs = refs[: own_end - pieces], refs[own_end - pieces : own_end]
    w_ref, kept_ref, *sent_refs, att, pair = refs[-4 - spans :]
    me, mp, sub = meta[0], meta[1], meta[2]
    group = pieces // 2
    piece = kvs[0].shape[1]
    tokens = att.shape[0]
    ready = min(tokens, sources[0].shape[0] - low)
    queries = sources[0][low : low + ready]
    if ready < tokens:
        late = queries_from(meta, sources[1:-1], sources[-1], low + ready, gain)
        queries = jnp.concatenate([queries, late], axis=0)
    local = lax.broadcasted_iota(jnp.int32, (piece, size), 0)
    for c in range(pair.shape[0]):
        masks = []
        for j in range(2):
            q = 2 * (first + c) + j
            owner = table[0, j, first + c]
            rank = jnp.int32(0)
            for e in range(q):
                rank = rank + (table[0, e % 2, e // 2] == owner).astype(jnp.int32)
            away = owner ^ me
            slot = away * cap + rank
            length = table[away, 4, table[0, 2 + j, first + c]]
            for p in range(pieces):
                at = (j * pieces + p) * piece
                pair[c, at : at + piece, :] = kvs[p][slot]
                place = lax.rem(mp - p // 2 + group, group) * 2 + lax.rem(sub + p % 2, 2)
                masks.append((local + place * piece < length).astype(f32))
        mask = jnp.concatenate(masks, axis=0)
        keys = pair[c, :, :size]
        values = jnp.concatenate(
            [(pair[c, :, size:].astype(f32) * mask).astype(bf16), mask.astype(bf16)], axis=1
        )
        rows = slice(c * span, (c + 1) * span)
        query = jnp.concatenate(
            [queries[rows, h * size : (h + 1) * size] for h in range(heads)], axis=0
        )
        scores = lax.dot_general(query, keys, (((1,), (1,)), ((), ())), preferred_element_type=f32)
        weights = jnp.exp(softcap * jnp.tanh(scores)).astype(bf16)
        summed = jnp.dot(weights, values, preferred_element_type=f32)
        attended = (summed[:, :size] / summed[:, size:]).astype(bf16)
        for h in range(heads):
            att[rows, h * size : (h + 1) * size] = attended[h * span : (h + 1) * span]
    width = kept_ref.shape[2]
    for ds in (1, 0):
        for dm in range(group):
            block = lax.rem(mp + dm, group) * 2 + lax.rem(sub + ds, 2)
            w = w_ref[:, pl.ds(pl.multiple_of(block * width, width), width)]
            result = jnp.dot(att[...], w, preferred_element_type=f32).astype(bf16)
            if ds:
                for c, sent_ref in enumerate(sent_refs):
                    sent_ref[dm] = result[c * span : (c + 1) * span]
            else:
                kept_ref[dm] = result


def run_chunk(meta, table, sources, pairs, weight, first, low, spans, span, out_width, cap, gain):
    width = weight.shape[0]
    tokens = spans * span
    pieces = len(pairs)
    piece, pair_width = pairs[0].shape[1:]
    size = pair_width // 2
    group = pieces // 2
    return pl.pallas_call(
        functools.partial(
            chunk_kernel, first=first, low=low, spans=spans, span=span, heads=width // size, size=size,
            pieces=pieces, cap=cap, gain=gain,
        ),
        in_specs=[SMEM] * 2 + [VMEM] * (1 + pieces + len(sources)),
        out_specs=[VMEM] * (1 + spans),
        scratch_shapes=[
            pltpu.VMEM((tokens, width), bf16),
            pltpu.VMEM((spans, 2 * pieces * piece, pair_width), bf16),
        ],
        out_shape=[jax.ShapeDtypeStruct((group, tokens, out_width), bf16)]
        + [jax.ShapeDtypeStruct((group, span, out_width), bf16)] * spans,
        compiler_params=params(),
        cost_estimate=cost(
            4 * tokens * width * out_width * group + 4 * tokens * width * 2 * pieces * piece,
            2 * tokens * width, 2 * tokens * width * 2,
        ),
        name="chunk",
    )(meta, table, *sources, *pairs, weight)


def shards(
    hidden,
    neighbour_states,
    query_weight,
    encoder_weight,
    output_weight,
    neighbour_owner,
    neighbour_slot,
    neighbour_length,
):
    row_count = lax.axis_size("rows")
    group = lax.axis_size("mp")
    pieces = group * lax.axis_size("sub")
    me, mp, sub = lax.axis_index("rows"), lax.axis_index("mp"), lax.axis_index("sub")
    spans_here = neighbour_owner.shape[0]
    count, slot_tokens, feature_shard = neighbour_states.shape
    features = feature_shard * pieces
    size = encoder_weight.shape[1] // 2
    token_count = hidden.shape[0]
    span_tokens = token_count // spans_here
    requests = 2 * spans_here
    cap = max(2, (requests + row_count - 1) // row_count)
    chunks = 2
    spans = spans_here // chunks
    first_tokens = token_count // 4
    last_low = token_count - token_count * 10 // 32
    gain = 1.0 / (softcap * math.sqrt(size))
    add = lambda *terms: functools.reduce(
        lambda a, b: a + b, [t.astype(f32) for t in terms]
    ).astype(bf16)

    meta = jnp.stack([me, mp, sub]).astype(jnp.int32)

    def cross(mine):
        return [shift(mine, "mp", dm) for dm in range(1, group)]

    def with_near(fars, *earlier):
        out = []
        for far in lax.optimization_barrier((fars, *earlier))[0]:
            out += [far, shift(far, "sub", 1)]
        return out

    fars_first = cross(hidden[:first_tokens])

    lanes = max(spans_here, count)
    widen = lambda t: jnp.pad(t, ((0, 0), (0, lanes - t.shape[1])))
    table = jnp.concatenate(
        [widen(neighbour_owner.T), widen(neighbour_slot.T), widen(neighbour_length[None])], axis=0
    )[None]

    kept, sent = encode(meta, neighbour_states, encoder_weight, pieces)
    received = shift(after(sent, *fars_first), "sub", 1)
    leaving = [add(kept[dm], received[dm]) for dm in range(1, group)]
    crossed = [shift(leaving[dm - 1], "mp", dm) for dm in range(1, group)]
    near = shift(after(hidden, *leaving), "sub", 1)
    table = after(table, *leaving)
    while table.shape[0] < row_count:
        table = jnp.concatenate([table, swap(table, "rows", table.shape[0])], axis=0)

    fars_second = cross(after(hidden[first_tokens:last_low], table, *crossed))

    routed = route(meta, table, kept, received, crossed, cap, features, count, requests)
    encoded = jnp.concatenate(
        [routed[0]]
        + list(lax.optimization_barrier([swap(routed[d], "rows", d) for d in range(1, row_count)])),
        axis=0,
    )
    pairs = [encoded, shift(encoded, "sub", 1)]
    fars = [shift(encoded, "mp", dm) for dm in range(1, group)]
    queries = project_queries(
        after(meta, encoded), hidden, near,
        [with_near(fars_first, encoded), with_near(fars_second, encoded)], query_weight, gain,
    )
    fars_last = cross(after(hidden[last_low:], encoded))
    pairs += with_near(fars, queries)

    def join(c, *earlier):
        got = after(received[c], *earlier)
        step = span_tokens
        parts = [
            [add(kept[c][dm, i * step : (i + 1) * step], g[dm]) for i, g in enumerate(got)]
            for dm in range(1, group)
        ]
        return [jnp.concatenate(p, axis=0) for p in parts]

    kept, received, leaving, arrived, outs = [], [], [], [], []

    def total(c, *earlier):
        got = jnp.concatenate([g[0] for g in received[c]], axis=0)
        outs.append(add(after(kept[c], *earlier)[0], got, *arrived[c]))

    for c in range(chunks):
        sources = [queries]
        if c == chunks - 1:
            sources += [hidden, near, *with_near(fars_last, *leaving[0]), query_weight]
        gate = leaving[c - 1] if c else []
        one, *others = run_chunk(
            after(meta, *gate), table, sources, pairs, output_weight, c * spans,
            c * spans * span_tokens, spans, span_tokens, feature_shard, cap, gain,
        )
        kept.append(one)
        received.append([shift(other, "sub", 1) for other in others])
        leaving.append(join(c, *([] if c else fars_last)))
        arrived.append([shift(leaving[c][dm - 1], "mp", dm) for dm in range(1, group)])
        if c:
            total(c - 1, *leaving[c])
    total(chunks - 1)
    mixed = jnp.zeros((token_count, feature_shard), bf16)
    for c, out in enumerate(outs):
        mixed = lax.dynamic_update_slice(after(mixed, meta), out, (c * spans * span_tokens, 0))
    return mixed


def solution(mesh):
    placed = (
        P(("groups", "rows"), ("mp", "sub")),
        P(("groups", "rows"), None, ("mp", "sub")),
        P(None, ("mp", "sub")),
        P(("mp", "sub"), None),
        P(("mp", "sub"), None),
        P(("groups", "rows"), None),
        P(("groups", "rows"), None),
        P(("groups", "rows")),
    )
    return jax.shard_map(
        shards,
        mesh=mesh,
        in_specs=placed,
        out_specs=P(("groups", "rows"), ("mp", "sub")),
        check_vma=False,
    )
```

```python
import functools
import math

import jax
import jax.numpy as jnp
from jax import lax
from jax.experimental import pallas as pl
from jax.experimental.pallas import tpu as pltpu
from jax.sharding import PartitionSpec as P

eps = 1e-05
softcap = 10.0
f32 = jnp.float32
bf16 = jnp.bfloat16

VMEM = pl.BlockSpec(memory_space=pltpu.VMEM)
SMEM = pl.BlockSpec(memory_space=pltpu.SMEM)


def shift(value, axis, by):
    size = lax.axis_size(axis)
    return lax.ppermute(value, axis, [(i, (i + by) % size) for i in range(size)])


def swap(value, axis, by):
    size = lax.axis_size(axis)
    return lax.ppermute(value, axis, [(i, i ^ by) for i in range(size)])


def after(value, *earlier):
    return lax.optimization_barrier((value, *earlier))[0]


def cost(flops, nbytes, transcendentals=0):
    return pl.CostEstimate(flops=flops, bytes_accessed=nbytes, transcendentals=transcendentals)


def params():
    return pltpu.CompilerParams(vmem_limit_bytes=16 * 1024 * 1024)


def diagonal_of(piece):
    down = lax.broadcasted_iota(jnp.int32, (piece, 128), 0)
    return down == lax.broadcasted_iota(jnp.int32, (piece, 128), 1)


def encode_kernel(meta, x_ref, w_ref, kept_ref, sent_ref, product, squares, *, pieces, piece, block):
    mp, sub, size = meta[1], meta[2], pieces // 2
    count, tokens, width = x_ref.shape
    diagonal = diagonal_of(piece)

    @pl.loop(0, count // block)
    def _(step):
        x = x_ref[pl.ds(step * block, block)].reshape(block * tokens, width)
        result = jnp.dot(x, w_ref[...], preferred_element_type=f32).astype(bf16)
        product[...] = result.reshape(product.shape)
        xf = x.astype(f32)
        square = jnp.sum(xf * xf, axis=1, keepdims=True)
        for a in range(pieces):
            for n in range(block):
                low = n * tokens + a * piece
                column = jnp.broadcast_to(square[low : low + piece], (piece, 128))
                squares[a, pl.ds(step * block + n, 1), :] = jnp.sum(
                    jnp.where(diagonal, column, 0.0), axis=0, keepdims=True
                )
        rows = pl.ds(pl.multiple_of(step * block * piece, block * piece), block * piece)
        for ds, out_ref in ((0, kept_ref), (1, sent_ref)):
            for dm in range(size):
                a = lax.rem(mp + dm, size) * 2 + lax.rem(sub + ds, 2)
                taken = product[:, pl.ds(pl.multiple_of(a * piece, piece), piece), :]
                out_ref[dm, rows, :] = taken.reshape(block * piece, taken.shape[2])

    for ds, out_ref in ((0, kept_ref), (1, sent_ref)):
        for dm in range(size):
            a = lax.rem(mp + dm, size) * 2 + lax.rem(sub + ds, 2)
            tail = jnp.concatenate([squares[a], jnp.zeros_like(squares[a])], axis=1)
            out_ref[dm, count * piece : count * piece + count, :] = tail.astype(bf16)


def encode(meta, states, weight, pieces):
    count, tokens, width = states.shape
    out_width = weight.shape[1]
    piece = tokens // pieces
    rows = count * piece + count
    block = 4
    return pl.pallas_call(
        functools.partial(encode_kernel, pieces=pieces, piece=piece, block=block),
        in_specs=[SMEM, VMEM, VMEM],
        out_specs=[VMEM] * 2,
        scratch_shapes=[
            pltpu.VMEM((block, tokens, out_width), bf16),
            pltpu.VMEM((pieces, count, 128), f32),
        ],
        out_shape=[jax.ShapeDtypeStruct((pieces // 2, rows, out_width), bf16)] * 2,
        compiler_params=params(),
        cost_estimate=cost(2 * count * tokens * width * out_width, 2 * count * tokens * width),
        name="encode",
    )(meta, states, weight)


def route_kernel(meta, table, kept, received, *refs, row_count, cap, piece, count, requests, features):
    crossed, outs = refs[: -2 - row_count], refs[-2 - row_count : -2]
    encoded, picks = refs[-2:]
    me = meta[0]
    total = kept[0].astype(f32) + received[0].astype(f32)
    for ref in crossed:
        total = total + ref[...].astype(f32)
    scale = lax.rsqrt(total[count * piece :, :128] * (1.0 / features) + eps)
    diagonal = diagonal_of(piece)
    for n in range(count):
        row = jnp.broadcast_to(scale[n : n + 1], (piece, 128))
        column = jnp.sum(jnp.where(diagonal, row, 0.0), axis=1, keepdims=True)
        encoded[n] = (total[n * piece : (n + 1) * piece] * column).astype(bf16)
    for d in range(row_count):
        for r in range(cap):
            picks[d, r] = 0
        seen = jnp.int32(0)
        for q in range(requests):
            mine = table[d, q % 2, q // 2] == me

            @pl.when(mine)
            def _(seen=seen, q=q, d=d):
                picks[d, jnp.minimum(seen, cap - 1)] = table[d, 2 + q % 2, q // 2]

            seen = seen + mine.astype(jnp.int32)
        for r in range(cap):
            outs[d][r] = encoded[picks[d, r]]


def route(meta, table, kept, received, crossed, cap, features, count, requests):
    row_count = table.shape[0]
    rows, width = kept.shape[-2:]
    piece = rows // count - 1
    return pl.pallas_call(
        functools.partial(
            route_kernel, row_count=row_count, cap=cap, piece=piece, count=count,
            requests=requests, features=features,
        ),
        in_specs=[SMEM] * 2 + [VMEM] * (2 + len(crossed)),
        out_specs=[VMEM] * row_count,
        scratch_shapes=[
            pltpu.VMEM((count, piece, width), bf16),
            pltpu.SMEM((row_count, cap), jnp.int32),
        ],
        out_shape=[jax.ShapeDtypeStruct((cap, piece, width), bf16)] * row_count,
        compiler_params=params(),
        cost_estimate=cost(8 * rows * width, 2 * rows * width * 3),
        name="route",
    )(meta, table, kept, received, *crossed)


def queries_from(meta, hs, w_ref, low, gain):
    mp, sub = meta[1], meta[2]
    tokens, width = hs[-1].shape
    features = w_ref.shape[0]
    group = features // width // 2
    total, squares = None, None
    for k, part in enumerate(hs):
        block = lax.rem(mp - k // 2 + group, group) * 2 + lax.rem(sub + k % 2, 2)
        rows = pl.ds(pl.multiple_of(block * width, width), width)
        h = part[low : low + tokens] if k < 2 else part[...]
        for i in range(0, width, 128):
            square = h[:, i : i + 128].astype(f32)
            square = square * square
            squares = square if squares is None else squares + square
        product = jnp.dot(h, w_ref[rows, :], preferred_element_type=f32)
        total = product if total is None else total + product
    squares = jnp.sum(squares, axis=1, keepdims=True)
    return (total * (lax.rsqrt(squares * (1.0 / features) + eps) * gain)).astype(bf16)


def query_kernel(meta, own_ref, near_ref, *refs, lows, gain):
    fars, w_ref, out_ref = refs[:-2], *refs[-2:]
    each = len(fars) // len(lows)
    for i, low in enumerate(lows):
        far = fars[i * each : (i + 1) * each]
        out_ref[low : low + far[0].shape[0], :] = queries_from(
            meta, (own_ref, near_ref, *far), w_ref, low, gain
        )


def project_queries(meta, own, near, segments, weight, gain):
    lows, tokens = [], 0
    for far in segments:
        lows.append(tokens)
        tokens += far[0].shape[0]
    parts = [own, near] + [part for far in segments for part in far]
    depth, out_width = weight.shape
    return pl.pallas_call(
        functools.partial(query_kernel, lows=tuple(lows), gain=gain),
        in_specs=[SMEM] + [VMEM] * (len(parts) + 1),
        out_specs=VMEM,
        out_shape=jax.ShapeDtypeStruct((tokens, out_width), bf16),
        compiler_params=params(),
        cost_estimate=cost(2 * tokens * depth * out_width, 2 * tokens * depth),
        name="queries",
    )(meta, *parts, weight)


def chunk_kernel(
    meta, table, *refs, first, low, spans, span, heads, size, pieces, cap, gain
):
    own_end = -4 - spans
    sources, kvs = refs[: own_end - pieces], refs[own_end - pieces : own_end]
    w_ref, kept_ref, *sent_refs, att, pair = refs[-4 - spans :]
    me, mp, sub = meta[0], meta[1], meta[2]
    group = pieces // 2
    piece = kvs[0].shape[1]
    tokens = att.shape[0]
    ready = min(tokens, sources[0].shape[0] - low)
    queries = sources[0][low : low + ready]
    if ready < tokens:
        late = queries_from(meta, sources[1:-1], sources[-1], low + ready, gain)
        queries = jnp.concatenate([queries, late], axis=0)
    local = lax.broadcasted_iota(jnp.int32, (piece, size), 0)
    for c in range(pair.shape[0]):
        masks = []
        for j in range(2):
            q = 2 * (first + c) + j
            owner = table[0, j, first + c]
            rank = jnp.int32(0)
            for e in range(q):
                rank = rank + (table[0, e % 2, e // 2] == owner).astype(jnp.int32)
            away = owner ^ me
            slot = away * cap + rank
            length = table[away, 4, table[0, 2 + j, first + c]]
            for p in range(pieces):
                at = (j * pieces + p) * piece
                pair[c, at : at + piece, :] = kvs[p][slot]
                place = lax.rem(mp - p // 2 + group, group) * 2 + lax.rem(sub + p % 2, 2)
                masks.append((local + place * piece < length).astype(f32))
        mask = jnp.concatenate(masks, axis=0)
        keys = pair[c, :, :size]
        values = jnp.concatenate(
            [(pair[c, :, size:].astype(f32) * mask).astype(bf16), mask.astype(bf16)], axis=1
        )
        rows = slice(c * span, (c + 1) * span)
        query = jnp.concatenate(
            [queries[rows, h * size : (h + 1) * size] for h in range(heads)], axis=0
        )
        scores = lax.dot_general(query, keys, (((1,), (1,)), ((), ())), preferred_element_type=f32)
        weights = jnp.exp(softcap * jnp.tanh(scores)).astype(bf16)
        summed = jnp.dot(weights, values, preferred_element_type=f32)
        attended = (summed[:, :size] / summed[:, size:]).astype(bf16)
        for h in range(heads):
            att[rows, h * size : (h + 1) * size] = attended[h * span : (h + 1) * span]
    width = kept_ref.shape[2]
    for ds in (1, 0):
        for dm in range(group):
            block = lax.rem(mp + dm, group) * 2 + lax.rem(sub + ds, 2)
            w = w_ref[:, pl.ds(pl.multiple_of(block * width, width), width)]
            result = jnp.dot(att[...], w, preferred_element_type=f32).astype(bf16)
            if ds:
                for c, sent_ref in enumerate(sent_refs):
                    sent_ref[dm] = result[c * span : (c + 1) * span]
            else:
                kept_ref[dm] = result


def run_chunk(meta, table, sources, pairs, weight, first, low, spans, span, out_width, cap, gain):
    width = weight.shape[0]
    tokens = spans * span
    pieces = len(pairs)
    piece, pair_width = pairs[0].shape[1:]
    size = pair_width // 2
    group = pieces // 2
    return pl.pallas_call(
        functools.partial(
            chunk_kernel, first=first, low=low, spans=spans, span=span, heads=width // size, size=size,
            pieces=pieces, cap=cap, gain=gain,
        ),
        in_specs=[SMEM] * 2 + [VMEM] * (1 + pieces + len(sources)),
        out_specs=[VMEM] * (1 + spans),
        scratch_shapes=[
            pltpu.VMEM((tokens, width), bf16),
            pltpu.VMEM((spans, 2 * pieces * piece, pair_width), bf16),
        ],
        out_shape=[jax.ShapeDtypeStruct((group, tokens, out_width), bf16)]
        + [jax.ShapeDtypeStruct((group, span, out_width), bf16)] * spans,
        compiler_params=params(),
        cost_estimate=cost(
            4 * tokens * width * out_width * group + 4 * tokens * width * 2 * pieces * piece,
            2 * tokens * width, 2 * tokens * width * 2,
        ),
        name="chunk",
    )(meta, table, *sources, *pairs, weight)


def shards(
    hidden,
    neighbour_states,
    query_weight,
    encoder_weight,
    output_weight,
    neighbour_owner,
    neighbour_slot,
    neighbour_length,
):
    row_count = lax.axis_size("rows")
    group = lax.axis_size("mp")
    pieces = group * lax.axis_size("sub")
    me, mp, sub = lax.axis_index("rows"), lax.axis_index("mp"), lax.axis_index("sub")
    spans_here = neighbour_owner.shape[0]
    count, slot_tokens, feature_shard = neighbour_states.shape
    features = feature_shard * pieces
    size = encoder_weight.shape[1] // 2
    token_count = hidden.shape[0]
    span_tokens = token_count // spans_here
    requests = 2 * spans_here
    cap = max(2, (requests + row_count - 1) // row_count)
    chunks = 2
    spans = spans_here // chunks
    first_tokens = token_count // 4
    last_low = token_count - token_count * 10 // 32
    gain = 1.0 / (softcap * math.sqrt(size))
    add = lambda *terms: functools.reduce(
        lambda a, b: a + b, [t.astype(f32) for t in terms]
    ).astype(bf16)

    meta = jnp.stack([me, mp, sub]).astype(jnp.int32)

    def cross(mine):
        return [shift(mine, "mp", dm) for dm in range(1, group)]

    def with_near(fars, *earlier):
        out = []
        for far in lax.optimization_barrier((fars, *earlier))[0]:
            out += [far, shift(far, "sub", 1)]
        return out

    fars_first = cross(hidden[:first_tokens])

    lanes = max(spans_here, count)
    widen = lambda t: jnp.pad(t, ((0, 0), (0, lanes - t.shape[1])))
    table = jnp.concatenate(
        [widen(neighbour_owner.T), widen(neighbour_slot.T), widen(neighbour_length[None])], axis=0
    )[None]

    kept, sent = encode(meta, neighbour_states, encoder_weight, pieces)
    received = shift(after(sent, *fars_first), "sub", 1)
    leaving = [add(kept[dm], received[dm]) for dm in range(1, group)]
    crossed = [shift(leaving[dm - 1], "mp", dm) for dm in range(1, group)]
    near = shift(after(hidden, *leaving), "sub", 1)
    table = after(table, *leaving)
    while table.shape[0] < row_count:
        table = jnp.concatenate([table, swap(table, "rows", table.shape[0])], axis=0)

    fars_second = cross(after(hidden[first_tokens:last_low], table, *crossed))

    routed = route(meta, table, kept, received, crossed, cap, features, count, requests)
    encoded = jnp.concatenate(
        [routed[0]]
        + list(lax.optimization_barrier([swap(routed[d], "rows", d) for d in range(row_count - 1, 0, -1)]))[::-1],
        axis=0,
    )
    pairs = [encoded, shift(encoded, "sub", 1)]
    fars = [shift(encoded, "mp", dm) for dm in range(1, group)]
    queries = project_queries(
        after(meta, encoded), hidden, near,
        [with_near(fars_first, encoded), with_near(fars_second, encoded)], query_weight, gain,
    )
    fars_last = cross(after(hidden[last_low:], encoded))
    pairs += with_near(fars, queries)

    def join(c, *earlier):
        got = after(received[c], *earlier)
        step = span_tokens
        parts = [
            [add(kept[c][dm, i * step : (i + 1) * step], g[dm]) for i, g in enumerate(got)]
            for dm in range(1, group)
        ]
        return [jnp.concatenate(p, axis=0) for p in parts]

    kept, received, leaving, arrived, outs = [], [], [], [], []

    def total(c, *earlier):
        got = jnp.concatenate([g[0] for g in received[c]], axis=0)
        outs.append(add(after(kept[c], *earlier)[0], got, *arrived[c]))

    for c in range(chunks):
        sources = [queries]
        if c == chunks - 1:
            sources += [hidden, near, *with_near(fars_last, *leaving[0]), query_weight]
        gate = leaving[c - 1] if c else []
        one, *others = run_chunk(
            after(meta, *gate), table, sources, pairs, output_weight, c * spans,
            c * spans * span_tokens, spans, span_tokens, feature_shard, cap, gain,
        )
        kept.append(one)
        received.append([shift(other, "sub", 1) for other in others])
        leaving.append(join(c, *([] if c else fars_last)))
        arrived.append([shift(leaving[c][dm - 1], "mp", dm) for dm in range(1, group)])
        if c:
            total(c - 1, *leaving[c])
    total(chunks - 1)
    mixed = jnp.zeros((token_count, feature_shard), bf16)
    for c, out in enumerate(outs):
        mixed = lax.dynamic_update_slice(after(mixed, meta), out, (c * spans * span_tokens, 0))
    return mixed


def solution(mesh):
    placed = (
        P(("groups", "rows"), ("mp", "sub")),
        P(("groups", "rows"), None, ("mp", "sub")),
        P(None, ("mp", "sub")),
        P(("mp", "sub"), None),
        P(("mp", "sub"), None),
        P(("groups", "rows"), None),
        P(("groups", "rows"), None),
        P(("groups", "rows")),
    )
    return jax.shard_map(
        shards,
        mesh=mesh,
        in_specs=placed,
        out_specs=P(("groups", "rows"), ("mp", "sub")),
        check_vma=False,
    )
```

```python
import functools
import math

import jax
import jax.numpy as jnp
from jax import lax
from jax.experimental import pallas as pl
from jax.experimental.pallas import tpu as pltpu
from jax.sharding import PartitionSpec as P

eps = 1e-05
softcap = 10.0
f32 = jnp.float32
bf16 = jnp.bfloat16

VMEM = pl.BlockSpec(memory_space=pltpu.VMEM)
SMEM = pl.BlockSpec(memory_space=pltpu.SMEM)


def shift(value, axis, by):
    size = lax.axis_size(axis)
    return lax.ppermute(value, axis, [(i, (i + by) % size) for i in range(size)])


def swap(value, axis, by):
    size = lax.axis_size(axis)
    return lax.ppermute(value, axis, [(i, i ^ by) for i in range(size)])


def after(value, *earlier):
    return lax.optimization_barrier((value, *earlier))[0]


def cost(flops, nbytes, transcendentals=0):
    return pl.CostEstimate(flops=flops, bytes_accessed=nbytes, transcendentals=transcendentals)


def params():
    return pltpu.CompilerParams(vmem_limit_bytes=16 * 1024 * 1024)


def diagonal_of(piece):
    down = lax.broadcasted_iota(jnp.int32, (piece, 128), 0)
    return down == lax.broadcasted_iota(jnp.int32, (piece, 128), 1)


def encode_kernel(meta, x_ref, w_ref, kept_ref, sent_ref, product, squares, *, pieces, piece, block):
    mp, sub, size = meta[1], meta[2], pieces // 2
    count, tokens, width = x_ref.shape
    diagonal = diagonal_of(piece)

    @pl.loop(0, count // block)
    def _(step):
        x = x_ref[pl.ds(step * block, block)].reshape(block * tokens, width)
        result = jnp.dot(x, w_ref[...], preferred_element_type=f32).astype(bf16)
        product[...] = result.reshape(product.shape)
        xf = x.astype(f32)
        square = jnp.sum(xf * xf, axis=1, keepdims=True)
        for a in range(pieces):
            for n in range(block):
                low = n * tokens + a * piece
                column = jnp.broadcast_to(square[low : low + piece], (piece, 128))
                squares[a, pl.ds(step * block + n, 1), :] = jnp.sum(
                    jnp.where(diagonal, column, 0.0), axis=0, keepdims=True
                )
        rows = pl.ds(pl.multiple_of(step * block * piece, block * piece), block * piece)
        for ds, out_ref in ((0, kept_ref), (1, sent_ref)):
            for dm in range(size):
                a = lax.rem(mp + dm, size) * 2 + lax.rem(sub + ds, 2)
                taken = product[:, pl.ds(pl.multiple_of(a * piece, piece), piece), :]
                out_ref[dm, rows, :] = taken.reshape(block * piece, taken.shape[2])

    for ds, out_ref in ((0, kept_ref), (1, sent_ref)):
        for dm in range(size):
            a = lax.rem(mp + dm, size) * 2 + lax.rem(sub + ds, 2)
            tail = jnp.concatenate([squares[a], jnp.zeros_like(squares[a])], axis=1)
            out_ref[dm, count * piece : count * piece + count, :] = tail.astype(bf16)


def encode(meta, states, weight, pieces):
    count, tokens, width = states.shape
    out_width = weight.shape[1]
    piece = tokens // pieces
    rows = count * piece + count
    block = 4
    return pl.pallas_call(
        functools.partial(encode_kernel, pieces=pieces, piece=piece, block=block),
        in_specs=[SMEM, VMEM, VMEM],
        out_specs=[VMEM] * 2,
        scratch_shapes=[
            pltpu.VMEM((block, tokens, out_width), bf16),
            pltpu.VMEM((pieces, count, 128), f32),
        ],
        out_shape=[jax.ShapeDtypeStruct((pieces // 2, rows, out_width), bf16)] * 2,
        compiler_params=params(),
        cost_estimate=cost(2 * count * tokens * width * out_width, 2 * count * tokens * width),
        name="encode",
    )(meta, states, weight)


def route_kernel(meta, table, kept, received, *refs, row_count, cap, piece, count, requests, features):
    crossed, outs = refs[: -2 - row_count], refs[-2 - row_count : -2]
    encoded, picks = refs[-2:]
    me = meta[0]
    total = kept[0].astype(f32) + received[0].astype(f32)
    for ref in crossed:
        total = total + ref[...].astype(f32)
    scale = lax.rsqrt(total[count * piece :, :128] * (1.0 / features) + eps)
    diagonal = diagonal_of(piece)
    for n in range(count):
        row = jnp.broadcast_to(scale[n : n + 1], (piece, 128))
        column = jnp.sum(jnp.where(diagonal, row, 0.0), axis=1, keepdims=True)
        encoded[n] = (total[n * piece : (n + 1) * piece] * column).astype(bf16)
    for d in range(row_count):
        for r in range(cap):
            picks[d, r] = 0
        seen = jnp.int32(0)
        for q in range(requests):
            mine = table[d, q % 2, q // 2] == me

            @pl.when(mine)
            def _(seen=seen, q=q, d=d):
                picks[d, jnp.minimum(seen, cap - 1)] = table[d, 2 + q % 2, q // 2]

            seen = seen + mine.astype(jnp.int32)
        for r in range(cap):
            outs[d][r] = encoded[picks[d, r]]


def route(meta, table, kept, received, crossed, cap, features, count, requests):
    row_count = table.shape[0]
    rows, width = kept.shape[-2:]
    piece = rows // count - 1
    return pl.pallas_call(
        functools.partial(
            route_kernel, row_count=row_count, cap=cap, piece=piece, count=count,
            requests=requests, features=features,
        ),
        in_specs=[SMEM] * 2 + [VMEM] * (2 + len(crossed)),
        out_specs=[VMEM] * row_count,
        scratch_shapes=[
            pltpu.VMEM((count, piece, width), bf16),
            pltpu.SMEM((row_count, cap), jnp.int32),
        ],
        out_shape=[jax.ShapeDtypeStruct((cap, piece, width), bf16)] * row_count,
        compiler_params=params(),
        cost_estimate=cost(8 * rows * width, 2 * rows * width * 3),
        name="route",
    )(meta, table, kept, received, *crossed)


def queries_from(meta, hs, w_ref, low, gain):
    mp, sub = meta[1], meta[2]
    tokens, width = hs[-1].shape
    features = w_ref.shape[0]
    group = features // width // 2
    total, squares = None, None
    for k, part in enumerate(hs):
        block = lax.rem(mp - k // 2 + group, group) * 2 + lax.rem(sub + k % 2, 2)
        rows = pl.ds(pl.multiple_of(block * width, width), width)
        h = part[low : low + tokens] if k < 2 else part[...]
        for i in range(0, width, 128):
            square = h[:, i : i + 128].astype(f32)
            square = square * square
            squares = square if squares is None else squares + square
        product = jnp.dot(h, w_ref[rows, :], preferred_element_type=f32)
        total = product if total is None else total + product
    squares = jnp.sum(squares, axis=1, keepdims=True)
    return (total * (lax.rsqrt(squares * (1.0 / features) + eps) * gain)).astype(bf16)


def query_kernel(meta, own_ref, near_ref, *refs, lows, gain):
    fars, w_ref, out_ref = refs[:-2], *refs[-2:]
    each = len(fars) // len(lows)
    for i, low in enumerate(lows):
        far = fars[i * each : (i + 1) * each]
        out_ref[low : low + far[0].shape[0], :] = queries_from(
            meta, (own_ref, near_ref, *far), w_ref, low, gain
        )


def project_queries(meta, own, near, segments, weight, gain):
    lows, tokens = [], 0
    for far in segments:
        lows.append(tokens)
        tokens += far[0].shape[0]
    parts = [own, near] + [part for far in segments for part in far]
    depth, out_width = weight.shape
    return pl.pallas_call(
        functools.partial(query_kernel, lows=tuple(lows), gain=gain),
        in_specs=[SMEM] + [VMEM] * (len(parts) + 1),
        out_specs=VMEM,
        out_shape=jax.ShapeDtypeStruct((tokens, out_width), bf16),
        compiler_params=params(),
        cost_estimate=cost(2 * tokens * depth * out_width, 2 * tokens * depth),
        name="queries",
    )(meta, *parts, weight)


def chunk_kernel(
    meta, table, *refs, first, low, spans, span, heads, size, pieces, cap, gain
):
    own_end = -4 - spans
    sources, kvs = refs[: own_end - pieces], refs[own_end - pieces : own_end]
    w_ref, kept_ref, *sent_refs, att, pair = refs[-4 - spans :]
    me, mp, sub = meta[0], meta[1], meta[2]
    group = pieces // 2
    piece = kvs[0].shape[1]
    tokens = att.shape[0]
    ready = min(tokens, sources[0].shape[0] - low)
    queries = sources[0][low : low + ready]
    if ready < tokens:
        late = queries_from(meta, sources[1:-1], sources[-1], low + ready, gain)
        queries = jnp.concatenate([queries, late], axis=0)
    local = lax.broadcasted_iota(jnp.int32, (piece, size), 0)
    for c in range(pair.shape[0]):
        masks = []
        for j in range(2):
            q = 2 * (first + c) + j
            owner = table[0, j, first + c]
            rank = jnp.int32(0)
            for e in range(q):
                rank = rank + (table[0, e % 2, e // 2] == owner).astype(jnp.int32)
            away = owner ^ me
            slot = away * cap + rank
            length = table[away, 4, table[0, 2 + j, first + c]]
            for p in range(pieces):
                at = (j * pieces + p) * piece
                pair[c, at : at + piece, :] = kvs[p][slot]
                place = lax.rem(mp - p // 2 + group, group) * 2 + lax.rem(sub + p % 2, 2)
                masks.append((local + place * piece < length).astype(f32))
        mask = jnp.concatenate(masks, axis=0)
        keys = pair[c, :, :size]
        values = jnp.concatenate(
            [(pair[c, :, size:].astype(f32) * mask).astype(bf16), mask.astype(bf16)], axis=1
        )
        rows = slice(c * span, (c + 1) * span)
        query = jnp.concatenate(
            [queries[rows, h * size : (h + 1) * size] for h in range(heads)], axis=0
        )
        scores = lax.dot_general(query, keys, (((1,), (1,)), ((), ())), preferred_element_type=f32)
        weights = jnp.exp(softcap * jnp.tanh(scores)).astype(bf16)
        summed = jnp.dot(weights, values, preferred_element_type=f32)
        attended = (summed[:, :size] / summed[:, size:]).astype(bf16)
        for h in range(heads):
            att[rows, h * size : (h + 1) * size] = attended[h * span : (h + 1) * span]
    width = kept_ref.shape[2]
    for ds in (1, 0):
        for dm in range(group):
            block = lax.rem(mp + dm, group) * 2 + lax.rem(sub + ds, 2)
            w = w_ref[:, pl.ds(pl.multiple_of(block * width, width), width)]
            result = jnp.dot(att[...], w, preferred_element_type=f32).astype(bf16)
            if ds:
                for c, sent_ref in enumerate(sent_refs):
                    sent_ref[dm] = result[c * span : (c + 1) * span]
            else:
                kept_ref[dm] = result


def run_chunk(meta, table, sources, pairs, weight, first, low, spans, span, out_width, cap, gain):
    width = weight.shape[0]
    tokens = spans * span
    pieces = len(pairs)
    piece, pair_width = pairs[0].shape[1:]
    size = pair_width // 2
    group = pieces // 2
    return pl.pallas_call(
        functools.partial(
            chunk_kernel, first=first, low=low, spans=spans, span=span, heads=width // size, size=size,
            pieces=pieces, cap=cap, gain=gain,
        ),
        in_specs=[SMEM] * 2 + [VMEM] * (1 + pieces + len(sources)),
        out_specs=[VMEM] * (1 + spans),
        scratch_shapes=[
            pltpu.VMEM((tokens, width), bf16),
            pltpu.VMEM((spans, 2 * pieces * piece, pair_width), bf16),
        ],
        out_shape=[jax.ShapeDtypeStruct((group, tokens, out_width), bf16)]
        + [jax.ShapeDtypeStruct((group, span, out_width), bf16)] * spans,
        compiler_params=params(),
        cost_estimate=cost(
            4 * tokens * width * out_width * group + 4 * tokens * width * 2 * pieces * piece,
            2 * tokens * width, 2 * tokens * width * 2,
        ),
        name="chunk",
    )(meta, table, *sources, *pairs, weight)


def shards(
    hidden,
    neighbour_states,
    query_weight,
    encoder_weight,
    output_weight,
    neighbour_owner,
    neighbour_slot,
    neighbour_length,
):
    row_count = lax.axis_size("rows")
    group = lax.axis_size("mp")
    pieces = group * lax.axis_size("sub")
    me, mp, sub = lax.axis_index("rows"), lax.axis_index("mp"), lax.axis_index("sub")
    spans_here = neighbour_owner.shape[0]
    count, slot_tokens, feature_shard = neighbour_states.shape
    features = feature_shard * pieces
    size = encoder_weight.shape[1] // 2
    token_count = hidden.shape[0]
    span_tokens = token_count // spans_here
    requests = 2 * spans_here
    cap = max(2, (requests + row_count - 1) // row_count)
    chunks = 2
    spans = spans_here // chunks
    first_tokens = token_count // 4
    last_low = token_count - token_count * 9 // 32
    gain = 1.0 / (softcap * math.sqrt(size))
    add = lambda *terms: functools.reduce(
        lambda a, b: a + b, [t.astype(f32) for t in terms]
    ).astype(bf16)

    meta = jnp.stack([me, mp, sub]).astype(jnp.int32)

    def cross(mine):
        return [shift(mine, "mp", dm) for dm in range(1, group)]

    def with_near(fars, *earlier):
        out = []
        for far in lax.optimization_barrier((fars, *earlier))[0]:
            out += [far, shift(far, "sub", 1)]
        return out

    fars_first = cross(hidden[:first_tokens])

    lanes = max(spans_here, count)
    widen = lambda t: jnp.pad(t, ((0, 0), (0, lanes - t.shape[1])))
    table = jnp.concatenate(
        [widen(neighbour_owner.T), widen(neighbour_slot.T), widen(neighbour_length[None])], axis=0
    )[None]

    kept, sent = encode(meta, neighbour_states, encoder_weight, pieces)
    received = shift(after(sent, *fars_first), "sub", 1)
    leaving = [add(kept[dm], received[dm]) for dm in range(1, group)]
    crossed = [shift(leaving[dm - 1], "mp", dm) for dm in range(1, group)]
    near = shift(after(hidden, *leaving), "sub", 1)
    table = after(table, *leaving)
    while table.shape[0] < row_count:
        table = jnp.concatenate([table, swap(table, "rows", table.shape[0])], axis=0)

    fars_second = cross(after(hidden[first_tokens:last_low], table, *crossed))

    routed = route(meta, table, kept, received, crossed, cap, features, count, requests)
    encoded = jnp.concatenate(
        [routed[0]]
        + list(lax.optimization_barrier([swap(routed[d], "rows", d) for d in range(row_count - 1, 0, -1)]))[::-1],
        axis=0,
    )
    pairs = [encoded, shift(encoded, "sub", 1)]
    fars = [shift(encoded, "mp", dm) for dm in range(1, group)]
    queries = project_queries(
        after(meta, encoded), hidden, near,
        [with_near(fars_first, encoded), with_near(fars_second, encoded)], query_weight, gain,
    )
    fars_last = cross(after(hidden[last_low:], encoded))
    pairs += with_near(fars, queries)

    def join(c, *earlier):
        got = after(received[c], *earlier)
        step = span_tokens
        parts = [
            [add(kept[c][dm, i * step : (i + 1) * step], g[dm]) for i, g in enumerate(got)]
            for dm in range(1, group)
        ]
        return [jnp.concatenate(p, axis=0) for p in parts]

    kept, received, leaving, arrived, outs = [], [], [], [], []

    def total(c, *earlier):
        got = jnp.concatenate([g[0] for g in received[c]], axis=0)
        outs.append(add(after(kept[c], *earlier)[0], got, *arrived[c]))

    for c in range(chunks):
        sources = [queries]
        if c == chunks - 1:
            sources += [hidden, near, *with_near(fars_last, *leaving[0]), query_weight]
        gate = leaving[c - 1] if c else []
        one, *others = run_chunk(
            after(meta, *gate), table, sources, pairs, output_weight, c * spans,
            c * spans * span_tokens, spans, span_tokens, feature_shard, cap, gain,
        )
        kept.append(one)
        received.append([shift(other, "sub", 1) for other in others])
        leaving.append(join(c, *([] if c else fars_last)))
        arrived.append([shift(leaving[c][dm - 1], "mp", dm) for dm in range(1, group)])
        if c:
            total(c - 1, *leaving[c])
    total(chunks - 1)
    mixed = jnp.zeros((token_count, feature_shard), bf16)
    for c, out in enumerate(outs):
        mixed = lax.dynamic_update_slice(after(mixed, meta), out, (c * spans * span_tokens, 0))
    return mixed


def solution(mesh):
    placed = (
        P(("groups", "rows"), ("mp", "sub")),
        P(("groups", "rows"), None, ("mp", "sub")),
        P(None, ("mp", "sub")),
        P(("mp", "sub"), None),
        P(("mp", "sub"), None),
        P(("groups", "rows"), None),
        P(("groups", "rows"), None),
        P(("groups", "rows")),
    )
    return jax.shard_map(
        shards,
        mesh=mesh,
        in_specs=placed,
        out_specs=P(("groups", "rows"), ("mp", "sub")),
        check_vma=False,
    )
```

```python
import functools
import math

import jax
import jax.numpy as jnp
from jax import lax
from jax.experimental import pallas as pl
from jax.experimental.pallas import tpu as pltpu
from jax.sharding import PartitionSpec as P

eps = 1e-05
softcap = 10.0
f32 = jnp.float32
bf16 = jnp.bfloat16

VMEM = pl.BlockSpec(memory_space=pltpu.VMEM)
SMEM = pl.BlockSpec(memory_space=pltpu.SMEM)


def shift(value, axis, by):
    size = lax.axis_size(axis)
    return lax.ppermute(value, axis, [(i, (i + by) % size) for i in range(size)])


def swap(value, axis, by):
    size = lax.axis_size(axis)
    return lax.ppermute(value, axis, [(i, i ^ by) for i in range(size)])


def after(value, *earlier):
    return lax.optimization_barrier((value, *earlier))[0]


def cost(flops, nbytes, transcendentals=0):
    return pl.CostEstimate(flops=flops, bytes_accessed=nbytes, transcendentals=transcendentals)


def params():
    return pltpu.CompilerParams(vmem_limit_bytes=16 * 1024 * 1024)


def diagonal_of(piece):
    down = lax.broadcasted_iota(jnp.int32, (piece, 128), 0)
    return down == lax.broadcasted_iota(jnp.int32, (piece, 128), 1)


def encode_kernel(meta, x_ref, w_ref, kept_ref, sent_ref, product, squares, *, pieces, piece, block):
    mp, sub, size = meta[1], meta[2], pieces // 2
    count, tokens, width = x_ref.shape
    diagonal = diagonal_of(piece)

    @pl.loop(0, count // block)
    def _(step):
        x = x_ref[pl.ds(step * block, block)].reshape(block * tokens, width)
        result = jnp.dot(x, w_ref[...], preferred_element_type=f32).astype(bf16)
        product[...] = result.reshape(product.shape)
        xf = x.astype(f32)
        square = jnp.sum(xf * xf, axis=1, keepdims=True)
        for a in range(pieces):
            for n in range(block):
                low = n * tokens + a * piece
                column = jnp.broadcast_to(square[low : low + piece], (piece, 128))
                squares[a, pl.ds(step * block + n, 1), :] = jnp.sum(
                    jnp.where(diagonal, column, 0.0), axis=0, keepdims=True
                )
        rows = pl.ds(pl.multiple_of(step * block * piece, block * piece), block * piece)
        for ds, out_ref in ((0, kept_ref), (1, sent_ref)):
            for dm in range(size):
                a = lax.rem(mp + dm, size) * 2 + lax.rem(sub + ds, 2)
                taken = product[:, pl.ds(pl.multiple_of(a * piece, piece), piece), :]
                out_ref[dm, rows, :] = taken.reshape(block * piece, taken.shape[2])

    for ds, out_ref in ((0, kept_ref), (1, sent_ref)):
        for dm in range(size):
            a = lax.rem(mp + dm, size) * 2 + lax.rem(sub + ds, 2)
            tail = jnp.concatenate([squares[a], jnp.zeros_like(squares[a])], axis=1)
            out_ref[dm, count * piece : count * piece + count, :] = tail.astype(bf16)


def encode(meta, states, weight, pieces):
    count, tokens, width = states.shape
    out_width = weight.shape[1]
    piece = tokens // pieces
    rows = count * piece + count
    block = 4
    return pl.pallas_call(
        functools.partial(encode_kernel, pieces=pieces, piece=piece, block=block),
        in_specs=[SMEM, VMEM, VMEM],
        out_specs=[VMEM] * 2,
        scratch_shapes=[
            pltpu.VMEM((block, tokens, out_width), bf16),
            pltpu.VMEM((pieces, count, 128), f32),
        ],
        out_shape=[jax.ShapeDtypeStruct((pieces // 2, rows, out_width), bf16)] * 2,
        compiler_params=params(),
        cost_estimate=cost(2 * count * tokens * width * out_width, 2 * count * tokens * width),
        name="encode",
    )(meta, states, weight)


def route_kernel(meta, table, kept, received, *refs, row_count, cap, piece, count, requests, features):
    crossed, outs = refs[: -2 - row_count], refs[-2 - row_count : -2]
    encoded, picks = refs[-2:]
    me = meta[0]
    total = kept[0].astype(f32) + received[0].astype(f32)
    for ref in crossed:
        total = total + ref[...].astype(f32)
    scale = lax.rsqrt(total[count * piece :, :128] * (1.0 / features) + eps)
    diagonal = diagonal_of(piece)
    for n in range(count):
        row = jnp.broadcast_to(scale[n : n + 1], (piece, 128))
        column = jnp.sum(jnp.where(diagonal, row, 0.0), axis=1, keepdims=True)
        encoded[n] = (total[n * piece : (n + 1) * piece] * column).astype(bf16)
    for d in range(row_count):
        for r in range(cap):
            picks[d, r] = 0
        seen = jnp.int32(0)
        for q in range(requests):
            mine = table[d, q % 2, q // 2] == me

            @pl.when(mine)
            def _(seen=seen, q=q, d=d):
                picks[d, jnp.minimum(seen, cap - 1)] = table[d, 2 + q % 2, q // 2]

            seen = seen + mine.astype(jnp.int32)
        for r in range(cap):
            outs[d][r] = encoded[picks[d, r]]


def route(meta, table, kept, received, crossed, cap, features, count, requests):
    row_count = table.shape[0]
    rows, width = kept.shape[-2:]
    piece = rows // count - 1
    return pl.pallas_call(
        functools.partial(
            route_kernel, row_count=row_count, cap=cap, piece=piece, count=count,
            requests=requests, features=features,
        ),
        in_specs=[SMEM] * 2 + [VMEM] * (2 + len(crossed)),
        out_specs=[VMEM] * row_count,
        scratch_shapes=[
            pltpu.VMEM((count, piece, width), bf16),
            pltpu.SMEM((row_count, cap), jnp.int32),
        ],
        out_shape=[jax.ShapeDtypeStruct((cap, piece, width), bf16)] * row_count,
        compiler_params=params(),
        cost_estimate=cost(8 * rows * width, 2 * rows * width * 3),
        name="route",
    )(meta, table, kept, received, *crossed)


def queries_from(meta, hs, w_ref, low, gain):
    mp, sub = meta[1], meta[2]
    tokens, width = hs[-1].shape
    features = w_ref.shape[0]
    group = features // width // 2
    total, squares = None, None
    for k, part in enumerate(hs):
        block = lax.rem(mp - k // 2 + group, group) * 2 + lax.rem(sub + k % 2, 2)
        rows = pl.ds(pl.multiple_of(block * width, width), width)
        h = part[low : low + tokens] if k < 2 else part[...]
        for i in range(0, width, 128):
            square = h[:, i : i + 128].astype(f32)
            square = square * square
            squares = square if squares is None else squares + square
        product = jnp.dot(h, w_ref[rows, :], preferred_element_type=f32)
        total = product if total is None else total + product
    squares = jnp.sum(squares, axis=1, keepdims=True)
    return (total * (lax.rsqrt(squares * (1.0 / features) + eps) * gain)).astype(bf16)


def query_kernel(meta, own_ref, near_ref, *refs, lows, gain):
    fars, w_ref, out_ref = refs[:-2], *refs[-2:]
    each = len(fars) // len(lows)
    for i, low in enumerate(lows):
        far = fars[i * each : (i + 1) * each]
        out_ref[low : low + far[0].shape[0], :] = queries_from(
            meta, (own_ref, near_ref, *far), w_ref, low, gain
        )


def project_queries(meta, own, near, segments, weight, gain):
    lows, tokens = [], 0
    for far in segments:
        lows.append(tokens)
        tokens += far[0].shape[0]
    parts = [own, near] + [part for far in segments for part in far]
    depth, out_width = weight.shape
    return pl.pallas_call(
        functools.partial(query_kernel, lows=tuple(lows), gain=gain),
        in_specs=[SMEM] + [VMEM] * (len(parts) + 1),
        out_specs=VMEM,
        out_shape=jax.ShapeDtypeStruct((tokens, out_width), bf16),
        compiler_params=params(),
        cost_estimate=cost(2 * tokens * depth * out_width, 2 * tokens * depth),
        name="queries",
    )(meta, *parts, weight)


def chunk_kernel(
    meta, table, *refs, first, low, spans, span, heads, size, pieces, cap, gain
):
    own_end = -4 - spans
    sources, kvs = refs[: own_end - pieces], refs[own_end - pieces : own_end]
    w_ref, kept_ref, *sent_refs, att, pair = refs[-4 - spans :]
    me, mp, sub = meta[0], meta[1], meta[2]
    group = pieces // 2
    piece = kvs[0].shape[1]
    tokens = att.shape[0]
    ready = min(tokens, sources[0].shape[0] - low)
    queries = sources[0][low : low + ready]
    if ready < tokens:
        late = queries_from(meta, sources[1:-1], sources[-1], low + ready, gain)
        queries = jnp.concatenate([queries, late], axis=0)
    local = lax.broadcasted_iota(jnp.int32, (piece, size), 0)
    for c in range(pair.shape[0]):
        masks = []
        for j in range(2):
            q = 2 * (first + c) + j
            owner = table[0, j, first + c]
            rank = jnp.int32(0)
            for e in range(q):
                rank = rank + (table[0, e % 2, e // 2] == owner).astype(jnp.int32)
            away = owner ^ me
            slot = away * cap + rank
            length = table[away, 4, table[0, 2 + j, first + c]]
            for p in range(pieces):
                at = (j * pieces + p) * piece
                pair[c, at : at + piece, :] = kvs[p][slot]
                place = lax.rem(mp - p // 2 + group, group) * 2 + lax.rem(sub + p % 2, 2)
                masks.append((local + place * piece < length).astype(f32))
        mask = jnp.concatenate(masks, axis=0)
        keys = pair[c, :, :size]
        values = jnp.concatenate(
            [(pair[c, :, size:].astype(f32) * mask).astype(bf16), mask.astype(bf16)], axis=1
        )
        rows = slice(c * span, (c + 1) * span)
        query = jnp.concatenate(
            [queries[rows, h * size : (h + 1) * size] for h in range(heads)], axis=0
        )
        scores = lax.dot_general(query, keys, (((1,), (1,)), ((), ())), preferred_element_type=f32)
        weights = jnp.exp(softcap * jnp.tanh(scores)).astype(bf16)
        summed = jnp.dot(weights, values, preferred_element_type=f32)
        attended = (summed[:, :size] / summed[:, size:]).astype(bf16)
        for h in range(heads):
            att[rows, h * size : (h + 1) * size] = attended[h * span : (h + 1) * span]
    width = kept_ref.shape[2]
    for ds in (1, 0):
        for dm in range(group):
            block = lax.rem(mp + dm, group) * 2 + lax.rem(sub + ds, 2)
            w = w_ref[:, pl.ds(pl.multiple_of(block * width, width), width)]
            result = jnp.dot(att[...], w, preferred_element_type=f32).astype(bf16)
            if ds:
                for c, sent_ref in enumerate(sent_refs):
                    sent_ref[dm] = result[c * span : (c + 1) * span]
            else:
                kept_ref[dm] = result


def run_chunk(meta, table, sources, pairs, weight, first, low, spans, span, out_width, cap, gain):
    width = weight.shape[0]
    tokens = spans * span
    pieces = len(pairs)
    piece, pair_width = pairs[0].shape[1:]
    size = pair_width // 2
    group = pieces // 2
    return pl.pallas_call(
        functools.partial(
            chunk_kernel, first=first, low=low, spans=spans, span=span, heads=width // size, size=size,
            pieces=pieces, cap=cap, gain=gain,
        ),
        in_specs=[SMEM] * 2 + [VMEM] * (1 + pieces + len(sources)),
        out_specs=[VMEM] * (1 + spans),
        scratch_shapes=[
            pltpu.VMEM((tokens, width), bf16),
            pltpu.VMEM((spans, 2 * pieces * piece, pair_width), bf16),
        ],
        out_shape=[jax.ShapeDtypeStruct((group, tokens, out_width), bf16)]
        + [jax.ShapeDtypeStruct((group, span, out_width), bf16)] * spans,
        compiler_params=params(),
        cost_estimate=cost(
            4 * tokens * width * out_width * group + 4 * tokens * width * 2 * pieces * piece,
            2 * tokens * width, 2 * tokens * width * 2,
        ),
        name="chunk",
    )(meta, table, *sources, *pairs, weight)


def shards(
    hidden,
    neighbour_states,
    query_weight,
    encoder_weight,
    output_weight,
    neighbour_owner,
    neighbour_slot,
    neighbour_length,
):
    row_count = lax.axis_size("rows")
    group = lax.axis_size("mp")
    pieces = group * lax.axis_size("sub")
    me, mp, sub = lax.axis_index("rows"), lax.axis_index("mp"), lax.axis_index("sub")
    spans_here = neighbour_owner.shape[0]
    count, slot_tokens, feature_shard = neighbour_states.shape
    features = feature_shard * pieces
    size = encoder_weight.shape[1] // 2
    token_count = hidden.shape[0]
    span_tokens = token_count // spans_here
    requests = 2 * spans_here
    cap = max(2, (requests + row_count - 1) // row_count)
    chunks = 2
    spans = spans_here // chunks
    first_tokens = token_count * 9 // 32
    last_low = token_count - token_count * 9 // 32
    gain = 1.0 / (softcap * math.sqrt(size))
    add = lambda *terms: functools.reduce(
        lambda a, b: a + b, [t.astype(f32) for t in terms]
    ).astype(bf16)

    meta = jnp.stack([me, mp, sub]).astype(jnp.int32)

    def cross(mine):
        return [shift(mine, "mp", dm) for dm in range(1, group)]

    def with_near(fars, *earlier):
        out = []
        for far in lax.optimization_barrier((fars, *earlier))[0]:
            out += [far, shift(far, "sub", 1)]
        return out

    fars_first = cross(hidden[:first_tokens])

    lanes = max(spans_here, count)
    widen = lambda t: jnp.pad(t, ((0, 0), (0, lanes - t.shape[1])))
    table = jnp.concatenate(
        [widen(neighbour_owner.T), widen(neighbour_slot.T), widen(neighbour_length[None])], axis=0
    )[None]

    kept, sent = encode(meta, neighbour_states, encoder_weight, pieces)
    received = shift(after(sent, *fars_first), "sub", 1)
    leaving = [add(kept[dm], received[dm]) for dm in range(1, group)]
    crossed = [shift(leaving[dm - 1], "mp", dm) for dm in range(1, group)]
    near = shift(after(hidden, *leaving), "sub", 1)
    table = after(table, *leaving)
    while table.shape[0] < row_count:
        table = jnp.concatenate([table, swap(table, "rows", table.shape[0])], axis=0)

    fars_second = cross(after(hidden[first_tokens:last_low], table, *crossed))

    routed = route(meta, table, kept, received, crossed, cap, features, count, requests)
    encoded = jnp.concatenate(
        [routed[0]]
        + list(lax.optimization_barrier([swap(routed[d], "rows", d) for d in range(1, row_count)])),
        axis=0,
    )
    pairs = [encoded, shift(encoded, "sub", 1)]
    fars = [shift(encoded, "mp", dm) for dm in range(1, group)]
    queries = project_queries(
        after(meta, encoded), hidden, near,
        [with_near(fars_first, encoded), with_near(fars_second, encoded)], query_weight, gain,
    )
    fars_last = cross(after(hidden[last_low:], encoded))
    pairs += with_near(fars, queries)

    def join(c, *earlier):
        got = after(received[c], *earlier)
        step = span_tokens
        parts = [
            [add(kept[c][dm, i * step : (i + 1) * step], g[dm]) for i, g in enumerate(got)]
            for dm in range(1, group)
        ]
        return [jnp.concatenate(p, axis=0) for p in parts]

    kept, received, leaving, arrived, outs = [], [], [], [], []

    def total(c, *earlier):
        got = jnp.concatenate([g[0] for g in received[c]], axis=0)
        outs.append(add(after(kept[c], *earlier)[0], got, *arrived[c]))

    for c in range(chunks):
        sources = [queries]
        if c == chunks - 1:
            sources += [hidden, near, *with_near(fars_last, *leaving[0]), query_weight]
        gate = leaving[c - 1] if c else []
        one, *others = run_chunk(
            after(meta, *gate), table, sources, pairs, output_weight, c * spans,
            c * spans * span_tokens, spans, span_tokens, feature_shard, cap, gain,
        )
        kept.append(one)
        received.append([shift(other, "sub", 1) for other in others])
        leaving.append(join(c, *([] if c else fars_last)))
        arrived.append([shift(leaving[c][dm - 1], "mp", dm) for dm in range(1, group)])
        if c:
            total(c - 1, *leaving[c])
    total(chunks - 1)
    mixed = jnp.zeros((token_count, feature_shard), bf16)
    for c, out in enumerate(outs):
        mixed = lax.dynamic_update_slice(after(mixed, meta), out, (c * spans * span_tokens, 0))
    return mixed


def solution(mesh):
    placed = (
        P(("groups", "rows"), ("mp", "sub")),
        P(("groups", "rows"), None, ("mp", "sub")),
        P(None, ("mp", "sub")),
        P(("mp", "sub"), None),
        P(("mp", "sub"), None),
        P(("groups", "rows"), None),
        P(("groups", "rows"), None),
        P(("groups", "rows")),
    )
    return jax.shard_map(
        shards,
        mesh=mesh,
        in_specs=placed,
        out_specs=P(("groups", "rows"), ("mp", "sub")),
        check_vma=False,
    )
```
